256 devices in a mesh: patch: 64 (over y, z_lo, x), quad: 4 (over z_hi, core).
Axes of the slice: x: 4, y: 4, z: 8 (z_hi: 2, z_lo: 4; z = z_hi * 4 + z_lo), core: 2. Of those that a mesh axis runs over, the one named last changes fastest.
Arguments:
- vectors: float32 [64, 24, 128, 512], P('patch', None, 'quad'), may hold values from -6 to 6
- log_kappa: float32 [64, 128, 512], P('patch', 'quad'), may hold values from -3 to 3, as said below
Outputs:
- basis: float32 [64, 24, 128, 256], P('patch', None, 'quad')
- coupling: float32 [64, 2, 24, 24], P('patch')
The draws below stay inside these ranges and needn't reach their ends.
Inputs may be any that keep to these rules, and one draw needn't show every extreme that they name: The patches are windows of one strip: log_kappa[p, r, 256 + c] equals log_kappa[p + 1, r, c] for 0 <= c < 256.
All inputs are finite; a program needn't handle non-finite values.
Results may differ from the reference program's by a relative error of at most 0.0003.
Values sent between devices are 32-bit elements; how exact they have to be, the bound alone decides.
No kernel may reach another device: no remote copies, remote signals or barrier semaphores. Data moves between devices by JAX's collectives and lax.ppermute only.
A program may use at most 64 MiB of HBM per device.

```python
import jax
import jax.numpy as jnp
from jax import lax

K = 24
PC = 512
SWEEPS = 8
PATCHES = 64
QROWS = 128
HALF = 256
BAND = 128


def draw_log_kappa(key, part):
    key = jax.random.fold_in(key, 11)
    whole_strip = jax.random.truncated_normal(key, -3.0, 3.0, (QROWS, PATCHES * HALF + 2 * BAND), jnp.float32)
    starts = jnp.arange(PATCHES) * HALF
    columns = starts[:, None] + jnp.arange(PC)[None, :]
    return jnp.transpose(whole_strip[:, columns], (1, 0, 2))


def block_scale(own_key, dims, shards, least, top_value):
    gain = 1.0
    for dim, parts in shards:
        draws = jax.random.uniform(jax.random.fold_in(jax.random.fold_in(own_key, 6), dim), (parts,), jnp.float32, least / len(shards), top_value / len(shards))
        gain = gain * jnp.repeat(jnp.exp(draws), dims[dim] // parts).reshape((-1,) + (1,) * (len(dims) - 1 - dim))
    return gain


def noise(key, dims, deviation, most, cuts=(), kind=jnp.bfloat16):
    entries = jax.random.normal(key, dims, jnp.float32) * deviation
    if len(cuts) > 0:
        entries = block_scale(key, dims, cuts, -0.22, 0.18) * entries
    return jnp.clip(entries, min=-most, max=most).astype(kind)


def setup_inputs(seed: int = 0) -> dict:
    key_of = jax.random.split(jax.random.key(seed), 3)
    vectors = noise(key_of[0], (PATCHES, K, QROWS, PC), 1.0, 6.0, ((0, 64), (2, 4)), jnp.float32)
    log_kappa = draw_log_kappa(jax.random.fold_in(key_of[2], 71), 0)
    return dict(vectors=vectors, log_kappa=log_kappa)


mass_term = 0.1
lower_bound = 0.05
upper_bound = 2.0
mid_value = 0.5 * (upper_bound + lower_bound)
half_width = 0.5 * (upper_bound - lower_bound)
ratio_start = mid_value / half_width
highest = lax.Precision.HIGHEST

def face_weights(kappa_pad, lo_row, hi_row):
    centre = kappa_pad[lo_row:hi_row, 1:-1]
    upper_face = 0.5 * (centre + kappa_pad[lo_row - 1:hi_row - 1, 1:-1])
    lower_face = 0.5 * (centre + kappa_pad[lo_row + 1:hi_row + 1, 1:-1])
    left_face = 0.5 * (centre + kappa_pad[lo_row:hi_row, :-2])
    right_face = 0.5 * (centre + kappa_pad[lo_row:hi_row, 2:])
    diagonal = upper_face + lower_face + left_face + right_face + mass_term * centre
    return (upper_face, lower_face, left_face, right_face, diagonal)

def apply_operator(padded, weights):
    upper_face, lower_face, left_face, right_face, diagonal = weights
    centre = padded[:, 1:-1, :]
    sideways = jnp.pad(centre, ((0, 0), (0, 0), (1, 1)))
    return diagonal * centre - (upper_face * padded[:, :-2, :] + lower_face * padded[:, 2:, :] + left_face * sideways[:, :, :-2] + right_face * sideways[:, :, 2:])

def pad_rows(values):
    return jnp.pad(values, ((0, 0), (1, 1), (0, 0)))

def patch_solve(inputs):
    vectors_one, log_one = inputs
    kappa_pad = jnp.exp(jnp.pad(log_one, ((2, 2), (1, 1))))
    weights = face_weights(kappa_pad, 2, kappa_pad.shape[0] - 2)
    iterate = vectors_one
    residual = -apply_operator(pad_rows(iterate), weights) / weights[4]
    direction = residual / mid_value
    rho_now = 1.0 / ratio_start
    for turn_index in range(SWEEPS):
        iterate = iterate + direction
        if turn_index < SWEEPS - 1:
            residual = residual - apply_operator(pad_rows(direction), weights) / weights[4]
            rho_next = 1.0 / (2.0 * ratio_start - rho_now)
            direction = rho_next * rho_now * direction + 2.0 * rho_next / half_width * residual
            rho_now = rho_next
    vec_count = iterate.shape[0]
    width_all = iterate.shape[2]
    half_cols = width_all // 2
    band_cols = width_all // 4
    subdomain = iterate[:, :, band_cols:band_cols + half_cols].reshape(vec_count, -1)
    factor = jnp.linalg.cholesky(jnp.dot(subdomain, subdomain.T, precision=highest))
    finished = jax.scipy.linalg.solve_triangular(factor, iterate.reshape(vec_count, -1), lower=True)
    finished = finished.reshape(iterate.shape)
    return (finished[:, :, band_cols:band_cols + half_cols], finished[:, :, :band_cols], finished[:, :, half_cols + band_cols:])

def reference(vectors, log_kappa):
    basis, left_band, right_band = lax.map(patch_solve, (vectors, log_kappa))
    band_cols = left_band.shape[3]
    zeros = jnp.zeros_like(basis[:1, :, :, :band_cols])
    partner_right = jnp.concatenate([basis[1:, :, :, :band_cols], zeros], axis=0)
    partner_left = jnp.concatenate([zeros, basis[:-1, :, :, band_cols:2 * band_cols]], axis=0)
    right_block = jnp.einsum('pkrc,pjrc->pkj', right_band, partner_right, precision=highest)
    left_block = jnp.einsum('pkrc,pjrc->pkj', left_band, partner_left, precision=highest)
    coupling = jnp.stack((left_block, right_block), axis=1)
    return (basis, coupling)
```

```python
import functools
import math

import jax
import jax.numpy as jnp
from jax import lax
from jax.experimental import pallas as pl
from jax.experimental.pallas import tpu as pltpu
from jax.sharding import PartitionSpec as P

SWEEPS = 8

mass_term = 0.1
lower_bound = 0.05
upper_bound = 2.0
mid_value = 0.5 * (upper_bound + lower_bound)
half_width = 0.5 * (upper_bound - lower_bound)
highest = lax.Precision.HIGHEST

CENTRE = 2.0 * (mid_value - 1.0) / half_width
FACE = 2.0 / half_width

PARAMS = pltpu.CompilerParams(vmem_limit_bytes=40 * 1024 * 1024)


def dot_nt(a, b):
    return lax.dot_general(
        a, b, (((1,), (1,)), ((), ())), precision=highest, preferred_element_type=jnp.float32
    )


def dot_nn(a, b):
    return lax.dot_general(
        a, b, (((1,), (0,)), ((), ())), precision=highest, preferred_element_type=jnp.float32
    )


def shift_columns(x, towards_right):
    axis = x.ndim - 1
    return pltpu.roll(x, 1 if towards_right else x.shape[axis] - 1, axis)


def store_weights(log_row, weights, first, last, alive_of):
    width = weights.shape[-1]
    lane = lax.broadcasted_iota(jnp.int32, (8, width), 1)
    is_first, is_last = lane == 0, lane == width - 1

    def kappa(row):
        return jnp.exp(jnp.broadcast_to(log_row(row), (8, width)))

    def body(row, carry):
        before, centre = carry
        after = kappa(row + 1)
        left = jnp.where(is_first, 1.0, shift_columns(centre, True))
        right = jnp.where(is_last, 1.0, shift_columns(centre, False))
        upper_face = 0.5 * (centre + before)
        lower_face = 0.5 * (centre + after)
        left_face = 0.5 * (centre + left)
        right_face = 0.5 * (centre + right)
        diagonal = upper_face + lower_face + left_face + right_face + mass_term * centre
        scale = FACE * alive_of(row) / diagonal
        weights[row - first, 0] = upper_face * scale
        weights[row - first, 1] = lower_face * scale
        weights[row - first, 2] = jnp.where(is_first, 0.0, left_face * scale)
        weights[row - first, 3] = jnp.where(is_last, 0.0, right_face * scale)
        return centre, after

    lax.fori_loop(first, last + 1, body, (kappa(first - 1), kappa(first)))


def apply_row(now, row, weights, wrow):
    centre = now[row]
    return (
        CENTRE * centre
        + weights[wrow, 0] * now[row - 1]
        + weights[wrow, 1] * now[row + 1]
        + weights[wrow, 2] * shift_columns(centre, True)
        + weights[wrow, 3] * shift_columns(centre, False)
    )


def prepare_kernel(quad, vec, log_kappa, send_a, send_b, sems):
    odd = lax.rem(lax.axis_index(quad), 2)
    count, height, _ = vec.shape
    far = height - SWEEPS
    row_a = pl.multiple_of((1 - odd) * far, 8)
    row_b = pl.multiple_of(odd * far, 8)
    copies = []
    for k, (row, dst) in enumerate(((row_b, send_b), (row_a, send_a))):
        copies.append(
            pltpu.make_async_copy(
                vec.at[:, pl.ds(row, SWEEPS), :], dst.at[pl.ds(0, count)], sems.at[2 * k]
            )
        )
        copies.append(
            pltpu.make_async_copy(
                log_kappa.at[pl.ds(row, SWEEPS), :], dst.at[count], sems.at[2 * k + 1]
            )
        )
    for c in copies:
        c.start()
    for c in copies:
        c.wait()


def blocks_of(value):
    flat = value.reshape(-1, value.shape[-1])
    band = flat.shape[-1] // 4
    return [flat[:, k * band : (k + 1) * band] for k in range(4)]


def fetch_columns(source, slabs, sems):
    copies = []
    for k in range(slabs.shape[0]):
        copy = pltpu.make_async_copy(
            source.at[:, :, pl.ds(128 * k, 128)], slabs.at[k], sems.at[k]
        )
        copy.start()
        copies.append(copy)
    return copies


def field_rows(slabs, group, row):
    height = slabs.shape[2]
    parts = []
    for k in range(slabs.shape[0]):
        flat = slabs.at[k].reshape(slabs.shape[1] * height, 128)
        parts.append(flat[pl.ds(8 * height * group + row, 8, stride=height), :])
    return jnp.concatenate(parts, axis=1)


def field_row(slabs, field, row):
    return jnp.concatenate(
        [slabs[k, field, pl.ds(row, 1), :] for k in range(slabs.shape[0])], axis=1
    )


def inner_kernel(
    quad, vec, halo_a, log_kappa, o0, o1, o2, o3, rim, gram,
    even, odd_buf, weights, vec_slabs, halo_slabs, sems,
):
    odd = lax.rem(lax.axis_index(quad), 2)
    total = even.shape[0]
    groups = even.shape[1]
    height = total - SWEEPS
    count = 8 * groups

    def own_row(row):
        return jnp.where(odd == 1, height - 1 - row, row)

    def halo_row(k):
        return jnp.where(odd == 1, SWEEPS - 1 - k, k)

    copies = fetch_columns(vec, vec_slabs, sems.at[0])
    copies += fetch_columns(halo_a, halo_slabs, sems.at[1])
    for copy in copies:
        copy.wait()

    def load_own(row, carry):
        r = own_row(row)
        for g in range(groups):
            even[row, g] = field_rows(vec_slabs, g, r)
        return carry

    lax.fori_loop(0, height, load_own, 0)

    def load_halo(k, carry):
        r = halo_row(k)
        for g in range(groups):
            even[height + k, g] = field_rows(halo_slabs, g, r)
        return carry

    lax.fori_loop(0, SWEEPS, load_halo, 0)

    def log_row(row):
        inside = log_kappa[pl.ds(own_row(jnp.minimum(row, height - 1)), 1), :]
        outside = field_row(halo_slabs, count, halo_row(jnp.maximum(row - height, 0)))
        return jnp.where(row < height, inside, outside)

    has_a = 1.0
    store_weights(log_row, weights, 1, total - 2, lambda row: has_a)

    bufs = (even, odd_buf)
    for level in range(1, SWEEPS + 1):
        now, new = bufs[(level - 1) % 2], bufs[level % 2]
        rim[level - 1, 0] = now[level - 1]
        rim[level - 1, 1] = now[level]

        def body(row, carry):
            value = apply_row(now, row, weights, row - 1)
            if level == 1:
                new[row] = 0.5 * value
            else:
                new[row] = value - new[row]
            return carry

        lax.fori_loop(level, total - level, body, 0, unroll=2)

    final = bufs[SWEEPS % 2]

    def finish(row, acc):
        parts = blocks_of(final[row + SWEEPS])
        for out, part in zip((o0, o1, o2, o3), parts):
            out[row] = part
        sub = jnp.concatenate(parts[1:3], axis=1)
        return acc + dot_nt(sub, sub)

    gram[...] = lax.fori_loop(
        0, height - SWEEPS, finish, jnp.zeros((count, count), jnp.float32)
    )


def edge_kernel(
    quad, halo_b, log_kappa, rim, gram_inner, o0, o1, o2, o3, gram,
    even, odd_buf, weights, halo_slabs, sems,
):
    index = lax.axis_index(quad)
    odd = lax.rem(index, 2)
    size = lax.axis_size(quad)
    alive = jnp.where(jnp.logical_or(index == 0, index == size - 1), 0.0, 1.0)
    groups = even.shape[1]
    height = log_kappa.shape[0]
    count = 8 * groups

    def halo_row(row):
        return jnp.where(odd == 1, -1 - row, SWEEPS + row)

    for copy in fetch_columns(halo_b, halo_slabs, sems):
        copy.wait()

    def load_halo(k, carry):
        r = halo_row(k - SWEEPS)
        for g in range(groups):
            even[k, g] = field_rows(halo_slabs, g, r)
        return carry

    lax.fori_loop(0, SWEEPS, load_halo, 0)

    def log_row(row):
        own = jnp.maximum(row, 0)
        inside = log_kappa[pl.ds(jnp.where(odd == 1, height - 1 - own, own), 1), :]
        outside = field_row(halo_slabs, count, halo_row(jnp.minimum(row, -1)))
        return jnp.where(row >= 0, inside, outside)

    store_weights(
        log_row, weights, 1 - SWEEPS, SWEEPS - 1, lambda row: jnp.where(row < 0, alive, 1.0)
    )

    bufs = (even, odd_buf)
    for level in range(1, SWEEPS + 1):
        now, new = bufs[(level - 1) % 2], bufs[level % 2]
        now[level + SWEEPS - 1] = rim[level - 1, 0]
        now[level + SWEEPS] = rim[level - 1, 1]

        def body(row, carry):
            value = apply_row(now, row, weights, row - 1)
            if level == 1:
                new[row] = 0.5 * value
            else:
                new[row] = value - new[row]
            return carry

        lax.fori_loop(level, level + SWEEPS, body, 0, unroll=2)

    final = bufs[SWEEPS % 2]
    acc = gram_inner[...]
    for row in range(SWEEPS):
        parts = blocks_of(final[row + SWEEPS])
        for out, part in zip((o0, o1, o2, o3), parts):
            out[row] = part
        sub = jnp.concatenate(parts[1:3], axis=1)
        acc = acc + dot_nt(sub, sub)
    gram[:, : gram.shape[1]] = jnp.zeros(gram.shape, jnp.float32)
    gram[:, :count] = acc


def product_kernel(
    left_in, left_edge, right_in, right_edge, from_left, from_left_edge, from_right,
    from_right_edge, gram, gram_left, gram_right, out,
):
    count = out.shape[0]

    def products(inner, edge, theirs, theirs_edge):
        def pair(a, b, k):
            x = jnp.concatenate([a[2 * k], a[2 * k + 1]], axis=1)
            y = jnp.concatenate([b[2 * k], b[2 * k + 1]], axis=1)
            return dot_nt(x, y)

        acc = lax.fori_loop(
            0,
            inner.shape[0] // 2,
            lambda k, acc: acc + pair(inner, theirs, k),
            jnp.zeros((count, count), jnp.float32),
        )
        for k in range(edge.shape[0] // 2):
            acc = acc + pair(edge, theirs_edge, k)
        return acc

    left = products(left_in, left_edge, from_left, from_left_edge)
    right = products(right_in, right_edge, from_right, from_right_edge)
    out[...] = jnp.zeros(out.shape, jnp.float32)
    mats = (gram[:, :count], gram_left[:, :count], gram_right[:, :count], left, right)
    for k, mat in enumerate(mats):
        out[:, k * count : (k + 1) * count] = mat


def final_kernel(
    quad, patch, gathered, s1, s1_edge, s2, s2_edge, basis, coupling, slabs, sems
):
    odd = lax.rem(lax.axis_index(quad), 2)
    place = lax.axis_index(patch)
    last = lax.axis_size(patch) - 1
    inner_rows, count, band = s1.shape
    height = inner_rows + SWEEPS
    total = gathered[0]
    for k in range(1, gathered.shape[0]):
        total = total + gathered[k]
    lanes = total.shape[1]
    mats = [total[:, k * count : (k + 1) * count] for k in range(5)]
    eye = (
        lax.broadcasted_iota(jnp.int32, (count, count), 0)
        == lax.broadcasted_iota(jnp.int32, (count, count), 1)
    ).astype(jnp.float32)
    missing = (None, place == 0, place == last)
    sub = lax.broadcasted_iota(jnp.int32, (count, lanes), 0)
    lane = lax.broadcasted_iota(jnp.int32, (count, lanes), 1)
    inverses = []
    for k in range(3):
        mat = mats[k] if missing[k] is None else jnp.where(missing[k], eye, mats[k])
        work = jnp.concatenate(
            [mat, eye, jnp.zeros((count, lanes - 2 * count), jnp.float32)], axis=1
        )
        for j in range(count - 1):
            pivot = work[j : j + 1, :]
            column = work[:, j : j + 1]
            ratio = jnp.where(sub > j, column / work[j : j + 1, j : j + 1], 0.0)
            work = work - ratio * pivot
        diagonal = jnp.sum(jnp.where(sub == lane, work, 0.0), axis=1, keepdims=True)
        inverses.append((work / jnp.sqrt(diagonal))[:, count : 2 * count])
    own, left, right = inverses
    coupling[0] = dot_nt(dot_nn(own, mats[3]), left)
    coupling[1] = dot_nt(dot_nn(own, mats[4]), right)

    def write(first, row, a, b):
        place_row = first + row
        r = jnp.where(odd == 1, height - 1 - place_row, place_row)
        value = dot_nn(own, jnp.concatenate([a[row], b[row]], axis=1))
        for k in range(2):
            flat = slabs.at[k].reshape(count * height, 128)
            for g in range(count // 8):
                flat[pl.ds(8 * height * g + r, 8, stride=height), :] = value[
                    8 * g : 8 * g + 8, 128 * k : 128 * k + 128
                ]

    lax.fori_loop(0, SWEEPS, lambda row, c: (write(0, row, s1_edge, s2_edge), c)[1], 0)
    lax.fori_loop(0, inner_rows, lambda row, c: (write(SWEEPS, row, s1, s2), c)[1], 0)
    copies = [
        pltpu.make_async_copy(slabs.at[k], basis.at[:, :, pl.ds(128 * k, 128)], sems.at[k])
        for k in range(2)
    ]
    for copy in copies:
        copy.start()
    for copy in copies:
        copy.wait()


def on_device(vectors, log_kappa):
    vec = vectors[0]
    log_own = log_kappa[0]
    count, height, width = vec.shape
    band = width // 4
    groups = count // 8
    f32 = jnp.float32
    patch_size, quad_size = lax.axis_size("patch"), lax.axis_size("quad")

    def shape(*dims):
        return jax.ShapeDtypeStruct(dims, f32)

    any_space = pl.BlockSpec(memory_space=pl.ANY)
    vmem_space = pl.BlockSpec(memory_space=pltpu.VMEM)
    send_a, send_b = pl.pallas_call(
        functools.partial(prepare_kernel, "quad"),
        out_shape=(shape(count + 1, SWEEPS, width),) * 2,
        in_specs=[any_space, any_space],
        out_specs=(any_space, any_space),
        scratch_shapes=[pltpu.SemaphoreType.DMA((4,))],
    )(vec, log_own)
    same_chip = [(i, i ^ 1) for i in range(quad_size)]
    other_chip = [
        (i, j)
        for i in range(quad_size)
        for j in (i - 1, i + 1)
        if 0 <= j < quad_size and i // 2 != j // 2
    ]
    halo_a = lax.ppermute(send_a, "quad", same_chip)
    halo_b = lax.ppermute(send_b, "quad", other_chip)
    inner = height - SWEEPS
    total = height + SWEEPS
    cost = 12 * count * width * SWEEPS * height
    *inner_parts, rim, gram_inner = pl.pallas_call(
        functools.partial(inner_kernel, "quad"),
        out_shape=(shape(inner, count, band),) * 4
        + (shape(SWEEPS, 2, groups, 8, width), shape(count, count)),
        scratch_shapes=[
            pltpu.VMEM((total, groups, 8, width), f32),
            pltpu.VMEM((total, groups, 8, width), f32),
            pltpu.VMEM((total - 2, 4, 8, width), f32),
            pltpu.VMEM((4, count, height, 128), f32),
            pltpu.VMEM((4, count + 1, SWEEPS, 128), f32),
            pltpu.SemaphoreType.DMA((2, 4)),
        ],
        in_specs=[any_space, any_space, vmem_space],
        compiler_params=PARAMS,
        cost_estimate=pl.CostEstimate(flops=cost, bytes_accessed=5 << 20, transcendentals=0),
    )(vec, halo_a, log_own)
    from_right_in = shifted(inner_parts[1], "patch", -1)
    from_left_in = shifted(inner_parts[2], "patch", 1)
    *edge_parts, gram = pl.pallas_call(
        functools.partial(edge_kernel, "quad"),
        out_shape=(shape(SWEEPS, count, band),) * 4 + (shape(count, 128),),
        scratch_shapes=[
            pltpu.VMEM((2 * SWEEPS + 1, groups, 8, width), f32),
            pltpu.VMEM((2 * SWEEPS + 1, groups, 8, width), f32),
            pltpu.VMEM((2 * SWEEPS - 1, 4, 8, width), f32),
            pltpu.VMEM((4, count + 1, SWEEPS, 128), f32),
            pltpu.SemaphoreType.DMA((4,)),
        ],
        in_specs=[any_space] + [vmem_space] * 3,
        compiler_params=PARAMS,
    )(halo_b, log_own, rim, gram_inner)
    right_pack = jnp.concatenate([edge_parts[1], gram[None]], axis=0)
    left_pack = jnp.concatenate([edge_parts[2], gram[None]], axis=0)
    from_right_edge = shifted(right_pack, "patch", -1)
    from_left_edge = shifted(left_pack, "patch", 1)
    packed = pl.pallas_call(
        product_kernel,
        out_shape=shape(count, 128),
        compiler_params=PARAMS,
    )(
        inner_parts[0], edge_parts[0], inner_parts[3], edge_parts[3],
        from_left_in, from_left_edge[:SWEEPS], from_right_in, from_right_edge[:SWEEPS],
        gram, from_left_edge[SWEEPS], from_right_edge[SWEEPS],
    )
    gathered = lax.all_gather(packed, "quad")
    basis, coupling = pl.pallas_call(
        functools.partial(final_kernel, "quad", "patch"),
        out_shape=(shape(count, height, 2 * band), shape(2, count, count)),
        out_specs=(any_space, vmem_space),
        scratch_shapes=[
            pltpu.VMEM((2, count, height, 128), f32),
            pltpu.SemaphoreType.DMA((2,)),
        ],
        compiler_params=PARAMS,
    )(gathered, inner_parts[1], edge_parts[1], inner_parts[2], edge_parts[2])
    return basis[None], coupling[None]


def shifted(block, axis, distance):
    devices = range(lax.axis_size(axis))
    route = [(i - distance, i) for i in devices if i - distance in devices]
    return lax.ppermute(block, axis, route)


def solution(mesh):
    placed = (P("patch", None, "quad", None), P("patch", "quad", None))
    return jax.shard_map(
        on_device,
        mesh=mesh,
        in_specs=placed,
        out_specs=(P("patch", None, "quad", None), P("patch", None, None, None)),
        check_vma=False,
    )
```

```python
import functools

import jax
import jax.numpy as jnp
from jax import lax
from jax.experimental import pallas as pl
from jax.experimental.pallas import tpu as pltpu
from jax.sharding import PartitionSpec as P

SWEEPS = 8

mass_term = 0.1
lower_bound = 0.05
upper_bound = 2.0
mid_value = 0.5 * (upper_bound + lower_bound)
half_width = 0.5 * (upper_bound - lower_bound)
highest = lax.Precision.HIGHEST
f32 = jnp.float32
bf16 = jnp.bfloat16

CENTRE = 2.0 * (mid_value - 1.0) / half_width
FACE = 2.0 / half_width

BLOCKS = 4
LANES = 128

PARAMS = pltpu.CompilerParams(vmem_limit_bytes=40 * 1024 * 1024)
ANY = pl.BlockSpec(memory_space=pl.ANY)
VMEM = pl.BlockSpec(memory_space=pltpu.VMEM)


def shape(*dims):
    return jax.ShapeDtypeStruct(dims, f32)


def dot_nt(a, b, precision=None):
    return lax.dot_general(
        a, b, (((1,), (1,)), ((), ())), precision=precision, preferred_element_type=f32
    )


def dot_nn(a, b, precision=None):
    return lax.dot_general(
        a, b, (((1,), (0,)), ((), ())), precision=precision, preferred_element_type=f32
    )


def three_parts(x):
    high = x.astype(bf16).astype(f32)
    rest = x - high
    middle = rest.astype(bf16).astype(f32)
    return jnp.concatenate([high, middle, rest - middle], axis=0).astype(bf16)


def two_parts(x):
    high = x.astype(bf16).astype(f32)
    return jnp.concatenate([high, x - high], axis=0).astype(bf16)


def gram_product(x, y):
    n, m = x.shape[0], y.shape[0]
    full = dot_nt(two_parts(x), two_parts(y))
    return (full[:n, :m] + full[n:, :m]) + (full[:n, m:] + full[n:, m:])


def permutation(width, inverse):
    row = lax.broadcasted_iota(jnp.int32, (width, width), 0)
    col = lax.broadcasted_iota(jnp.int32, (width, width), 1)
    if inverse:
        row, col = col, row
    target = (row % BLOCKS) * LANES + row // BLOCKS
    return jnp.where(target == col, 1.0, 0.0).astype(bf16)


def permute_columns(x, matrix):
    n = x.shape[0]
    out = dot_nn(three_parts(x), matrix)
    return (out[:n] + out[n : 2 * n]) + out[2 * n :]


def blocks_of(value):
    return [value[..., k * LANES : (k + 1) * LANES] for k in range(BLOCKS)]


def left_neighbour(x):
    b = blocks_of(x)
    axis = x.ndim - 1
    return jnp.concatenate([pltpu.roll(b[-1], 1, axis)] + b[:-1], axis=axis)


def right_neighbour(x):
    b = blocks_of(x)
    axis = x.ndim - 1
    return jnp.concatenate(b[1:] + [pltpu.roll(b[0], LANES - 1, axis)], axis=axis)


def face_weights(logs, alive):
    n, width = logs.shape
    kappa = jnp.exp(logs)
    rows = lax.slice_in_dim
    centre = rows(kappa, 8, n - 8, axis=0)
    before = rows(kappa, 7, n - 9, axis=0)
    after = rows(kappa, 9, n - 7, axis=0)
    lane = lax.broadcasted_iota(jnp.int32, centre.shape, 1)
    is_first, is_last = lane == 0, lane == width - 1
    left = jnp.where(is_first, 1.0, left_neighbour(centre))
    right = jnp.where(is_last, 1.0, right_neighbour(centre))
    upper_face = 0.5 * (centre + before)
    lower_face = 0.5 * (centre + after)
    left_face = 0.5 * (centre + left)
    right_face = 0.5 * (centre + right)
    diagonal = upper_face + lower_face + left_face + right_face + mass_term * centre
    scale = FACE * alive / diagonal
    return (
        upper_face * scale,
        lower_face * scale,
        jnp.where(is_first, 0.0, left_face * scale),
        jnp.where(is_last, 0.0, right_face * scale),
    )


def spread_weights(natural, weights, count, natural_row, odd):
    width = weights.shape[-1]

    def body(k, carry):
        r = natural_row(k)
        for i in range(4):
            source = jnp.where(odd == 1, 1 - i, i) if i < 2 else i
            weights[k, i] = jnp.broadcast_to(natural[source, pl.ds(r, 1), :], (8, width))
        return carry

    lax.fori_loop(0, count, body, 0, unroll=2)


def apply_row(now, row, weights, wrow):
    centre = now[row]
    return (
        CENTRE * centre
        + weights[wrow, 0] * now[row - 1]
        + weights[wrow, 1] * now[row + 1]
        + (weights[wrow, 2] * left_neighbour(centre) + weights[wrow, 3] * right_neighbour(centre))
    )


def sweep(level, now, new, weights, first, last, wfirst):
    def body(row, carry):
        value = apply_row(now, row, weights, row - wfirst)
        if level == 1:
            new[row] = 0.5 * value
        else:
            new[row] = value - new[row]
        return carry

    lax.fori_loop(first, last, body, 0, unroll=2)


def fetch_columns(source, slabs, sems):
    copies = []
    for k in range(slabs.shape[0]):
        copy = pltpu.make_async_copy(
            source.at[:, :, pl.ds(LANES * k, LANES)], slabs.at[k], sems.at[k]
        )
        copy.start()
        copies.append(copy)
    return copies


def rows_of_fields(slabs, rows, groups):
    height = slabs.shape[2]
    pieces = []
    for r in rows:
        for g in range(groups):
            parts = []
            for k in range(slabs.shape[0]):
                flat = slabs.at[k].reshape(slabs.shape[1] * height, LANES)
                parts.append(flat[pl.ds(8 * height * g + r, 8, stride=height), :])
            pieces.append(jnp.concatenate(parts, axis=1))
    return jnp.concatenate(pieces, axis=0)


def field_block(slabs, field):
    return jnp.concatenate([slabs[k, field] for k in range(slabs.shape[0])], axis=1)


def load_rows(slabs, target, first, natural_row, groups, matrix):
    rows = [natural_row(k) for k in range(8)]
    x = permute_columns(rows_of_fields(slabs, rows, groups), matrix)
    width = x.shape[1]
    target[pl.ds(first, 8)] = x.reshape(8, groups, 8, width)


def emit(final, first, count, groups, matrix, swap, outs, out_first):
    outer_left, outer_right, sub, send_right_pair, send_left_pair = outs
    width = final.shape[-1]
    x = final[pl.ds(first, 8)].reshape(8 * count, width)
    x = permute_columns(x, matrix).reshape(8, count, width)
    b = blocks_of(x)
    at = pl.ds(out_first, 8)
    outer_left[at] = b[0]
    outer_right[at] = b[3]
    sub[at] = jnp.concatenate(b[1:3], axis=2)
    send_right_pair[at] = jnp.where(swap, b[1], b[2])
    send_left_pair[at] = jnp.where(swap, b[2], b[1])


def rows_as_columns(ref, first, count):
    return jnp.concatenate([ref[first + k] for k in range(count)], axis=1)


def prepare_kernel(quad, vec, log_kappa, send_a, send_b, sems):
    odd = lax.rem(lax.axis_index(quad), 2)
    count, height, _ = vec.shape
    far = height - SWEEPS
    row_a = pl.multiple_of((1 - odd) * far, 8)
    row_b = pl.multiple_of(odd * far, 8)
    copies = []
    for k, (row, dst) in enumerate(((row_b, send_b), (row_a, send_a))):
        copies.append(
            pltpu.make_async_copy(
                vec.at[:, pl.ds(row, SWEEPS), :], dst.at[pl.ds(0, count)], sems.at[2 * k]
            )
        )
        copies.append(
            pltpu.make_async_copy(
                log_kappa.at[pl.ds(row, SWEEPS), :], dst.at[count], sems.at[2 * k + 1]
            )
        )
    for c in copies:
        c.start()
    for c in copies:
        c.wait()


def inner_kernel(
    quad, patch, vec, halo_a, log_kappa,
    outer_left, outer_right, sub, send_right, send_left, rim, gram,
    even, odd_buf, weights, vec_slabs, halo_slabs, logs, natural, sems,
):
    odd = lax.rem(lax.axis_index(quad), 2)
    swap = lax.rem(lax.axis_index(patch), 2) == 1
    total, groups = even.shape[:2]
    height = total - SWEEPS
    count = 8 * groups
    width = even.shape[-1]
    copies = fetch_columns(vec, vec_slabs, sems.at[0])
    copies += fetch_columns(halo_a, halo_slabs, sems.at[1])
    matrix = permutation(width, False)
    logs[...] = jnp.zeros(logs.shape, f32)
    logs[pl.ds(16, height)] = permute_columns(log_kappa[...], matrix)
    for copy in copies:
        copy.wait()
    below = pl.multiple_of(8 + (1 - odd) * (height + 8), 8)
    logs[pl.ds(below, 8)] = permute_columns(field_block(halo_slabs, count), matrix)
    values = face_weights(logs[...], 1.0)
    for i in range(4):
        natural[i] = values[i]

    def natural_row(k):
        return jnp.where(odd == 1, height + 7 - k, k + 8)

    def own_row(k):
        return jnp.where(odd == 1, height - 1 - k, k)

    def load(block, carry):
        first = pl.multiple_of(8 * block, 8)
        load_rows(vec_slabs, even, first, lambda k: own_row(first + k), groups, matrix)
        return carry

    lax.fori_loop(0, height // 8, load, 0)
    load_rows(
        halo_slabs, even, height, lambda k: jnp.where(odd == 1, 7 - k, k), groups, matrix
    )
    spread_weights(natural, weights, total - 2, lambda k: natural_row(k + 1), odd)

    bufs = (even, odd_buf)
    for level in range(1, SWEEPS + 1):
        now, new = bufs[(level - 1) % 2], bufs[level % 2]
        rim[level - 1, 0] = now[level - 1]
        rim[level - 1, 1] = now[level]
        sweep(level, now, new, weights, level, total - level, 1)

    final = bufs[SWEEPS % 2]
    back = permutation(width, True)
    outs = (outer_left, outer_right, sub, send_right, send_left)

    def finish(block, carry):
        row = pl.multiple_of(8 * block, 8)
        emit(final, row + 8, count, groups, back, swap, outs, row)
        return carry

    lax.fori_loop(0, (height - SWEEPS) // 8, finish, 0)
    x = rows_as_columns(sub, 0, height - SWEEPS)
    gram[...] = gram_product(x, x)


def edge_kernel(
    quad, patch, halo_b, log_kappa, rim, gram_inner, send_right_in, send_left_in,
    outer_left, outer_right, sub, send_right, send_left,
    even, odd_buf, weights, halo_slabs, logs, natural, sems,
):
    index = lax.axis_index(quad)
    odd = lax.rem(index, 2)
    swap = lax.rem(lax.axis_index(patch), 2) == 1
    size = lax.axis_size(quad)
    alive = jnp.where(jnp.logical_or(index == 0, index == size - 1), 0.0, 1.0)
    groups = even.shape[1]
    width = even.shape[-1]
    height = log_kappa.shape[0]
    count = 8 * groups
    copies = fetch_columns(halo_b, halo_slabs, sems)
    matrix = permutation(width, False)
    logs[...] = jnp.zeros(logs.shape, f32)
    own_at = pl.multiple_of(odd * (height - 16), 8)
    place = pl.multiple_of(16 - 8 * odd, 8)
    logs[pl.ds(place, 16)] = permute_columns(log_kappa[pl.ds(own_at, 16), :], matrix)
    for copy in copies:
        copy.wait()
    halo_at = pl.multiple_of(8 + 16 * odd, 8)
    logs[pl.ds(halo_at, 8)] = permute_columns(field_block(halo_slabs, count), matrix)
    position = lax.broadcasted_iota(jnp.int32, (24, width), 0)
    outside = jnp.logical_and(position >= 16 * odd, position < 8 + 16 * odd)
    values = face_weights(logs[...], jnp.where(outside, alive, 1.0))
    for i in range(4):
        natural[i] = values[i]

    load_rows(
        halo_slabs, even, 0, lambda k: jnp.where(odd == 1, 7 - k, k), groups, matrix
    )
    spread_weights(
        natural, weights, 15, lambda k: jnp.where(odd == 1, 22 - k, k + 1), odd
    )

    bufs = (even, odd_buf)
    for level in range(1, SWEEPS + 1):
        now, new = bufs[(level - 1) % 2], bufs[level % 2]
        now[level + SWEEPS - 1] = rim[level - 1, 0]
        now[level + SWEEPS] = rim[level - 1, 1]
        sweep(level, now, new, weights, level, level + SWEEPS, 1)

    final = bufs[SWEEPS % 2]
    back = permutation(width, True)
    emit(final, SWEEPS, count, groups, back, swap, (outer_left, outer_right, sub, send_right, send_left), 0)
    x = rows_as_columns(sub, 0, SWEEPS)
    total = gram_inner[...] + gram_product(x, x)
    inner = height - SWEEPS
    for out, source in ((send_right, send_right_in), (send_left, send_left_in)):
        out[pl.ds(SWEEPS, inner)] = source[...]
        out[height] = jnp.zeros((count, LANES), f32)
        out[height, :, :count] = total


def product_kernel(
    patch, left_in, left_edge, right_in, right_edge, from_right_pair, from_left_pair, sent, out
):
    swap = lax.rem(lax.axis_index(patch), 2) == 1
    count = out.shape[0]
    inner = left_in.shape[0]
    height = inner + SWEEPS

    def products(mine, mine_edge, theirs):
        x = jnp.concatenate(
            [rows_as_columns(mine_edge, 0, SWEEPS), rows_as_columns(mine, 0, inner)], axis=1
        )
        return gram_product(x, rows_as_columns(theirs, 0, height))

    out[...] = jnp.zeros(out.shape, f32)

    def write(from_left, from_right):
        mats = (
            sent[height, :, :count],
            from_left[height, :, :count],
            from_right[height, :, :count],
            products(left_in, left_edge, from_left),
            products(right_in, right_edge, from_right),
        )
        for k, mat in enumerate(mats):
            out[:, k * count : (k + 1) * count] = mat

    @pl.when(swap)
    def _():
        write(from_right_pair, from_left_pair)

    @pl.when(jnp.logical_not(swap))
    def _():
        write(from_left_pair, from_right_pair)


def inverse_factor(mat, eye, lanes):
    count = mat.shape[0]
    sub = lax.broadcasted_iota(jnp.int32, (count, lanes), 0)
    lane = lax.broadcasted_iota(jnp.int32, (count, lanes), 1)
    work = jnp.concatenate([mat, eye, jnp.zeros((count, lanes - 2 * count), f32)], axis=1)
    for j in range(count - 1):
        pivot = work[j : j + 1, :]
        column = work[:, j : j + 1]
        ratio = jnp.where(sub > j, column / work[j : j + 1, j : j + 1], 0.0)
        work = work - ratio * pivot
    diagonal = jnp.sum(jnp.where(sub == lane, work, 0.0), axis=1, keepdims=True)
    return (work / jnp.sqrt(diagonal))[:, count : 2 * count]


def final_kernel(quad, patch, gathered, sub_in, sub_edge, basis, coupling, slabs, sems):
    odd = lax.rem(lax.axis_index(quad), 2)
    place = lax.axis_index(patch)
    last = lax.axis_size(patch) - 1
    inner, count, sub_width = sub_in.shape
    height = inner + SWEEPS
    total = gathered[0]
    for k in range(1, gathered.shape[0]):
        total = total + gathered[k]
    lanes = total.shape[1]
    mats = [total[:, k * count : (k + 1) * count] for k in range(5)]
    eye = (
        lax.broadcasted_iota(jnp.int32, (count, count), 0)
        == lax.broadcasted_iota(jnp.int32, (count, count), 1)
    ).astype(f32)
    own = inverse_factor(mats[0], eye, lanes)
    left = inverse_factor(jnp.where(place == 0, eye, mats[1]), eye, lanes)
    right = inverse_factor(jnp.where(place == last, eye, mats[2]), eye, lanes)
    coupling[0] = dot_nt(dot_nn(own, mats[3], highest), left, highest)
    coupling[1] = dot_nt(dot_nn(own, mats[4], highest), right, highest)

    high = own.astype(bf16).astype(f32)
    low = own - high
    factor = jnp.concatenate([high, high, low, low], axis=1).astype(bf16)

    def write(source, row, place_row):
        r = jnp.where(odd == 1, height - 1 - place_row, place_row)
        x = source[row]
        x_high = x.astype(bf16).astype(f32)
        x_low = x - x_high
        value = dot_nn(
            factor, jnp.concatenate([x_high, x_low, x_high, x_low], axis=0).astype(bf16)
        )
        for k in range(sub_width // LANES):
            flat = slabs.at[k].reshape(count * height, LANES)
            for g in range(count // 8):
                flat[pl.ds(8 * height * g + r, 8, stride=height), :] = value[
                    8 * g : 8 * g + 8, LANES * k : LANES * (k + 1)
                ]

    lax.fori_loop(0, SWEEPS, lambda row, c: (write(sub_edge, row, row), c)[1], 0, unroll=4)
    lax.fori_loop(
        0, inner, lambda row, c: (write(sub_in, row, row + SWEEPS), c)[1], 0, unroll=4
    )
    copies = [
        pltpu.make_async_copy(
            slabs.at[k], basis.at[:, :, pl.ds(LANES * k, LANES)], sems.at[k]
        )
        for k in range(sub_width // LANES)
    ]
    for copy in copies:
        copy.start()
    for copy in copies:
        copy.wait()


def call_prepare(vec, log_own):
    count, _, width = vec.shape
    return pl.pallas_call(
        functools.partial(prepare_kernel, "quad"),
        out_shape=(shape(count + 1, SWEEPS, width),) * 2,
        in_specs=[ANY, ANY],
        out_specs=(VMEM, VMEM),
        scratch_shapes=[pltpu.SemaphoreType.DMA((4,))],
        compiler_params=PARAMS,
        name="prepare",
    )(vec, log_own)


def call_inner(vec, halo_a, log_own):
    count, height, width = vec.shape
    band, groups, inner, total = width // 4, count // 8, height - SWEEPS, height + SWEEPS
    cost = 12 * count * width * SWEEPS * height
    return pl.pallas_call(
        functools.partial(inner_kernel, "quad", "patch"),
        out_shape=(
            shape(inner, count, band),
            shape(inner, count, band),
            shape(inner, count, 2 * band),
            shape(inner, count, band),
            shape(inner, count, band),
            shape(SWEEPS, 2, groups, 8, width),
            shape(count, count),
        ),
        scratch_shapes=[
            pltpu.VMEM((total, groups, 8, width), f32),
            pltpu.VMEM((total, groups, 8, width), f32),
            pltpu.VMEM((total - 2, 4, 8, width), f32),
            pltpu.VMEM((width // LANES, count, height, LANES), f32),
            pltpu.VMEM((width // LANES, count + 1, SWEEPS, LANES), f32),
            pltpu.VMEM((height + 32, width), f32),
            pltpu.VMEM((4, height + 16, width), f32),
            pltpu.SemaphoreType.DMA((2, width // LANES)),
        ],
        in_specs=[ANY, ANY, VMEM],
        compiler_params=PARAMS,
        cost_estimate=pl.CostEstimate(flops=cost, bytes_accessed=5 << 20, transcendentals=0),
        name="inner",
    )(vec, halo_a, log_own)


def call_edge(halo_b, log_own, rim, gram_inner, send_right, send_left):
    height, width = log_own.shape
    inner, count, band = send_right.shape
    groups = count // 8
    return pl.pallas_call(
        functools.partial(edge_kernel, "quad", "patch"),
        out_shape=(
            shape(SWEEPS, count, band),
            shape(SWEEPS, count, band),
            shape(SWEEPS, count, 2 * band),
            shape(height + 1, count, band),
            shape(height + 1, count, band),
        ),
        scratch_shapes=[
            pltpu.VMEM((2 * SWEEPS + 1, groups, 8, width), f32),
            pltpu.VMEM((2 * SWEEPS + 1, groups, 8, width), f32),
            pltpu.VMEM((2 * SWEEPS - 1, 4, 8, width), f32),
            pltpu.VMEM((width // LANES, count + 1, SWEEPS, LANES), f32),
            pltpu.VMEM((40, width), f32),
            pltpu.VMEM((4, 24, width), f32),
            pltpu.SemaphoreType.DMA((width // LANES,)),
        ],
        in_specs=[ANY] + [VMEM] * 5,
        compiler_params=PARAMS,
        name="edge",
    )(halo_b, log_own, rim, gram_inner, send_right, send_left)


def call_product(left_in, left_edge, right_in, right_edge, from_right_pair, from_left_pair, sent):
    count = left_in.shape[1]
    return pl.pallas_call(
        functools.partial(product_kernel, "patch"),
        out_shape=shape(count, LANES),
        compiler_params=PARAMS,
        name="product",
    )(left_in, left_edge, right_in, right_edge, from_right_pair, from_left_pair, sent)


def call_final(gathered, sub_in, sub_edge):
    inner, count, sub_width = sub_in.shape
    height = inner + SWEEPS
    return pl.pallas_call(
        functools.partial(final_kernel, "quad", "patch"),
        out_shape=(shape(count, height, sub_width), shape(2, count, count)),
        out_specs=(ANY, VMEM),
        scratch_shapes=[
            pltpu.VMEM((sub_width // LANES, count, height, LANES), f32),
            pltpu.SemaphoreType.DMA((sub_width // LANES,)),
        ],
        compiler_params=PARAMS,
        name="final",
    )(gathered, sub_in, sub_edge)


def pairs(size, first):
    swaps = [(i, i + 1) for i in range(first, size - 1, 2)]
    return swaps + [(j, i) for i, j in swaps]


def on_device(vectors, log_kappa):
    vec, log_own = vectors[0], log_kappa[0]
    patch_size, quad_size = lax.axis_size("patch"), lax.axis_size("quad")
    send_a, send_b = call_prepare(vec, log_own)
    halo_a = lax.ppermute(send_a, "quad", pairs(quad_size, 0))
    halo_b = lax.ppermute(send_b, "quad", pairs(quad_size, 1))
    left_in, right_in, sub_in, send_1_in, send_2_in, rim, gram_in = call_inner(
        vec, halo_a, log_own
    )
    left_edge, right_edge, sub_edge, send_1, send_2 = call_edge(
        halo_b, log_own, rim, gram_in, send_1_in, send_2_in
    )
    from_2 = lax.ppermute(send_2, "patch", pairs(patch_size, 1))
    from_1 = lax.ppermute(send_1, "patch", pairs(patch_size, 0))
    packed = call_product(left_in, left_edge, right_in, right_edge, from_1, from_2, send_1)
    gathered = lax.all_gather(packed, "quad")
    basis, coupling = call_final(gathered, sub_in, sub_edge)
    return basis[None], coupling[None]


def solution(mesh):
    placed = (P("patch", None, "quad", None), P("patch", "quad", None))
    return jax.shard_map(
        on_device,
        mesh=mesh,
        in_specs=placed,
        out_specs=(P("patch", None, "quad", None), P("patch", None, None, None)),
        check_vma=False,
    )
```

```python
import functools

import jax
import jax.numpy as jnp
from jax import lax
from jax.experimental import pallas as pl
from jax.experimental.pallas import tpu as pltpu
from jax.sharding import PartitionSpec as P

SWEEPS = 8

mass_term = 0.1
lower_bound = 0.05
upper_bound = 2.0
mid_value = 0.5 * (upper_bound + lower_bound)
half_width = 0.5 * (upper_bound - lower_bound)
highest = lax.Precision.HIGHEST
f32 = jnp.float32
bf16 = jnp.bfloat16

CENTRE = 2.0 * (mid_value - 1.0) / half_width
FACE = 2.0 / half_width

BLOCKS = 4
LANES = 128
CHUNK = 8
PAD = 8

PARAMS = pltpu.CompilerParams(vmem_limit_bytes=40 * 1024 * 1024)
ANY = pl.BlockSpec(memory_space=pl.ANY)
VMEM = pl.BlockSpec(memory_space=pltpu.VMEM)


def shape(*dims):
    return jax.ShapeDtypeStruct(dims, f32)


def dot_nt(a, b, precision=None):
    return lax.dot_general(
        a, b, (((1,), (1,)), ((), ())), precision=precision, preferred_element_type=f32
    )


def dot_nn(a, b, precision=None):
    return lax.dot_general(
        a, b, (((1,), (0,)), ((), ())), precision=precision, preferred_element_type=f32
    )


def two_parts(x):
    high = x.astype(bf16).astype(f32)
    return jnp.concatenate([high, x - high], axis=0).astype(bf16)


def gram_product(x, y):
    n, m = x.shape[0], y.shape[0]
    full = dot_nt(two_parts(x), two_parts(y))
    return (full[:n, :m] + full[n:, :m]) + (full[:n, m:] + full[n:, m:])


def permutation(width, inverse):
    row = lax.broadcasted_iota(jnp.int32, (width, width), 0)
    col = lax.broadcasted_iota(jnp.int32, (width, width), 1)
    if inverse:
        row, col = col, row
    target = (row % BLOCKS) * LANES + row // BLOCKS
    return jnp.where(target == col, 1.0, 0.0).astype(bf16)


def permute_columns(x, matrix):
    n = x.shape[0]
    out = dot_nn(two_parts(x), matrix)
    return out[:n] + out[n:]


def blocks_of(value):
    return [value[..., k * LANES : (k + 1) * LANES] for k in range(BLOCKS)]


def left_neighbour(x):
    b = blocks_of(x)
    axis = x.ndim - 1
    return jnp.concatenate([pltpu.roll(b[-1], 1, axis)] + b[:-1], axis=axis)


def right_neighbour(x):
    b = blocks_of(x)
    axis = x.ndim - 1
    return jnp.concatenate(b[1:] + [pltpu.roll(b[0], LANES - 1, axis)], axis=axis)


def face_weights(logs, alive):
    n, width = logs.shape
    kappa = jnp.exp(logs)
    rows = lax.slice_in_dim
    centre = rows(kappa, 8, n - 8, axis=0)
    before = rows(kappa, 7, n - 9, axis=0)
    after = rows(kappa, 9, n - 7, axis=0)
    lane = lax.broadcasted_iota(jnp.int32, centre.shape, 1)
    is_first, is_last = lane == 0, lane == width - 1
    left = jnp.where(is_first, 1.0, left_neighbour(centre))
    right = jnp.where(is_last, 1.0, right_neighbour(centre))
    upper_face = 0.5 * (centre + before)
    lower_face = 0.5 * (centre + after)
    left_face = 0.5 * (centre + left)
    right_face = 0.5 * (centre + right)
    diagonal = upper_face + lower_face + left_face + right_face + mass_term * centre
    scale = FACE * alive / diagonal
    return (
        upper_face * scale,
        lower_face * scale,
        jnp.where(is_first, 0.0, left_face * scale),
        jnp.where(is_last, 0.0, right_face * scale),
    )


def spread_weights(natural, weights, count, natural_row, odd):
    width = weights.shape[-1]

    def body(k, carry):
        r = natural_row(k)
        for i in range(4):
            source = jnp.where(odd == 1, 1 - i, i) if i < 2 else i
            weights[k, i] = jnp.broadcast_to(natural[source, pl.ds(r, 1), :], (8, width))
        return carry

    lax.fori_loop(0, count, body, 0, unroll=2)


def apply_row(now, row, weights, wrow):
    centre = now[row]
    return (
        CENTRE * centre
        + weights[wrow, 0] * now[row - 1]
        + weights[wrow, 1] * now[row + 1]
        + (weights[wrow, 2] * left_neighbour(centre) + weights[wrow, 3] * right_neighbour(centre))
    )


def row_loop(first, last, chunk, body):
    whole = (last - first) // chunk

    def step(k, carry):
        for i in range(chunk):
            body(first + chunk * k + i)
        return carry

    if whole > 1:
        lax.fori_loop(0, whole, step, 0)
    elif whole == 1:
        step(0, 0)
    for row in range(first + whole * chunk, last):
        body(row)


def sweep(level, now, new, weights, first, last, wfirst):
    def body(row):
        value = apply_row(now, row, weights, row - wfirst)
        if level == 1:
            new[row] = 0.5 * value
        else:
            new[row] = value - new[row]

    row_loop(first, last, CHUNK, body)


def fetch_columns(source, slabs, sems, rows=0):
    copies = []
    for k in range(slabs.shape[0]):
        copy = pltpu.make_async_copy(
            source.at[:, pl.ds(rows, 8), pl.ds(LANES * k, LANES)],
            slabs.at[k, :, pl.ds(rows, 8)],
            sems.at[k],
        )
        copy.start()
        copies.append(copy)
    return copies


def wait_all(copies):
    for copy in copies:
        copy.wait()


def rows_of_fields(slabs, rows, groups):
    height = slabs.shape[2]
    pieces = []
    for r in rows:
        for g in range(groups):
            parts = []
            for k in range(slabs.shape[0]):
                flat = slabs.at[k].reshape(slabs.shape[1] * height, LANES)
                parts.append(flat[pl.ds(8 * height * g + r, 8, stride=height), :])
            pieces.append(jnp.concatenate(parts, axis=1))
    return jnp.concatenate(pieces, axis=0)


def field_block(slabs, field):
    return jnp.concatenate([slabs[k, field] for k in range(slabs.shape[0])], axis=1)


def load_rows(slabs, target, first, natural_row, groups, matrix):
    rows = [natural_row(k) for k in range(8)]
    x = permute_columns(rows_of_fields(slabs, rows, groups), matrix)
    width = x.shape[1]
    target[pl.ds(first, 8)] = x.reshape(8, groups, 8, width)


def emit(final, first, count, groups, matrix, swap, outs, out_first):
    outer_left, outer_right, sub, send_right_pair, send_left_pair = outs
    width = final.shape[-1]
    x = final[pl.ds(first, 8)].reshape(8 * count, width)
    x = permute_columns(x, matrix).reshape(8, count, width)
    b = blocks_of(x)
    at = pl.ds(out_first, 8)
    outer_left[at] = b[0]
    outer_right[at] = b[3]
    sub[at] = jnp.concatenate(b[1:3], axis=2)
    send_right_pair[at] = jnp.where(swap, b[1], b[2])
    send_left_pair[at] = jnp.where(swap, b[2], b[1])


def rows_as_columns(ref, first, count):
    return jnp.concatenate([ref[first + k] for k in range(count)], axis=1)


def prepare_kernel(quad, vec, log_kappa, send_a, send_b, sems):
    odd = lax.rem(lax.axis_index(quad), 2)
    count, height, _ = vec.shape
    far = height - SWEEPS
    row_a = pl.multiple_of((1 - odd) * far, 8)
    row_b = pl.multiple_of(odd * far, 8)
    copies = []
    for k, (row, dst) in enumerate(((row_b, send_b), (row_a, send_a))):
        copies.append(
            pltpu.make_async_copy(
                vec.at[:, pl.ds(row, SWEEPS), :], dst.at[pl.ds(0, count)], sems.at[2 * k]
            )
        )
        copies.append(
            pltpu.make_async_copy(
                log_kappa.at[pl.ds(row, SWEEPS), :], dst.at[count], sems.at[2 * k + 1]
            )
        )
    for c in copies:
        c.start()
    for c in copies:
        c.wait()


def inner_kernel(
    quad, patch, vec, halo_a, log_kappa,
    outer_left, outer_right, sub, send_right, send_left, rim, gram,
    even, odd_buf, weights, vec_slabs, halo_slabs, logs, natural, sems,
):
    odd = lax.rem(lax.axis_index(quad), 2)
    swap = lax.rem(lax.axis_index(patch), 2) == 1
    total, groups = even.shape[:2]
    height = total - SWEEPS
    count = 8 * groups
    width = even.shape[-1]

    def own_block(b):
        return jnp.where(odd == 1, height // 8 - 1 - b, b)

    blocks = height // 8
    halo_copies = fetch_columns(halo_a, halo_slabs, sems.at[blocks])
    block_copies = [
        fetch_columns(vec, vec_slabs, sems.at[b], pl.multiple_of(own_block(b) * 8, 8))
        for b in range(blocks)
    ]
    matrix = permutation(width, False)
    logs[...] = jnp.zeros(logs.shape, f32)
    logs[pl.ds(16, height)] = permute_columns(log_kappa[...], matrix)
    wait_all(halo_copies)
    below = pl.multiple_of(8 + (1 - odd) * (height + 8), 8)
    logs[pl.ds(below, 8)] = permute_columns(field_block(halo_slabs, count), matrix)
    values = face_weights(logs[...], 1.0)
    for i in range(4):
        natural[i] = values[i]

    def natural_row(k):
        return jnp.where(odd == 1, height + 7 - k, k + 8)

    def own_row(k):
        return jnp.where(odd == 1, height - 1 - k, k)

    load_rows(
        halo_slabs, even, height, lambda k: jnp.where(odd == 1, 7 - k, k), groups, matrix
    )
    for block in range(blocks):
        wait_all(block_copies[block])
        load_rows(
            vec_slabs, even, 8 * block, lambda k: own_row(8 * block + k), groups, matrix
        )
    spread_weights(natural, weights, total - 2, lambda k: natural_row(k + 1), odd)

    bufs = (even, odd_buf)
    for level in range(1, SWEEPS + 1):
        now, new = bufs[(level - 1) % 2], bufs[level % 2]
        rim[level - 1, 0] = now[level - 1]
        rim[level - 1, 1] = now[level]
        sweep(level, now, new, weights, level, total - level, 1)

    final = bufs[SWEEPS % 2]
    back = permutation(width, True)
    outs = (outer_left, outer_right, sub, send_right, send_left)

    def finish(block, carry):
        row = pl.multiple_of(8 * block, 8)
        emit(final, row + 8, count, groups, back, swap, outs, row)
        return carry

    lax.fori_loop(0, (height - SWEEPS) // 8, finish, 0, unroll=True)
    x = rows_as_columns(sub, 0, height - SWEEPS)
    gram[...] = gram_product(x, x)


def edge_kernel(
    quad, patch, halo_b, log_kappa, rim, gram_inner, send_right_in, send_left_in,
    outer_left, outer_right, sub, send_right, send_left,
    even, odd_buf, weights, halo_slabs, logs, natural, sems,
):
    index = lax.axis_index(quad)
    odd = lax.rem(index, 2)
    swap = lax.rem(lax.axis_index(patch), 2) == 1
    size = lax.axis_size(quad)
    alive = jnp.where(jnp.logical_or(index == 0, index == size - 1), 0.0, 1.0)
    groups = even.shape[1]
    width = even.shape[-1]
    height = log_kappa.shape[0]
    count = 8 * groups
    halo_copies = fetch_columns(halo_b, halo_slabs, sems)
    matrix = permutation(width, False)
    logs[...] = jnp.zeros(logs.shape, f32)
    own_at = pl.multiple_of(odd * (height - 16), 8)
    place = pl.multiple_of(16 - 8 * odd, 8)
    logs[pl.ds(place, 16)] = permute_columns(log_kappa[pl.ds(own_at, 16), :], matrix)
    wait_all(halo_copies)
    halo_at = pl.multiple_of(8 + 16 * odd, 8)
    logs[pl.ds(halo_at, 8)] = permute_columns(field_block(halo_slabs, count), matrix)
    position = lax.broadcasted_iota(jnp.int32, (24, width), 0)
    outside = jnp.logical_and(position >= 16 * odd, position < 8 + 16 * odd)
    values = face_weights(logs[...], jnp.where(outside, alive, 1.0))
    for i in range(4):
        natural[i] = values[i]

    load_rows(
        halo_slabs, even, 0, lambda k: jnp.where(odd == 1, 7 - k, k), groups, matrix
    )
    spread_weights(
        natural, weights, 15, lambda k: jnp.where(odd == 1, 22 - k, k + 1), odd
    )

    bufs = (even, odd_buf)
    for level in range(1, SWEEPS + 1):
        now, new = bufs[(level - 1) % 2], bufs[level % 2]
        now[level + SWEEPS - 1] = rim[level - 1, 0]
        now[level + SWEEPS] = rim[level - 1, 1]
        sweep(level, now, new, weights, level, level + SWEEPS, 1)

    final = bufs[SWEEPS % 2]
    back = permutation(width, True)
    emit(final, SWEEPS, count, groups, back, swap, (outer_left, outer_right, sub, send_right, send_left), 0)
    x = rows_as_columns(sub, 0, SWEEPS)
    total = gram_inner[...] + gram_product(x, x)
    inner = height - SWEEPS
    for out, source in ((send_right, send_right_in), (send_left, send_left_in)):
        out[pl.ds(SWEEPS, inner)] = source[...]
        out[height] = jnp.zeros((count, LANES), f32)
        out[height, :, :count] = total


def product_kernel(
    patch, left_in, left_edge, right_in, right_edge, from_right_pair, from_left_pair, sent, out
):
    swap = lax.rem(lax.axis_index(patch), 2) == 1
    count = out.shape[0]
    inner = left_in.shape[0]
    height = inner + SWEEPS

    def products(mine, mine_edge, theirs):
        x = jnp.concatenate(
            [rows_as_columns(mine_edge, 0, SWEEPS), rows_as_columns(mine, 0, inner)], axis=1
        )
        return gram_product(x, rows_as_columns(theirs, 0, height))

    out[...] = jnp.zeros(out.shape, f32)

    def write(from_left, from_right):
        mats = (
            sent[height, :, :count],
            from_left[height, :, :count],
            from_right[height, :, :count],
            products(left_in, left_edge, from_left),
            products(right_in, right_edge, from_right),
        )
        for k, mat in enumerate(mats):
            out[:, k * count : (k + 1) * count] = mat

    @pl.when(swap)
    def _():
        write(from_right_pair, from_left_pair)

    @pl.when(jnp.logical_not(swap))
    def _():
        write(from_left_pair, from_right_pair)


def inverse_factors(mats, eye, lanes):
    count = eye.shape[0]
    sub = lax.broadcasted_iota(jnp.int32, (count, lanes), 0)
    lane = lax.broadcasted_iota(jnp.int32, (count, lanes), 1)
    zeros = jnp.zeros((count, lanes - 2 * count), f32)
    works = [jnp.concatenate([mat, eye, zeros], axis=1) for mat in mats]
    for j in range(0, count, 2):
        for m, work in enumerate(works):
            first = jnp.broadcast_to(work[:, j : j + 1], (count, lanes))
            second = jnp.broadcast_to(work[:, j + 1 : j + 2], (count, lanes))
            a, b, c = first[j : j + 1], second[j : j + 1], second[j + 1 : j + 2]
            row_j = work[j : j + 1]
            over_a = 1.0 / a
            part = b * over_a
            row_next = work[j + 1 : j + 2] - part * row_j
            over_c = 1.0 / (c - part * b)
            change = first * (row_j * over_a) + (second - first * part) * (row_next * over_c)
            work = jnp.where(sub > j + 1, work - change, work)
            works[m] = jnp.where(sub == j + 1, row_next, work)
    out = []
    for work in works:
        diagonal = jnp.sum(jnp.where(sub == lane, work, 0.0), axis=1, keepdims=True)
        out.append((work / jnp.sqrt(diagonal))[:, count : 2 * count])
    return out


def final_kernel(quad, patch, gathered, sub_in, sub_edge, basis, coupling, slabs, sems):
    odd = lax.rem(lax.axis_index(quad), 2)
    place = lax.axis_index(patch)
    last = lax.axis_size(patch) - 1
    inner, count, sub_width = sub_in.shape
    height = inner + SWEEPS
    total = (gathered[0] + gathered[1]) + (gathered[2] + gathered[3])
    lanes = total.shape[1]
    mats = [total[:, k * count : (k + 1) * count] for k in range(5)]
    eye = (
        lax.broadcasted_iota(jnp.int32, (count, count), 0)
        == lax.broadcasted_iota(jnp.int32, (count, count), 1)
    ).astype(f32)
    grams = [
        mats[0],
        jnp.where(place == 0, eye, mats[1]),
        jnp.where(place == last, eye, mats[2]),
    ]
    own, left, right = inverse_factors(grams, eye, lanes)

    high = own.astype(bf16).astype(f32)
    low = own - high
    factor = jnp.concatenate([high, high, low, low], axis=1).astype(bf16)
    stride = slabs.shape[2]
    copies = []
    for block in range(height // 8):
        natural = jnp.where(odd == 1, height // 8 - 1 - block, block)
        for k in range(8):
            row = 8 * block + k
            x = sub_edge[row] if row < SWEEPS else sub_in[row - SWEEPS]
            r = jnp.where(odd == 1, height - 1 - row, row)
            x_high = x.astype(bf16).astype(f32)
            x_low = x - x_high
            value = dot_nn(
                factor, jnp.concatenate([x_high, x_low, x_high, x_low], axis=0).astype(bf16)
            )
            for c in range(sub_width // LANES):
                flat = slabs.at[c].reshape(count * stride, LANES)
                for g in range(count // 8):
                    flat[pl.ds(8 * stride * g + r, 8, stride=stride), :] = value[
                        8 * g : 8 * g + 8, LANES * c : LANES * (c + 1)
                    ]
        at = pl.ds(pl.multiple_of(8 * natural, 8), 8)
        for c in range(sub_width // LANES):
            copy = pltpu.make_async_copy(
                slabs.at[c, :, at],
                basis.at[:, at, pl.ds(LANES * c, LANES)],
                sems.at[block, c],
            )
            copy.start()
            copies.append(copy)
    coupling[0] = dot_nt(dot_nn(own, mats[3], highest), left, highest)
    coupling[1] = dot_nt(dot_nn(own, mats[4], highest), right, highest)
    wait_all(copies)


def call_prepare(vec, log_own):
    count, _, width = vec.shape
    return pl.pallas_call(
        functools.partial(prepare_kernel, "quad"),
        out_shape=(shape(count + 1, SWEEPS, width),) * 2,
        in_specs=[pl.BlockSpec(memory_space=pltpu.HBM)] * 2,
        out_specs=(VMEM, VMEM),
        scratch_shapes=[pltpu.SemaphoreType.DMA((4,))],
        compiler_params=PARAMS,
        name="prepare",
    )(
        pltpu.with_memory_space_constraint(vec, pltpu.HBM),
        pltpu.with_memory_space_constraint(log_own, pltpu.HBM),
    )


def call_inner(vec, halo_a, log_own):
    count, height, width = vec.shape
    band, groups, inner, total = width // 4, count // 8, height - SWEEPS, height + SWEEPS
    cost = 12 * count * width * SWEEPS * height
    return pl.pallas_call(
        functools.partial(inner_kernel, "quad", "patch"),
        out_shape=(
            shape(inner, count, band),
            shape(inner, count, band),
            shape(inner, count, 2 * band),
            shape(inner, count, band),
            shape(inner, count, band),
            shape(SWEEPS, 2, groups, 8, width),
            shape(count, count),
        ),
        scratch_shapes=[
            pltpu.VMEM((total, groups, 8, width), f32),
            pltpu.VMEM((total, groups, 8, width), f32),
            pltpu.VMEM((total - 2, 4, 8, width), f32),
            pltpu.VMEM((width // LANES, count, height + PAD, LANES), f32),
            pltpu.VMEM((width // LANES, count + 1, SWEEPS, LANES), f32),
            pltpu.VMEM((height + 32, width), f32),
            pltpu.VMEM((4, height + 16, width), f32),
            pltpu.SemaphoreType.DMA((height // 8 + 1, width // LANES)),
        ],
        in_specs=[ANY, ANY, VMEM],
        compiler_params=PARAMS,
        cost_estimate=pl.CostEstimate(flops=cost, bytes_accessed=5 << 20, transcendentals=0),
        name="inner",
    )(vec, halo_a, log_own)


def call_edge(halo_b, log_own, rim, gram_inner, send_right, send_left):
    height, width = log_own.shape
    inner, count, band = send_right.shape
    groups = count // 8
    return pl.pallas_call(
        functools.partial(edge_kernel, "quad", "patch"),
        out_shape=(
            shape(SWEEPS, count, band),
            shape(SWEEPS, count, band),
            shape(SWEEPS, count, 2 * band),
            shape(height + 1, count, band),
            shape(height + 1, count, band),
        ),
        scratch_shapes=[
            pltpu.VMEM((2 * SWEEPS + 1, groups, 8, width), f32),
            pltpu.VMEM((2 * SWEEPS + 1, groups, 8, width), f32),
            pltpu.VMEM((2 * SWEEPS - 1, 4, 8, width), f32),
            pltpu.VMEM((width // LANES, count + 1, SWEEPS, LANES), f32),
            pltpu.VMEM((40, width), f32),
            pltpu.VMEM((4, 24, width), f32),
            pltpu.SemaphoreType.DMA((width // LANES,)),
        ],
        in_specs=[ANY] + [VMEM] * 5,
        compiler_params=PARAMS,
        name="edge",
    )(halo_b, log_own, rim, gram_inner, send_right, send_left)


def call_product(left_in, left_edge, right_in, right_edge, from_right_pair, from_left_pair, sent):
    count = left_in.shape[1]
    return pl.pallas_call(
        functools.partial(product_kernel, "patch"),
        out_shape=shape(count, LANES),
        compiler_params=PARAMS,
        name="product",
    )(left_in, left_edge, right_in, right_edge, from_right_pair, from_left_pair, sent)


def call_final(gathered, sub_in, sub_edge):
    inner, count, sub_width = sub_in.shape
    height = inner + SWEEPS
    return pl.pallas_call(
        functools.partial(final_kernel, "quad", "patch"),
        out_shape=(shape(count, height, sub_width), shape(2, count, count)),
        out_specs=(ANY, VMEM),
        scratch_shapes=[
            pltpu.VMEM((sub_width // LANES, count, height + PAD, LANES), f32),
            pltpu.SemaphoreType.DMA((height // 8, sub_width // LANES)),
        ],
        compiler_params=PARAMS,
        name="final",
    )(gathered, sub_in, sub_edge)


def pairs(size, first):
    swaps = [(i, i + 1) for i in range(first, size - 1, 2)]
    return swaps + [(j, i) for i, j in swaps]


def on_device(vectors, log_kappa):
    vec, log_own = vectors[0], log_kappa[0]
    patch_size, quad_size = lax.axis_size("patch"), lax.axis_size("quad")
    send_a, send_b = call_prepare(vec, log_own)
    halo_a = lax.ppermute(send_a, "quad", pairs(quad_size, 0))
    halo_b = lax.ppermute(send_b, "quad", pairs(quad_size, 1))
    left_in, right_in, sub_in, send_1_in, send_2_in, rim, gram_in = call_inner(
        vec, halo_a, log_own
    )
    left_edge, right_edge, sub_edge, send_1, send_2 = call_edge(
        halo_b, log_own, rim, gram_in, send_1_in, send_2_in
    )
    from_2 = lax.ppermute(send_2, "patch", pairs(patch_size, 1))
    from_1 = lax.ppermute(send_1, "patch", pairs(patch_size, 0))
    packed = call_product(left_in, left_edge, right_in, right_edge, from_1, from_2, send_1)
    gathered = lax.all_gather(packed, "quad")
    basis, coupling = call_final(gathered, sub_in, sub_edge)
    return basis[None], coupling[None]


def solution(mesh):
    placed = (P("patch", None, "quad", None), P("patch", "quad", None))
    return jax.shard_map(
        on_device,
        mesh=mesh,
        in_specs=placed,
        out_specs=(P("patch", None, "quad", None), P("patch", None, None, None)),
        check_vma=False,
    )
```

```python
import functools

import jax
import jax.numpy as jnp
from jax import lax
from jax.experimental import pallas as pl
from jax.experimental.pallas import tpu as pltpu
from jax.sharding import PartitionSpec as P

SWEEPS = 8

mass_term = 0.1
lower_bound = 0.05
upper_bound = 2.0
mid_value = 0.5 * (upper_bound + lower_bound)
half_width = 0.5 * (upper_bound - lower_bound)
highest = lax.Precision.HIGHEST
f32 = jnp.float32
bf16 = jnp.bfloat16

CENTRE = 2.0 * (mid_value - 1.0) / half_width
FACE = 2.0 / half_width

BLOCKS = 4
LANES = 128
CHUNK = 8
PAD = 8

PARAMS = pltpu.CompilerParams(vmem_limit_bytes=40 * 1024 * 1024)
ANY = pl.BlockSpec(memory_space=pl.ANY)
VMEM = pl.BlockSpec(memory_space=pltpu.VMEM)


def shape(*dims):
    return jax.ShapeDtypeStruct(dims, f32)


def dot_nt(a, b, precision=None):
    return lax.dot_general(
        a, b, (((1,), (1,)), ((), ())), precision=precision, preferred_element_type=f32
    )


def dot_nn(a, b, precision=None):
    return lax.dot_general(
        a, b, (((1,), (0,)), ((), ())), precision=precision, preferred_element_type=f32
    )


def two_parts(x):
    high = x.astype(bf16).astype(f32)
    return jnp.concatenate([high, x - high], axis=0).astype(bf16)


def gram_product(x, y):
    n, m = x.shape[0], y.shape[0]
    full = dot_nt(two_parts(x), two_parts(y))
    return (full[:n, :m] + full[n:, :m]) + (full[:n, m:] + full[n:, m:])


def permutation(width, inverse):
    row = lax.broadcasted_iota(jnp.int32, (width, width), 0)
    col = lax.broadcasted_iota(jnp.int32, (width, width), 1)
    if inverse:
        row, col = col, row
    target = (row % BLOCKS) * LANES + row // BLOCKS
    return jnp.where(target == col, 1.0, 0.0).astype(bf16)


def permute_columns(x, matrix):
    n = x.shape[0]
    out = dot_nn(two_parts(x), matrix)
    return out[:n] + out[n:]


def blocks_of(value):
    return [value[..., k * LANES : (k + 1) * LANES] for k in range(BLOCKS)]


def left_neighbour(x):
    b = blocks_of(x)
    axis = x.ndim - 1
    return jnp.concatenate([pltpu.roll(b[-1], 1, axis)] + b[:-1], axis=axis)


def right_neighbour(x):
    b = blocks_of(x)
    axis = x.ndim - 1
    return jnp.concatenate(b[1:] + [pltpu.roll(b[0], LANES - 1, axis)], axis=axis)


def face_weights(logs, alive):
    n, width = logs.shape
    kappa = jnp.exp(logs)
    rows = lax.slice_in_dim
    centre = rows(kappa, 8, n - 8, axis=0)
    before = rows(kappa, 7, n - 9, axis=0)
    after = rows(kappa, 9, n - 7, axis=0)
    lane = lax.broadcasted_iota(jnp.int32, centre.shape, 1)
    is_first, is_last = lane == 0, lane == width - 1
    left = jnp.where(is_first, 1.0, left_neighbour(centre))
    right = jnp.where(is_last, 1.0, right_neighbour(centre))
    upper_face = 0.5 * (centre + before)
    lower_face = 0.5 * (centre + after)
    left_face = 0.5 * (centre + left)
    right_face = 0.5 * (centre + right)
    diagonal = upper_face + lower_face + left_face + right_face + mass_term * centre
    scale = FACE * alive / diagonal
    return (
        upper_face * scale,
        lower_face * scale,
        jnp.where(is_first, 0.0, left_face * scale),
        jnp.where(is_last, 0.0, right_face * scale),
    )


def spread_weights(natural, weights, count, natural_row, odd):
    width = weights.shape[-1]

    def body(k, carry):
        r = natural_row(k)
        for i in range(4):
            source = jnp.where(odd == 1, 1 - i, i) if i < 2 else i
            weights[k, i] = jnp.broadcast_to(natural[source, pl.ds(r, 1), :], (8, width))
        return carry

    lax.fori_loop(0, count, body, 0, unroll=2)


def apply_row(now, row, weights, wrow):
    centre = now[row]
    return (
        CENTRE * centre
        + weights[wrow, 0] * now[row - 1]
        + weights[wrow, 1] * now[row + 1]
        + (weights[wrow, 2] * left_neighbour(centre) + weights[wrow, 3] * right_neighbour(centre))
    )


def row_loop(first, last, chunk, body):
    whole = (last - first) // chunk

    def step(k, carry):
        for i in range(chunk):
            body(first + chunk * k + i)
        return carry

    if whole > 1:
        lax.fori_loop(0, whole, step, 0)
    elif whole == 1:
        step(0, 0)
    for row in range(first + whole * chunk, last):
        body(row)


def sweep(level, now, new, weights, first, last, wfirst):
    def body(row):
        value = apply_row(now, row, weights, row - wfirst)
        if level == 1:
            new[row] = 0.5 * value
        else:
            new[row] = value - new[row]

    row_loop(first, last, CHUNK, body)


def fetch_columns(source, slabs, sems, rows=0):
    copies = []
    for k in range(slabs.shape[0]):
        copy = pltpu.make_async_copy(
            source.at[:, pl.ds(rows, 8), pl.ds(LANES * k, LANES)],
            slabs.at[k, :, pl.ds(rows, 8)],
            sems.at[k],
        )
        copy.start()
        copies.append(copy)
    return copies


def wait_all(copies):
    for copy in copies:
        copy.wait()


def rows_of_fields(slabs, rows, groups):
    height = slabs.shape[2]
    pieces = []
    for r in rows:
        for g in range(groups):
            parts = []
            for k in range(slabs.shape[0]):
                flat = slabs.at[k].reshape(slabs.shape[1] * height, LANES)
                parts.append(flat[pl.ds(8 * height * g + r, 8, stride=height), :])
            pieces.append(jnp.concatenate(parts, axis=1))
    return jnp.concatenate(pieces, axis=0)


def field_block(slabs, field):
    return jnp.concatenate([slabs[k, field] for k in range(slabs.shape[0])], axis=1)


def load_rows(slabs, target, first, natural_row, groups, matrix):
    rows = [natural_row(k) for k in range(8)]
    x = permute_columns(rows_of_fields(slabs, rows, groups), matrix)
    width = x.shape[1]
    target[pl.ds(first, 8)] = x.reshape(8, groups, 8, width)


def emit(final, first, count, groups, matrix, swap, outs, out_first):
    outer_left, outer_right, sub, send_right_pair, send_left_pair = outs
    width = final.shape[-1]
    x = final[pl.ds(first, 8)].reshape(8 * count, width)
    x = permute_columns(x, matrix).reshape(8, count, width)
    b = blocks_of(x)
    at = pl.ds(out_first, 8)
    outer_left[at] = b[0]
    outer_right[at] = b[3]
    sub[at] = jnp.concatenate(b[1:3], axis=2)
    send_right_pair[at] = jnp.where(swap, b[1], b[2])
    send_left_pair[at] = jnp.where(swap, b[2], b[1])


def rows_as_columns(ref, first, count):
    return jnp.concatenate([ref[first + k] for k in range(count)], axis=1)


def prepare_kernel(quad, vec, log_kappa, send_a, send_b, sems):
    odd = lax.rem(lax.axis_index(quad), 2)
    count, height, _ = vec.shape
    far = height - SWEEPS
    row_a = pl.multiple_of((1 - odd) * far, 8)
    row_b = pl.multiple_of(odd * far, 8)
    copies = []
    for k, (row, dst) in enumerate(((row_b, send_b), (row_a, send_a))):
        copies.append(
            pltpu.make_async_copy(
                vec.at[:, pl.ds(row, SWEEPS), :], dst.at[pl.ds(0, count)], sems.at[2 * k]
            )
        )
        copies.append(
            pltpu.make_async_copy(
                log_kappa.at[pl.ds(row, SWEEPS), :], dst.at[count], sems.at[2 * k + 1]
            )
        )
    for c in copies:
        c.start()
    for c in copies:
        c.wait()


def inner_kernel(
    quad, patch, vec, halo_a, log_kappa,
    outer_left, outer_right, sub, send_right, send_left, rim, gram,
    even, odd_buf, weights, vec_slabs, halo_slabs, logs, natural, sems,
):
    odd = lax.rem(lax.axis_index(quad), 2)
    swap = lax.rem(lax.axis_index(patch), 2) == 1
    total, groups = even.shape[:2]
    height = total - SWEEPS
    count = 8 * groups
    width = even.shape[-1]

    def own_block(b):
        return jnp.where(odd == 1, height // 8 - 1 - b, b)

    blocks = height // 8
    halo_copies = fetch_columns(halo_a, halo_slabs, sems.at[blocks])
    block_copies = [
        fetch_columns(vec, vec_slabs, sems.at[b], pl.multiple_of(own_block(b) * 8, 8))
        for b in range(blocks)
    ]
    matrix = permutation(width, False)
    logs[...] = jnp.zeros(logs.shape, f32)
    logs[pl.ds(16, height)] = permute_columns(log_kappa[...], matrix)
    wait_all(halo_copies)
    below = pl.multiple_of(8 + (1 - odd) * (height + 8), 8)
    logs[pl.ds(below, 8)] = permute_columns(field_block(halo_slabs, count), matrix)
    values = face_weights(logs[...], 1.0)
    for i in range(4):
        natural[i] = values[i]

    def natural_row(k):
        return jnp.where(odd == 1, height + 7 - k, k + 8)

    def own_row(k):
        return jnp.where(odd == 1, height - 1 - k, k)

    load_rows(
        halo_slabs, even, height, lambda k: jnp.where(odd == 1, 7 - k, k), groups, matrix
    )
    for block in range(blocks):
        wait_all(block_copies[block])
        load_rows(
            vec_slabs, even, 8 * block, lambda k: own_row(8 * block + k), groups, matrix
        )
    spread_weights(natural, weights, total - 2, lambda k: natural_row(k + 1), odd)

    bufs = (even, odd_buf)
    for level in range(1, SWEEPS + 1):
        now, new = bufs[(level - 1) % 2], bufs[level % 2]
        rim[level - 1, 0] = now[level - 1]
        rim[level - 1, 1] = now[level]
        sweep(level, now, new, weights, level, total - level, 1)

    final = bufs[SWEEPS % 2]
    back = permutation(width, True)
    outs = (outer_left, outer_right, sub, send_right, send_left)

    def finish(block, carry):
        row = pl.multiple_of(8 * block, 8)
        emit(final, row + 8, count, groups, back, swap, outs, row)
        return carry

    lax.fori_loop(0, (height - SWEEPS) // 8, finish, 0, unroll=True)
    x = rows_as_columns(sub, 0, height - SWEEPS)
    gram[...] = gram_product(x, x)


def edge_kernel(
    quad, patch, halo_b, log_kappa, rim, gram_inner, send_right_in, send_left_in,
    outer_left, outer_right, sub, send_right, send_left,
    even, odd_buf, weights, halo_slabs, logs, natural, sems,
):
    index = lax.axis_index(quad)
    odd = lax.rem(index, 2)
    swap = lax.rem(lax.axis_index(patch), 2) == 1
    size = lax.axis_size(quad)
    alive = jnp.where(jnp.logical_or(index == 0, index == size - 1), 0.0, 1.0)
    groups = even.shape[1]
    width = even.shape[-1]
    height = log_kappa.shape[0]
    count = 8 * groups
    halo_copies = fetch_columns(halo_b, halo_slabs, sems)
    matrix = permutation(width, False)
    logs[...] = jnp.zeros(logs.shape, f32)
    own_at = pl.multiple_of(odd * (height - 16), 8)
    place = pl.multiple_of(16 - 8 * odd, 8)
    logs[pl.ds(place, 16)] = permute_columns(log_kappa[pl.ds(own_at, 16), :], matrix)
    wait_all(halo_copies)
    halo_at = pl.multiple_of(8 + 16 * odd, 8)
    logs[pl.ds(halo_at, 8)] = permute_columns(field_block(halo_slabs, count), matrix)
    position = lax.broadcasted_iota(jnp.int32, (24, width), 0)
    outside = jnp.logical_and(position >= 16 * odd, position < 8 + 16 * odd)
    values = face_weights(logs[...], jnp.where(outside, alive, 1.0))
    for i in range(4):
        natural[i] = values[i]

    load_rows(
        halo_slabs, even, 0, lambda k: jnp.where(odd == 1, 7 - k, k), groups, matrix
    )
    spread_weights(
        natural, weights, 15, lambda k: jnp.where(odd == 1, 22 - k, k + 1), odd
    )

    bufs = (even, odd_buf)
    for level in range(1, SWEEPS + 1):
        now, new = bufs[(level - 1) % 2], bufs[level % 2]
        now[level + SWEEPS - 1] = rim[level - 1, 0]
        now[level + SWEEPS] = rim[level - 1, 1]
        sweep(level, now, new, weights, level, level + SWEEPS, 1)

    final = bufs[SWEEPS % 2]
    back = permutation(width, True)
    emit(final, SWEEPS, count, groups, back, swap, (outer_left, outer_right, sub, send_right, send_left), 0)
    x = rows_as_columns(sub, 0, SWEEPS)
    total = gram_inner[...] + gram_product(x, x)
    inner = height - SWEEPS
    for out, source in ((send_right, send_right_in), (send_left, send_left_in)):
        out[pl.ds(SWEEPS, inner)] = source[...]
        out[height] = jnp.zeros((count, LANES), f32)
        out[height, :, :count] = total


def product_kernel(
    patch, left_in, left_edge, right_in, right_edge, from_right_pair, from_left_pair, sent, out
):
    swap = lax.rem(lax.axis_index(patch), 2) == 1
    count = out.shape[0]
    inner = left_in.shape[0]
    height = inner + SWEEPS

    def products(mine, mine_edge, theirs):
        x = jnp.concatenate(
            [rows_as_columns(mine_edge, 0, SWEEPS), rows_as_columns(mine, 0, inner)], axis=1
        )
        return gram_product(x, rows_as_columns(theirs, 0, height))

    out[...] = jnp.zeros(out.shape, f32)

    def write(from_left, from_right):
        mats = (
            sent[height, :, :count],
            from_left[height, :, :count],
            from_right[height, :, :count],
            products(left_in, left_edge, from_left),
            products(right_in, right_edge, from_right),
        )
        for k, mat in enumerate(mats):
            out[:, k * count : (k + 1) * count] = mat

    @pl.when(swap)
    def _():
        write(from_right_pair, from_left_pair)

    @pl.when(jnp.logical_not(swap))
    def _():
        write(from_left_pair, from_right_pair)


def inverse_factors(mats, eye, lanes):
    count = eye.shape[0]
    sub = lax.broadcasted_iota(jnp.int32, (count, lanes), 0)
    lane = lax.broadcasted_iota(jnp.int32, (count, lanes), 1)
    zeros = jnp.zeros((count, lanes - 2 * count), f32)
    works = [jnp.concatenate([mat, eye, zeros], axis=1) for mat in mats]
    for j in range(0, count, 2):
        for m, work in enumerate(works):
            first = jnp.broadcast_to(work[:, j : j + 1], (count, lanes))
            second = jnp.broadcast_to(work[:, j + 1 : j + 2], (count, lanes))
            a, b, c = first[j : j + 1], second[j : j + 1], second[j + 1 : j + 2]
            row_j = work[j : j + 1]
            over_a = 1.0 / a
            part = b * over_a
            row_next = work[j + 1 : j + 2] - part * row_j
            over_c = 1.0 / (c - part * b)
            change = first * (row_j * over_a) + (second - first * part) * (row_next * over_c)
            work = jnp.where(sub > j + 1, work - change, work)
            works[m] = jnp.where(sub == j + 1, row_next, work)
    out = []
    for work in works:
        diagonal = jnp.sum(jnp.where(sub == lane, work, 0.0), axis=1, keepdims=True)
        out.append((work / jnp.sqrt(diagonal))[:, count : 2 * count])
    return out


def final_kernel(
    quad, patch, outer_total, passed, sub_in, sub_edge, basis, coupling, slabs, sems
):
    odd = lax.rem(lax.axis_index(quad), 2)
    place = lax.axis_index(patch)
    last = lax.axis_size(patch) - 1
    inner, count, sub_width = sub_in.shape
    height = inner + SWEEPS
    index = lax.axis_index(quad)
    outer = jnp.logical_or(index == 0, index == lax.axis_size(quad) - 1)
    total = jnp.where(outer, outer_total[...], passed[...])
    lanes = total.shape[1]
    mats = [total[:, k * count : (k + 1) * count] for k in range(5)]
    eye = (
        lax.broadcasted_iota(jnp.int32, (count, count), 0)
        == lax.broadcasted_iota(jnp.int32, (count, count), 1)
    ).astype(f32)
    grams = [
        mats[0],
        jnp.where(place == 0, eye, mats[1]),
        jnp.where(place == last, eye, mats[2]),
    ]
    own, left, right = inverse_factors(grams, eye, lanes)

    high = own.astype(bf16).astype(f32)
    low = own - high
    factor = jnp.concatenate([high, high, low, low], axis=1).astype(bf16)
    stride = slabs.shape[2]
    copies = []
    for block in range(height // 8):
        natural = jnp.where(odd == 1, height // 8 - 1 - block, block)
        for k in range(8):
            row = 8 * block + k
            x = sub_edge[row] if row < SWEEPS else sub_in[row - SWEEPS]
            r = jnp.where(odd == 1, height - 1 - row, row)
            x_high = x.astype(bf16).astype(f32)
            x_low = x - x_high
            value = dot_nn(
                factor, jnp.concatenate([x_high, x_low, x_high, x_low], axis=0).astype(bf16)
            )
            for c in range(sub_width // LANES):
                flat = slabs.at[c].reshape(count * stride, LANES)
                for g in range(count // 8):
                    flat[pl.ds(8 * stride * g + r, 8, stride=stride), :] = value[
                        8 * g : 8 * g + 8, LANES * c : LANES * (c + 1)
                    ]
        at = pl.ds(pl.multiple_of(8 * natural, 8), 8)
        for c in range(sub_width // LANES):
            copy = pltpu.make_async_copy(
                slabs.at[c, :, at],
                basis.at[:, at, pl.ds(LANES * c, LANES)],
                sems.at[block, c],
            )
            copy.start()
            copies.append(copy)
    coupling[0] = dot_nt(dot_nn(own, mats[3], highest), left, highest)
    coupling[1] = dot_nt(dot_nn(own, mats[4], highest), right, highest)
    wait_all(copies)


def call_prepare(vec, log_own):
    count, _, width = vec.shape
    return pl.pallas_call(
        functools.partial(prepare_kernel, "quad"),
        out_shape=(shape(count + 1, SWEEPS, width),) * 2,
        in_specs=[pl.BlockSpec(memory_space=pltpu.HBM)] * 2,
        out_specs=(VMEM, VMEM),
        scratch_shapes=[pltpu.SemaphoreType.DMA((4,))],
        compiler_params=PARAMS,
        name="prepare",
    )(
        pltpu.with_memory_space_constraint(vec, pltpu.HBM),
        pltpu.with_memory_space_constraint(log_own, pltpu.HBM),
    )


def call_inner(vec, halo_a, log_own):
    count, height, width = vec.shape
    band, groups, inner, total = width // 4, count // 8, height - SWEEPS, height + SWEEPS
    cost = 12 * count * width * SWEEPS * height
    return pl.pallas_call(
        functools.partial(inner_kernel, "quad", "patch"),
        out_shape=(
            shape(inner, count, band),
            shape(inner, count, band),
            shape(inner, count, 2 * band),
            shape(inner, count, band),
            shape(inner, count, band),
            shape(SWEEPS, 2, groups, 8, width),
            shape(count, count),
        ),
        scratch_shapes=[
            pltpu.VMEM((total, groups, 8, width), f32),
            pltpu.VMEM((total, groups, 8, width), f32),
            pltpu.VMEM((total - 2, 4, 8, width), f32),
            pltpu.VMEM((width // LANES, count, height + PAD, LANES), f32),
            pltpu.VMEM((width // LANES, count + 1, SWEEPS, LANES), f32),
            pltpu.VMEM((height + 32, width), f32),
            pltpu.VMEM((4, height + 16, width), f32),
            pltpu.SemaphoreType.DMA((height // 8 + 1, width // LANES)),
        ],
        in_specs=[ANY, ANY, VMEM],
        compiler_params=PARAMS,
        cost_estimate=pl.CostEstimate(flops=cost, bytes_accessed=5 << 20, transcendentals=0),
        name="inner",
    )(vec, halo_a, log_own)


def call_edge(halo_b, log_own, rim, gram_inner, send_right, send_left):
    height, width = log_own.shape
    inner, count, band = send_right.shape
    groups = count // 8
    return pl.pallas_call(
        functools.partial(edge_kernel, "quad", "patch"),
        out_shape=(
            shape(SWEEPS, count, band),
            shape(SWEEPS, count, band),
            shape(SWEEPS, count, 2 * band),
            shape(height + 1, count, band),
            shape(height + 1, count, band),
        ),
        scratch_shapes=[
            pltpu.VMEM((2 * SWEEPS + 1, groups, 8, width), f32),
            pltpu.VMEM((2 * SWEEPS + 1, groups, 8, width), f32),
            pltpu.VMEM((2 * SWEEPS - 1, 4, 8, width), f32),
            pltpu.VMEM((width // LANES, count + 1, SWEEPS, LANES), f32),
            pltpu.VMEM((40, width), f32),
            pltpu.VMEM((4, 24, width), f32),
            pltpu.SemaphoreType.DMA((width // LANES,)),
        ],
        in_specs=[ANY] + [VMEM] * 5,
        compiler_params=PARAMS,
        name="edge",
    )(halo_b, log_own, rim, gram_inner, send_right, send_left)


def call_product(left_in, left_edge, right_in, right_edge, from_right_pair, from_left_pair, sent):
    count = left_in.shape[1]
    return pl.pallas_call(
        functools.partial(product_kernel, "patch"),
        out_shape=shape(count, LANES),
        compiler_params=PARAMS,
        name="product",
    )(left_in, left_edge, right_in, right_edge, from_right_pair, from_left_pair, sent)


def call_final(outer_total, passed, sub_in, sub_edge):
    inner, count, sub_width = sub_in.shape
    height = inner + SWEEPS
    return pl.pallas_call(
        functools.partial(final_kernel, "quad", "patch"),
        out_shape=(shape(count, height, sub_width), shape(2, count, count)),
        out_specs=(ANY, VMEM),
        scratch_shapes=[
            pltpu.VMEM((sub_width // LANES, count, height + PAD, LANES), f32),
            pltpu.SemaphoreType.DMA((height // 8, sub_width // LANES)),
        ],
        compiler_params=PARAMS,
        name="final",
    )(outer_total, passed, sub_in, sub_edge)


def pairs(size, first):
    swaps = [(i, i + 1) for i in range(first, size - 1, 2)]
    return swaps + [(j, i) for i, j in swaps]


def on_device(vectors, log_kappa):
    vec, log_own = vectors[0], log_kappa[0]
    patch_size, quad_size = lax.axis_size("patch"), lax.axis_size("quad")
    send_a, send_b = call_prepare(vec, log_own)
    halo_a = lax.ppermute(send_a, "quad", pairs(quad_size, 0))
    halo_b = lax.ppermute(send_b, "quad", pairs(quad_size, 1))
    left_in, right_in, sub_in, send_1_in, send_2_in, rim, gram_in = call_inner(
        vec, halo_a, log_own
    )
    left_edge, right_edge, sub_edge, send_1, send_2 = call_edge(
        halo_b, log_own, rim, gram_in, send_1_in, send_2_in
    )
    from_2 = lax.ppermute(send_2, "patch", pairs(patch_size, 1))
    from_1 = lax.ppermute(send_1, "patch", pairs(patch_size, 0))
    packed = call_product(left_in, left_edge, right_in, right_edge, from_1, from_2, send_1)
    far = lax.ppermute(packed, "quad", [(1, 3), (2, 0)])
    ends = lax.ppermute(packed, "quad", [(0, 3), (3, 0)])
    near = lax.ppermute(packed, "quad", [(1, 0), (2, 3)])
    outer_total = (packed + near) + (far + ends)
    passed = lax.ppermute(outer_total, "quad", [(0, 1), (3, 2)])
    basis, coupling = call_final(outer_total, passed, sub_in, sub_edge)
    return basis[None], coupling[None]


def solution(mesh):
    placed = (P("patch", None, "quad", None), P("patch", "quad", None))
    return jax.shard_map(
        on_device,
        mesh=mesh,
        in_specs=placed,
        out_specs=(P("patch", None, "quad", None), P("patch", None, None, None)),
        check_vma=False,
    )
```

```python
import functools

import jax
import jax.numpy as jnp
from jax import lax
from jax.experimental import pallas as pl
from jax.experimental.pallas import tpu as pltpu
from jax.sharding import PartitionSpec as P

SWEEPS = 8

mass_term = 0.1
lower_bound = 0.05
upper_bound = 2.0
mid_value = 0.5 * (upper_bound + lower_bound)
half_width = 0.5 * (upper_bound - lower_bound)
highest = lax.Precision.HIGHEST
f32 = jnp.float32
bf16 = jnp.bfloat16

CENTRE = 2.0 * (mid_value - 1.0) / half_width
FACE = 2.0 / half_width

BLOCKS = 4
LANES = 128
CHUNK = 8
PAD = 8

PARAMS = pltpu.CompilerParams(vmem_limit_bytes=40 * 1024 * 1024)
ANY = pl.BlockSpec(memory_space=pl.ANY)
VMEM = pl.BlockSpec(memory_space=pltpu.VMEM)


def shape(*dims):
    return jax.ShapeDtypeStruct(dims, f32)


def dot_nt(a, b, precision=None):
    return lax.dot_general(
        a, b, (((1,), (1,)), ((), ())), precision=precision, preferred_element_type=f32
    )


def dot_nn(a, b, precision=None):
    return lax.dot_general(
        a, b, (((1,), (0,)), ((), ())), precision=precision, preferred_element_type=f32
    )


def two_parts(x):
    high = x.astype(bf16).astype(f32)
    return jnp.concatenate([high, x - high], axis=0).astype(bf16)


def gram_product(x, y):
    n, m = x.shape[0], y.shape[0]
    full = dot_nt(two_parts(x), two_parts(y))
    return (full[:n, :m] + full[n:, :m]) + (full[:n, m:] + full[n:, m:])


def permutation(width, inverse):
    row = lax.broadcasted_iota(jnp.int32, (width, width), 0)
    col = lax.broadcasted_iota(jnp.int32, (width, width), 1)
    if inverse:
        row, col = col, row
    target = (row % BLOCKS) * LANES + row // BLOCKS
    return jnp.where(target == col, 1.0, 0.0).astype(bf16)


def permute_columns(x, matrix):
    n = x.shape[0]
    out = dot_nn(two_parts(x), matrix)
    return out[:n] + out[n:]


def blocks_of(value):
    return [value[..., k * LANES : (k + 1) * LANES] for k in range(BLOCKS)]


def left_neighbour(x):
    b = blocks_of(x)
    axis = x.ndim - 1
    return jnp.concatenate([pltpu.roll(b[-1], 1, axis)] + b[:-1], axis=axis)


def right_neighbour(x):
    b = blocks_of(x)
    axis = x.ndim - 1
    return jnp.concatenate(b[1:] + [pltpu.roll(b[0], LANES - 1, axis)], axis=axis)


def face_weights(logs, alive):
    n, width = logs.shape
    kappa = jnp.exp(logs)
    rows = lax.slice_in_dim
    centre = rows(kappa, 8, n - 8, axis=0)
    before = rows(kappa, 7, n - 9, axis=0)
    after = rows(kappa, 9, n - 7, axis=0)
    lane = lax.broadcasted_iota(jnp.int32, centre.shape, 1)
    is_first, is_last = lane == 0, lane == width - 1
    left = jnp.where(is_first, 1.0, left_neighbour(centre))
    right = jnp.where(is_last, 1.0, right_neighbour(centre))
    upper_face = 0.5 * (centre + before)
    lower_face = 0.5 * (centre + after)
    left_face = 0.5 * (centre + left)
    right_face = 0.5 * (centre + right)
    diagonal = upper_face + lower_face + left_face + right_face + mass_term * centre
    scale = FACE * alive / diagonal
    return (
        upper_face * scale,
        lower_face * scale,
        jnp.where(is_first, 0.0, left_face * scale),
        jnp.where(is_last, 0.0, right_face * scale),
    )


def spread_weights(natural, weights, count, natural_row, odd):
    width = weights.shape[-1]

    def body(k, carry):
        r = natural_row(k)
        for i in range(4):
            source = jnp.where(odd == 1, 1 - i, i) if i < 2 else i
            weights[k, i] = jnp.broadcast_to(natural[source, pl.ds(r, 1), :], (8, width))
        return carry

    lax.fori_loop(0, count, body, 0, unroll=2)


def apply_row(now, row, weights, wrow):
    centre = now[row]
    return (
        CENTRE * centre
        + weights[wrow, 0] * now[row - 1]
        + weights[wrow, 1] * now[row + 1]
        + (weights[wrow, 2] * left_neighbour(centre) + weights[wrow, 3] * right_neighbour(centre))
    )


def row_loop(first, last, chunk, body):
    whole = (last - first) // chunk

    def step(k, carry):
        for i in range(chunk):
            body(first + chunk * k + i)
        return carry

    if whole > 1:
        lax.fori_loop(0, whole, step, 0)
    elif whole == 1:
        step(0, 0)
    for row in range(first + whole * chunk, last):
        body(row)


def sweep(level, now, new, weights, first, last, wfirst):
    def body(row):
        value = apply_row(now, row, weights, row - wfirst)
        if level == 1:
            new[row] = 0.5 * value
        else:
            new[row] = value - new[row]

    row_loop(first, last, CHUNK, body)


def fetch_columns(source, slabs, sems, rows=0):
    copies = []
    for k in range(slabs.shape[0]):
        copy = pltpu.make_async_copy(
            source.at[:, pl.ds(rows, 8), pl.ds(LANES * k, LANES)],
            slabs.at[k, :, pl.ds(rows, 8)],
            sems.at[k],
        )
        copy.start()
        copies.append(copy)
    return copies


def wait_all(copies):
    for copy in copies:
        copy.wait()


def rows_of_fields(slabs, rows, groups):
    height = slabs.shape[2]
    pieces = []
    for r in rows:
        for g in range(groups):
            parts = []
            for k in range(slabs.shape[0]):
                flat = slabs.at[k].reshape(slabs.shape[1] * height, LANES)
                parts.append(flat[pl.ds(8 * height * g + r, 8, stride=height), :])
            pieces.append(jnp.concatenate(parts, axis=1))
    return jnp.concatenate(pieces, axis=0)


def field_block(slabs, field):
    return jnp.concatenate([slabs[k, field] for k in range(slabs.shape[0])], axis=1)


def load_rows(slabs, target, first, natural_row, groups, matrix):
    rows = [natural_row(k) for k in range(8)]
    x = permute_columns(rows_of_fields(slabs, rows, groups), matrix)
    width = x.shape[1]
    target[pl.ds(first, 8)] = x.reshape(8, groups, 8, width)


def emit(final, first, count, groups, matrix, swap, outs, out_first):
    outer, sub, send_right_pair, send_left_pair = outs
    width = final.shape[-1]
    x = final[pl.ds(first, 8)].reshape(8 * count, width)
    x = permute_columns(x, matrix).reshape(8, count, width)
    b = blocks_of(x)
    at = pl.ds(out_first, 8)
    outer[0, at] = b[0]
    outer[1, at] = b[3]
    sub[at] = jnp.concatenate(b[1:3], axis=2)
    send_right_pair[at] = jnp.where(swap, b[1], b[2])
    send_left_pair[at] = jnp.where(swap, b[2], b[1])


def rows_as_columns(ref, first, count):
    return jnp.concatenate([ref[first + k] for k in range(count)], axis=1)


def prepare_kernel(quad, vec, log_kappa, send_a, send_b, sems):
    odd = lax.rem(lax.axis_index(quad), 2)
    count, height, _ = vec.shape
    far = height - SWEEPS
    row_a = pl.multiple_of((1 - odd) * far, 8)
    row_b = pl.multiple_of(odd * far, 8)
    copies = []
    for k, (row, dst) in enumerate(((row_b, send_b), (row_a, send_a))):
        copies.append(
            pltpu.make_async_copy(
                vec.at[:, pl.ds(row, SWEEPS), :], dst.at[pl.ds(0, count)], sems.at[2 * k]
            )
        )
        copies.append(
            pltpu.make_async_copy(
                log_kappa.at[pl.ds(row, SWEEPS), :], dst.at[count], sems.at[2 * k + 1]
            )
        )
    for c in copies:
        c.start()
    for c in copies:
        c.wait()


def inner_kernel(
    quad, patch, vec, halo_a, log_kappa,
    outer, sub, send_right, send_left, rim, gram,
    even, odd_buf, weights, vec_slabs, halo_slabs, logs, natural, sems,
):
    odd = lax.rem(lax.axis_index(quad), 2)
    swap = lax.rem(lax.axis_index(patch), 2) == 1
    total, groups = even.shape[:2]
    height = total - SWEEPS
    count = 8 * groups
    width = even.shape[-1]

    def own_block(b):
        return jnp.where(odd == 1, height // 8 - 1 - b, b)

    blocks = height // 8
    halo_copies = fetch_columns(halo_a, halo_slabs, sems.at[blocks])
    block_copies = [
        fetch_columns(vec, vec_slabs, sems.at[b], pl.multiple_of(own_block(b) * 8, 8))
        for b in range(blocks)
    ]
    matrix = permutation(width, False)
    logs[...] = jnp.zeros(logs.shape, f32)
    logs[pl.ds(16, height)] = permute_columns(log_kappa[...], matrix)
    wait_all(halo_copies)
    below = pl.multiple_of(8 + (1 - odd) * (height + 8), 8)
    logs[pl.ds(below, 8)] = permute_columns(field_block(halo_slabs, count), matrix)
    values = face_weights(logs[...], 1.0)
    for i in range(4):
        natural[i] = values[i]

    def natural_row(k):
        return jnp.where(odd == 1, height + 7 - k, k + 8)

    def own_row(k):
        return jnp.where(odd == 1, height - 1 - k, k)

    load_rows(
        halo_slabs, even, height, lambda k: jnp.where(odd == 1, 7 - k, k), groups, matrix
    )
    for block in range(blocks):
        wait_all(block_copies[block])
        load_rows(
            vec_slabs, even, 8 * block, lambda k: own_row(8 * block + k), groups, matrix
        )
    spread_weights(natural, weights, total - 2, lambda k: natural_row(k + 1), odd)

    bufs = (even, odd_buf)
    for level in range(1, SWEEPS + 1):
        now, new = bufs[(level - 1) % 2], bufs[level % 2]
        rim[level - 1, 0] = now[level - 1]
        rim[level - 1, 1] = now[level]
        sweep(level, now, new, weights, level, total - level, 1)

    final = bufs[SWEEPS % 2]
    back = permutation(width, True)
    outs = (outer, sub, send_right, send_left)

    def finish(block, carry):
        row = pl.multiple_of(8 * block, 8)
        emit(final, row + 8, count, groups, back, swap, outs, row)
        return carry

    lax.fori_loop(0, (height - SWEEPS) // 8, finish, 0, unroll=True)
    x = rows_as_columns(sub, 0, height - SWEEPS)
    gram[...] = gram_product(x, x)


def edge_kernel(
    quad, patch, halo_b, log_kappa, rim, gram_inner, outer_in, send_right_in, send_left_in,
    outer, sub, send_right, send_left,
    even, odd_buf, weights, halo_slabs, logs, natural, sems,
):
    index = lax.axis_index(quad)
    odd = lax.rem(index, 2)
    swap = lax.rem(lax.axis_index(patch), 2) == 1
    size = lax.axis_size(quad)
    alive = jnp.where(jnp.logical_or(index == 0, index == size - 1), 0.0, 1.0)
    groups = even.shape[1]
    width = even.shape[-1]
    height = log_kappa.shape[0]
    count = 8 * groups
    halo_copies = fetch_columns(halo_b, halo_slabs, sems)
    matrix = permutation(width, False)
    logs[...] = jnp.zeros(logs.shape, f32)
    own_at = pl.multiple_of(odd * (height - 16), 8)
    place = pl.multiple_of(16 - 8 * odd, 8)
    logs[pl.ds(place, 16)] = permute_columns(log_kappa[pl.ds(own_at, 16), :], matrix)
    wait_all(halo_copies)
    halo_at = pl.multiple_of(8 + 16 * odd, 8)
    logs[pl.ds(halo_at, 8)] = permute_columns(field_block(halo_slabs, count), matrix)
    position = lax.broadcasted_iota(jnp.int32, (24, width), 0)
    outside = jnp.logical_and(position >= 16 * odd, position < 8 + 16 * odd)
    values = face_weights(logs[...], jnp.where(outside, alive, 1.0))
    for i in range(4):
        natural[i] = values[i]

    load_rows(
        halo_slabs, even, 0, lambda k: jnp.where(odd == 1, 7 - k, k), groups, matrix
    )
    spread_weights(
        natural, weights, 15, lambda k: jnp.where(odd == 1, 22 - k, k + 1), odd
    )

    bufs = (even, odd_buf)
    for level in range(1, SWEEPS + 1):
        now, new = bufs[(level - 1) % 2], bufs[level % 2]
        now[level + SWEEPS - 1] = rim[level - 1, 0]
        now[level + SWEEPS] = rim[level - 1, 1]
        sweep(level, now, new, weights, level, level + SWEEPS, 1)

    final = bufs[SWEEPS % 2]
    back = permutation(width, True)
    emit(final, SWEEPS, count, groups, back, swap, (outer, sub, send_right, send_left), 0)
    x = rows_as_columns(sub, 0, SWEEPS)
    total = gram_inner[...] + gram_product(x, x)
    inner = height - SWEEPS
    for out, source in (
        (send_right, send_right_in),
        (send_left, send_left_in),
        (outer.at[0], outer_in.at[0]),
        (outer.at[1], outer_in.at[1]),
    ):
        out[pl.ds(SWEEPS, inner)] = source[...]
        out[height] = jnp.zeros((count, LANES), f32)
        out[height, :, :count] = total


def at_end(quad):
    index = lax.axis_index(quad)
    return jnp.logical_or(index == 0, index == lax.axis_size(quad) - 1)


def product_kernel(
    quad, patch, left_pair, left_pair_mate, right_pair, right_pair_mate, chip_mate, mine, out
):
    end = at_end(quad)
    swap = lax.rem(lax.axis_index(patch), 2) == 1
    count = out.shape[0]
    height = mine.shape[1] - 1
    out[...] = jnp.zeros(out.shape, f32)

    def both(a, b):
        return jnp.concatenate(
            [rows_as_columns(a, 0, height), rows_as_columns(b, 0, height)], axis=1
        )

    def gram(a, b):
        return a[height, :, :count] + b[height, :, :count]

    def write(left, left_mate, right, right_mate):
        mats = (
            gram(mine.at[0], chip_mate.at[0]),
            gram(left, left_mate),
            gram(right, right_mate),
            gram_product(both(mine.at[0], chip_mate.at[0]), both(left, left_mate)),
            gram_product(both(mine.at[1], chip_mate.at[1]), both(right, right_mate)),
        )
        for k, mat in enumerate(mats):
            out[:, k * count : (k + 1) * count] = mat

    @pl.when(jnp.logical_and(end, swap))
    def _():
        write(right_pair, right_pair_mate, left_pair, left_pair_mate)

    @pl.when(jnp.logical_and(end, jnp.logical_not(swap)))
    def _():
        write(left_pair, left_pair_mate, right_pair, right_pair_mate)


def inverse_factors(mats, eye, lanes):
    count = eye.shape[0]
    sub = lax.broadcasted_iota(jnp.int32, (count, lanes), 0)
    lane = lax.broadcasted_iota(jnp.int32, (count, lanes), 1)
    zeros = jnp.zeros((count, lanes - 2 * count), f32)
    works = [jnp.concatenate([mat, eye, zeros], axis=1) for mat in mats]
    for j in range(0, count, 2):
        for m, work in enumerate(works):
            first = jnp.broadcast_to(work[:, j : j + 1], (count, lanes))
            second = jnp.broadcast_to(work[:, j + 1 : j + 2], (count, lanes))
            a, b, c = first[j : j + 1], second[j : j + 1], second[j + 1 : j + 2]
            row_j = work[j : j + 1]
            over_a = 1.0 / a
            part = b * over_a
            row_next = work[j + 1 : j + 2] - part * row_j
            over_c = 1.0 / (c - part * b)
            change = first * (row_j * over_a) + (second - first * part) * (row_next * over_c)
            work = jnp.where(sub > j + 1, work - change, work)
            works[m] = jnp.where(sub == j + 1, row_next, work)
    out = []
    for work in works:
        diagonal = jnp.sum(jnp.where(sub == lane, work, 0.0), axis=1, keepdims=True)
        out.append((work / jnp.sqrt(diagonal))[:, count : 2 * count])
    return out


def final_kernel(
    quad, patch, near, far, passed, sub_in, sub_edge, basis, coupling, slabs, sems
):
    odd = lax.rem(lax.axis_index(quad), 2)
    place = lax.axis_index(patch)
    last = lax.axis_size(patch) - 1
    inner, count, sub_width = sub_in.shape
    height = inner + SWEEPS
    total = jnp.where(at_end(quad), passed[...], near[...] + far[...])
    lanes = total.shape[1]
    mats = [total[:, k * count : (k + 1) * count] for k in range(5)]
    eye = (
        lax.broadcasted_iota(jnp.int32, (count, count), 0)
        == lax.broadcasted_iota(jnp.int32, (count, count), 1)
    ).astype(f32)
    grams = [
        mats[0],
        jnp.where(place == 0, eye, mats[1]),
        jnp.where(place == last, eye, mats[2]),
    ]
    own, left, right = inverse_factors(grams, eye, lanes)

    high = own.astype(bf16).astype(f32)
    low = own - high
    factor = jnp.concatenate([high, high, low, low], axis=1).astype(bf16)
    stride = slabs.shape[2]
    copies = []
    for block in range(height // 8):
        natural = jnp.where(odd == 1, height // 8 - 1 - block, block)
        for k in range(8):
            row = 8 * block + k
            x = sub_edge[row] if row < SWEEPS else sub_in[row - SWEEPS]
            r = jnp.where(odd == 1, height - 1 - row, row)
            x_high = x.astype(bf16).astype(f32)
            x_low = x - x_high
            value = dot_nn(
                factor, jnp.concatenate([x_high, x_low, x_high, x_low], axis=0).astype(bf16)
            )
            for c in range(sub_width // LANES):
                flat = slabs.at[c].reshape(count * stride, LANES)
                for g in range(count // 8):
                    flat[pl.ds(8 * stride * g + r, 8, stride=stride), :] = value[
                        8 * g : 8 * g + 8, LANES * c : LANES * (c + 1)
                    ]
        at = pl.ds(pl.multiple_of(8 * natural, 8), 8)
        for c in range(sub_width // LANES):
            copy = pltpu.make_async_copy(
                slabs.at[c, :, at],
                basis.at[:, at, pl.ds(LANES * c, LANES)],
                sems.at[block, c],
            )
            copy.start()
            copies.append(copy)
    coupling[0] = dot_nt(dot_nn(own, mats[3], highest), left, highest)
    coupling[1] = dot_nt(dot_nn(own, mats[4], highest), right, highest)
    wait_all(copies)


def call_prepare(vec, log_own):
    count, _, width = vec.shape
    return pl.pallas_call(
        functools.partial(prepare_kernel, "quad"),
        out_shape=(shape(count + 1, SWEEPS, width),) * 2,
        in_specs=[pl.BlockSpec(memory_space=pltpu.HBM)] * 2,
        out_specs=(VMEM, VMEM),
        scratch_shapes=[pltpu.SemaphoreType.DMA((4,))],
        compiler_params=PARAMS,
        name="prepare",
    )(
        pltpu.with_memory_space_constraint(vec, pltpu.HBM),
        pltpu.with_memory_space_constraint(log_own, pltpu.HBM),
    )


def call_inner(vec, halo_a, log_own):
    count, height, width = vec.shape
    band, groups, inner, total = width // 4, count // 8, height - SWEEPS, height + SWEEPS
    cost = 12 * count * width * SWEEPS * height
    return pl.pallas_call(
        functools.partial(inner_kernel, "quad", "patch"),
        out_shape=(
            shape(2, inner, count, band),
            shape(inner, count, 2 * band),
            shape(inner, count, band),
            shape(inner, count, band),
            shape(SWEEPS, 2, groups, 8, width),
            shape(count, count),
        ),
        scratch_shapes=[
            pltpu.VMEM((total, groups, 8, width), f32),
            pltpu.VMEM((total, groups, 8, width), f32),
            pltpu.VMEM((total - 2, 4, 8, width), f32),
            pltpu.VMEM((width // LANES, count, height + PAD, LANES), f32),
            pltpu.VMEM((width // LANES, count + 1, SWEEPS, LANES), f32),
            pltpu.VMEM((height + 32, width), f32),
            pltpu.VMEM((4, height + 16, width), f32),
            pltpu.SemaphoreType.DMA((height // 8 + 1, width // LANES)),
        ],
        in_specs=[ANY, ANY, VMEM],
        compiler_params=PARAMS,
        cost_estimate=pl.CostEstimate(flops=cost, bytes_accessed=5 << 20, transcendentals=0),
        name="inner",
    )(vec, halo_a, log_own)


def call_edge(halo_b, log_own, rim, gram_inner, outer, send_right, send_left):
    height, width = log_own.shape
    inner, count, band = send_right.shape
    groups = count // 8
    return pl.pallas_call(
        functools.partial(edge_kernel, "quad", "patch"),
        out_shape=(
            shape(2, height + 1, count, band),
            shape(SWEEPS, count, 2 * band),
            shape(height + 1, count, band),
            shape(height + 1, count, band),
        ),
        scratch_shapes=[
            pltpu.VMEM((2 * SWEEPS + 1, groups, 8, width), f32),
            pltpu.VMEM((2 * SWEEPS + 1, groups, 8, width), f32),
            pltpu.VMEM((2 * SWEEPS - 1, 4, 8, width), f32),
            pltpu.VMEM((width // LANES, count + 1, SWEEPS, LANES), f32),
            pltpu.VMEM((40, width), f32),
            pltpu.VMEM((4, 24, width), f32),
            pltpu.SemaphoreType.DMA((width // LANES,)),
        ],
        in_specs=[ANY] + [VMEM] * 6,
        compiler_params=PARAMS,
        name="edge",
    )(halo_b, log_own, rim, gram_inner, outer, send_right, send_left)


def call_product(*blocks):
    count = blocks[0].shape[1]
    return pl.pallas_call(
        functools.partial(product_kernel, "quad", "patch"),
        out_shape=shape(count, LANES),
        compiler_params=PARAMS,
        name="product",
    )(*blocks)


def call_final(near, far, passed, sub_in, sub_edge):
    inner, count, sub_width = sub_in.shape
    height = inner + SWEEPS
    return pl.pallas_call(
        functools.partial(final_kernel, "quad", "patch"),
        out_shape=(shape(count, height, sub_width), shape(2, count, count)),
        out_specs=(ANY, VMEM),
        scratch_shapes=[
            pltpu.VMEM((sub_width // LANES, count, height + PAD, LANES), f32),
            pltpu.SemaphoreType.DMA((height // 8, sub_width // LANES)),
        ],
        compiler_params=PARAMS,
        name="final",
    )(near, far, passed, sub_in, sub_edge)


def pairs(size, first):
    swaps = [(i, i + 1) for i in range(first, size - 1, 2)]
    return swaps + [(j, i) for i, j in swaps]


def on_device(vectors, log_kappa):
    vec, log_own = vectors[0], log_kappa[0]
    patches, quads = lax.axis_size("patch"), lax.axis_size("quad")
    send_a, send_b = call_prepare(vec, log_own)
    halo_a = lax.ppermute(send_a, "quad", pairs(quads, 0))
    halo_b = lax.ppermute(send_b, "quad", pairs(quads, 1))
    outer_in, sub_in, send_1_in, send_2_in, rim, gram_in = call_inner(vec, halo_a, log_own)
    outer, sub_edge, send_1, send_2 = call_edge(
        halo_b, log_own, rim, gram_in, outer_in, send_1_in, send_2_in
    )

    ends, mates = [(0, 0), (3, 3)], [(1, 0), (2, 3)]

    def across(block, first, routes):
        return lax.ppermute(
            block,
            ("patch", "quad"),
            [
                (quads * i + a, quads * j + b)
                for i, j in pairs(patches, first)
                for a, b in routes
            ],
        )

    mate_2 = across(send_2, 1, mates)
    mate_1 = across(send_1, 0, mates)
    chip_mate = lax.ppermute(outer, "quad", mates)
    end_2 = across(send_2, 1, ends)
    end_1 = across(send_1, 0, ends)
    packed = call_product(end_2, mate_2, end_1, mate_1, chip_mate, outer)
    far = lax.ppermute(packed, "quad", [(0, 2), (3, 1)])
    near = lax.ppermute(packed, "quad", [(0, 1), (3, 2)])
    passed = lax.ppermute(near + far, "quad", mates)
    basis, coupling = call_final(near, far, passed, sub_in, sub_edge)
    return basis[None], coupling[None]


def solution(mesh):
    placed = (P("patch", None, "quad", None), P("patch", "quad", None))
    return jax.shard_map(
        on_device,
        mesh=mesh,
        in_specs=placed,
        out_specs=(P("patch", None, "quad", None), P("patch", None, None, None)),
        check_vma=False,
    )
```

```python
import functools

import jax
import jax.numpy as jnp
from jax import lax
from jax.experimental import pallas as pl
from jax.experimental.pallas import tpu as pltpu
from jax.sharding import PartitionSpec as P

SWEEPS = 8

mass_term = 0.1
lower_bound = 0.05
upper_bound = 2.0
mid_value = 0.5 * (upper_bound + lower_bound)
half_width = 0.5 * (upper_bound - lower_bound)
highest = lax.Precision.HIGHEST
f32 = jnp.float32
bf16 = jnp.bfloat16

CENTRE = 2.0 * (mid_value - 1.0) / half_width
FACE = 2.0 / half_width

BLOCKS = 4
LANES = 128
CHUNK = 8
PAD = 8
STEP = 8

PARAMS = pltpu.CompilerParams(vmem_limit_bytes=40 * 1024 * 1024)
ANY = pl.BlockSpec(memory_space=pl.ANY)
VMEM = pl.BlockSpec(memory_space=pltpu.VMEM)


def shape(*dims):
    return jax.ShapeDtypeStruct(dims, f32)


def dot_nt(a, b, precision=None):
    return lax.dot_general(
        a, b, (((1,), (1,)), ((), ())), precision=precision, preferred_element_type=f32
    )


def dot_nn(a, b, precision=None):
    return lax.dot_general(
        a, b, (((1,), (0,)), ((), ())), precision=precision, preferred_element_type=f32
    )


def two_parts(x):
    high = x.astype(bf16).astype(f32)
    return jnp.concatenate([high, x - high], axis=0).astype(bf16)


def gram_product(x, y):
    n, m = x.shape[0], y.shape[0]
    full = dot_nt(two_parts(x), two_parts(y))
    return (full[:n, :m] + full[n:, :m]) + (full[:n, m:] + full[n:, m:])


def permutation(width, inverse):
    row = lax.broadcasted_iota(jnp.int32, (width, width), 0)
    col = lax.broadcasted_iota(jnp.int32, (width, width), 1)
    if inverse:
        row, col = col, row
    target = (row % BLOCKS) * LANES + row // BLOCKS
    return jnp.where(target == col, 1.0, 0.0).astype(bf16)


def permute_columns(x, matrix):
    n = x.shape[0]
    out = dot_nn(two_parts(x), matrix)
    return out[:n] + out[n:]


def blocks_of(value):
    return [value[..., k * LANES : (k + 1) * LANES] for k in range(BLOCKS)]


def left_neighbour(x):
    b = blocks_of(x)
    axis = x.ndim - 1
    return jnp.concatenate([pltpu.roll(b[-1], 1, axis)] + b[:-1], axis=axis)


def right_neighbour(x):
    b = blocks_of(x)
    axis = x.ndim - 1
    return jnp.concatenate(b[1:] + [pltpu.roll(b[0], LANES - 1, axis)], axis=axis)


def face_weights(logs, alive):
    n, width = logs.shape
    kappa = jnp.exp(logs)
    rows = lax.slice_in_dim
    centre = rows(kappa, 8, n - 8, axis=0)
    before = rows(kappa, 7, n - 9, axis=0)
    after = rows(kappa, 9, n - 7, axis=0)
    lane = lax.broadcasted_iota(jnp.int32, centre.shape, 1)
    is_first, is_last = lane == 0, lane == width - 1
    left = jnp.where(is_first, 1.0, left_neighbour(centre))
    right = jnp.where(is_last, 1.0, right_neighbour(centre))
    upper_face = 0.5 * (centre + before)
    lower_face = 0.5 * (centre + after)
    left_face = 0.5 * (centre + left)
    right_face = 0.5 * (centre + right)
    diagonal = upper_face + lower_face + left_face + right_face + mass_term * centre
    scale = FACE * alive / diagonal
    return (
        upper_face * scale,
        lower_face * scale,
        jnp.where(is_first, 0.0, left_face * scale),
        jnp.where(is_last, 0.0, right_face * scale),
    )


def spread_weights(natural, weights, count, natural_row, odd):
    width = weights.shape[-1]

    def body(k, carry):
        r = natural_row(k)
        for i in range(4):
            source = jnp.where(odd == 1, 1 - i, i) if i < 2 else i
            weights[k, i] = jnp.broadcast_to(natural[source, pl.ds(r, 1), :], (8, width))
        return carry

    lax.fori_loop(0, count, body, 0, unroll=2)


def apply_row(now, row, weights, wrow):
    centre = now[row]
    return (
        CENTRE * centre
        + weights[wrow, 0] * now[row - 1]
        + weights[wrow, 1] * now[row + 1]
        + (weights[wrow, 2] * left_neighbour(centre) + weights[wrow, 3] * right_neighbour(centre))
    )


def row_loop(first, last, chunk, body):
    whole = (last - first) // chunk

    def step(k, carry):
        for i in range(chunk):
            body(first + chunk * k + i)
        return carry

    if whole > 1:
        lax.fori_loop(0, whole, step, 0)
    elif whole == 1:
        step(0, 0)
    for row in range(first + whole * chunk, last):
        body(row)


def sweep(level, now, new, weights, first, last, wfirst):
    def body(row):
        value = apply_row(now, row, weights, row - wfirst)
        if level == 1:
            new[row] = 0.5 * value
        else:
            new[row] = value - new[row]

    row_loop(first, last, CHUNK, body)


def load_rows(fields, mixed, target, first, odd, matrix):
    count, rows, width = fields.shape
    x = permute_columns(fields.reshape(count * rows, width), matrix)
    for k, block in enumerate(blocks_of(x)):
        mixed[k] = block
    for i in range(rows):
        r = jnp.where(odd == 1, rows - 1 - i, i)
        for g in range(count // 8):
            parts = [
                mixed[k, pl.ds(8 * rows * g + r, 8, stride=rows), :] for k in range(BLOCKS)
            ]
            target[first + i, g] = jnp.concatenate(parts, axis=1)


def emit(final, first, count, groups, matrix, swap, outs, out_first):
    outer_left, outer_right, sub, send_right_pair, send_left_pair = outs
    width = final.shape[-1]
    x = final[pl.ds(first, 8)].reshape(8 * count, width)
    x = permute_columns(x, matrix).reshape(8, count, width)
    b = blocks_of(x)
    at = pl.ds(out_first, 8)
    outer_left[at] = b[0]
    outer_right[at] = b[3]
    sub[at] = jnp.concatenate(b[1:3], axis=2)
    send_right_pair[at] = jnp.where(swap, b[1], b[2])
    send_left_pair[at] = jnp.where(swap, b[2], b[1])


def rows_as_columns(ref, first, count):
    return jnp.concatenate([ref[first + k] for k in range(count)], axis=1)


def prepare_kernel(quad, vec, log_kappa, send_a, send_b, sems):
    odd = lax.rem(lax.axis_index(quad), 2)
    count, height, _ = vec.shape
    far = height - SWEEPS
    row_a = pl.multiple_of((1 - odd) * far, 8)
    row_b = pl.multiple_of(odd * far, 8)
    copies = []
    for k, (row, dst) in enumerate(((row_b, send_b), (row_a, send_a))):
        copies.append(
            pltpu.make_async_copy(
                vec.at[:, pl.ds(row, SWEEPS), :], dst.at[pl.ds(0, count)], sems.at[2 * k]
            )
        )
        copies.append(
            pltpu.make_async_copy(
                log_kappa.at[pl.ds(row, SWEEPS), :], dst.at[count], sems.at[2 * k + 1]
            )
        )
    for c in copies:
        c.start()
    for c in copies:
        c.wait()


def inner_kernel(
    quad, patch, vec, halo_a, log_kappa,
    outer_left, outer_right, sub, send_right, send_left, rim, gram, own_weights, forth, back,
    even, odd_buf, weights, mixed, logs, natural,
):
    odd = lax.rem(lax.axis_index(quad), 2)
    swap = lax.rem(lax.axis_index(patch), 2) == 1
    total, groups = even.shape[:2]
    height = total - SWEEPS
    count = 8 * groups
    width = even.shape[-1]

    matrix = permutation(width, False)
    forth[...] = matrix
    logs[...] = jnp.zeros(logs.shape, f32)
    logs[pl.ds(16, height)] = permute_columns(log_kappa[...], matrix)
    below = pl.multiple_of(8 + (1 - odd) * (height + 8), 8)
    logs[pl.ds(below, 8)] = permute_columns(halo_a[count], matrix)
    values = face_weights(logs[...], 1.0)
    for i in range(4):
        natural[i] = values[i]

    def natural_row(k):
        return jnp.where(odd == 1, height + 7 - k, k + 8)

    load_rows(halo_a[pl.ds(0, count)], mixed.at[0], even, height, odd, matrix)
    for block in range(height // 8):
        own = pl.multiple_of(8 * jnp.where(odd == 1, height // 8 - 1 - block, block), 8)
        load_rows(
            vec[:, pl.ds(own, 8), :], mixed.at[block + 1], even, 8 * block, odd, matrix
        )
    spread_weights(natural, weights, total - 2, lambda k: natural_row(k + 1), odd)
    own_weights[...] = weights[pl.ds(0, SWEEPS - 1)]

    bufs = (even, odd_buf)
    for level in range(1, SWEEPS + 1):
        now, new = bufs[(level - 1) % 2], bufs[level % 2]
        rim[level - 1, 0] = now[level - 1]
        rim[level - 1, 1] = now[level]
        sweep(level, now, new, weights, level, total - level, 1)

    final = bufs[SWEEPS % 2]
    unmix = permutation(width, True)
    back[...] = unmix
    outs = (outer_left, outer_right, sub, send_right, send_left)

    def finish(block, carry):
        row = pl.multiple_of(8 * block, 8)
        emit(final, row + 8, count, groups, unmix, swap, outs, row)
        return carry

    lax.fori_loop(0, (height - SWEEPS) // 8, finish, 0, unroll=True)
    x = rows_as_columns(sub, 0, height - SWEEPS)
    gram[...] = gram_product(x, x)


def edge_kernel(
    quad, patch, halo_b, log_kappa, rim, gram_inner, own_weights, forth, back,
    send_right_in, send_left_in, outer_left, outer_right, sub, send_right, send_left,
    even, odd_buf, weights, mixed, logs, natural,
):
    index = lax.axis_index(quad)
    odd = lax.rem(index, 2)
    swap = lax.rem(lax.axis_index(patch), 2) == 1
    size = lax.axis_size(quad)
    alive = jnp.where(jnp.logical_or(index == 0, index == size - 1), 0.0, 1.0)
    groups = even.shape[1]
    width = even.shape[-1]
    height = log_kappa.shape[0]
    count = 8 * groups
    matrix = forth[...]
    logs[...] = jnp.zeros(logs.shape, f32)
    own_at = pl.multiple_of(odd * (height - 16), 8)
    place = pl.multiple_of(16 - 8 * odd, 8)
    logs[pl.ds(place, 16)] = permute_columns(log_kappa[pl.ds(own_at, 16), :], matrix)
    halo_at = pl.multiple_of(8 + 16 * odd, 8)
    logs[pl.ds(halo_at, 8)] = permute_columns(halo_b[count], matrix)
    position = lax.broadcasted_iota(jnp.int32, (24, width), 0)
    outside = jnp.logical_and(position >= 16 * odd, position < 8 + 16 * odd)
    values = face_weights(logs[...], jnp.where(outside, alive, 1.0))
    for i in range(4):
        natural[i] = values[i]

    load_rows(halo_b[pl.ds(0, count)], mixed, even, 0, odd, matrix)
    spread_weights(
        natural, weights, SWEEPS, lambda k: jnp.where(odd == 1, 22 - k, k + 1), odd
    )
    weights[pl.ds(SWEEPS, SWEEPS - 1)] = own_weights[...]

    bufs = (even, odd_buf)
    for level in range(1, SWEEPS + 1):
        now, new = bufs[(level - 1) % 2], bufs[level % 2]
        now[level + SWEEPS - 1] = rim[level - 1, 0]
        now[level + SWEEPS] = rim[level - 1, 1]
        sweep(level, now, new, weights, level, level + SWEEPS, 1)

    final = bufs[SWEEPS % 2]
    emit(final, SWEEPS, count, groups, back[...], swap, (outer_left, outer_right, sub, send_right, send_left), 0)
    x = rows_as_columns(sub, 0, SWEEPS)
    total = gram_inner[...] + gram_product(x, x)
    inner = height - SWEEPS
    for out, source in ((send_right, send_right_in), (send_left, send_left_in)):
        out[pl.ds(SWEEPS, inner)] = source[...]
        out[height] = jnp.zeros((count, LANES), f32)
        out[height, :, :count] = total


def product_kernel(
    patch, left_in, left_edge, right_in, right_edge, from_right_pair, from_left_pair, sent, out
):
    swap = lax.rem(lax.axis_index(patch), 2) == 1
    count = out.shape[0]
    inner = left_in.shape[0]
    height = inner + SWEEPS

    def products(mine, mine_edge, theirs):
        x = jnp.concatenate(
            [rows_as_columns(mine_edge, 0, SWEEPS), rows_as_columns(mine, 0, inner)], axis=1
        )
        return gram_product(x, rows_as_columns(theirs, 0, height))

    out[...] = jnp.zeros(out.shape, f32)

    def write(from_left, from_right):
        mats = (
            sent[height, :, :count],
            from_left[height, :, :count],
            from_right[height, :, :count],
            products(left_in, left_edge, from_left),
            products(right_in, right_edge, from_right),
        )
        for k, mat in enumerate(mats):
            out[:, k * count : (k + 1) * count] = mat

    @pl.when(swap)
    def _():
        write(from_right_pair, from_left_pair)

    @pl.when(jnp.logical_not(swap))
    def _():
        write(from_left_pair, from_right_pair)


def inverse_factors(mats, eye, lanes):
    count = eye.shape[0]
    sub = lax.broadcasted_iota(jnp.int32, (count, lanes), 0)
    lane = lax.broadcasted_iota(jnp.int32, (count, lanes), 1)
    zeros = jnp.zeros((count, lanes - 2 * count), f32)
    works = [jnp.concatenate([mat, eye, zeros], axis=1) for mat in mats]
    for j in range(0, count, STEP):
        for m, work in enumerate(works):
            cols = [jnp.broadcast_to(work[:, k : k + 1], (count, lanes)) for k in range(j, j + STEP)]
            rows = [work[k : k + 1] for k in range(j, j + STEP)]
            change = jnp.zeros_like(work)
            for i in range(STEP):
                over = 1.0 / cols[i][j + i : j + i + 1]
                scaled = rows[i] * over
                for k in range(i + 1, STEP):
                    rows[k] = rows[k] - cols[i][j + k : j + k + 1] * scaled
                    cols[k] = cols[k] - cols[i] * (cols[k][j + i : j + i + 1] * over)
                change = change + cols[i] * scaled
            work = jnp.where(sub >= j + STEP, work - change, work)
            for i in range(1, STEP):
                work = jnp.where(sub == j + i, rows[i], work)
            works[m] = work
    out = []
    for work in works:
        diagonal = jnp.sum(jnp.where(sub == lane, work, 0.0), axis=1, keepdims=True)
        out.append((work / jnp.sqrt(diagonal))[:, count : 2 * count])
    return out


def final_kernel(quad, patch, gathered, sub_in, sub_edge, basis, coupling, slabs, sems):
    odd = lax.rem(lax.axis_index(quad), 2)
    place = lax.axis_index(patch)
    last = lax.axis_size(patch) - 1
    inner, count, sub_width = sub_in.shape
    height = inner + SWEEPS
    total = (gathered[0] + gathered[1]) + (gathered[2] + gathered[3])
    lanes = total.shape[1]
    mats = [total[:, k * count : (k + 1) * count] for k in range(5)]
    eye = (
        lax.broadcasted_iota(jnp.int32, (count, count), 0)
        == lax.broadcasted_iota(jnp.int32, (count, count), 1)
    ).astype(f32)
    grams = [
        mats[0],
        jnp.where(place == 0, eye, mats[1]),
        jnp.where(place == last, eye, mats[2]),
    ]
    own, left, right = inverse_factors(grams, eye, lanes)

    high = own.astype(bf16).astype(f32)
    low = own - high
    factor = jnp.concatenate([high, high, low, low], axis=1).astype(bf16)
    stride = slabs.shape[2]
    copies = []
    for block in range(height // 8):
        natural = jnp.where(odd == 1, height // 8 - 1 - block, block)
        for k in range(8):
            row = 8 * block + k
            x = sub_edge[row] if row < SWEEPS else sub_in[row - SWEEPS]
            r = jnp.where(odd == 1, height - 1 - row, row)
            x_high = x.astype(bf16).astype(f32)
            x_low = x - x_high
            value = dot_nn(
                factor, jnp.concatenate([x_high, x_low, x_high, x_low], axis=0).astype(bf16)
            )
            for c in range(sub_width // LANES):
                flat = slabs.at[c].reshape(count * stride, LANES)
                for g in range(count // 8):
                    flat[pl.ds(8 * stride * g + r, 8, stride=stride), :] = value[
                        8 * g : 8 * g + 8, LANES * c : LANES * (c + 1)
                    ]
        at = pl.ds(pl.multiple_of(8 * natural, 8), 8)
        for c in range(sub_width // LANES):
            copy = pltpu.make_async_copy(
                slabs.at[c, :, at],
                basis.at[:, at, pl.ds(LANES * c, LANES)],
                sems.at[block, c],
            )
            copy.start()
            copies.append(copy)
    coupling[0] = dot_nt(dot_nn(own, mats[3], highest), left, highest)
    coupling[1] = dot_nt(dot_nn(own, mats[4], highest), right, highest)
    for copy in copies:
        copy.wait()


def call_prepare(vec, log_own):
    count, _, width = vec.shape
    return pl.pallas_call(
        functools.partial(prepare_kernel, "quad"),
        out_shape=(shape(count + 1, SWEEPS, width),) * 2,
        in_specs=[pl.BlockSpec(memory_space=pltpu.HBM)] * 2,
        out_specs=(VMEM, VMEM),
        scratch_shapes=[pltpu.SemaphoreType.DMA((4,))],
        compiler_params=PARAMS,
        name="prepare",
    )(
        pltpu.with_memory_space_constraint(vec, pltpu.HBM),
        pltpu.with_memory_space_constraint(log_own, pltpu.HBM),
    )


def call_inner(vec, halo_a, log_own):
    count, height, width = vec.shape
    band, groups, inner, total = width // 4, count // 8, height - SWEEPS, height + SWEEPS
    cost = 12 * count * width * SWEEPS * height
    return pl.pallas_call(
        functools.partial(inner_kernel, "quad", "patch"),
        out_shape=(
            shape(inner, count, band),
            shape(inner, count, band),
            shape(inner, count, 2 * band),
            shape(inner, count, band),
            shape(inner, count, band),
            shape(SWEEPS, 2, groups, 8, width),
            shape(count, count),
            shape(SWEEPS - 1, 4, 8, width),
            jax.ShapeDtypeStruct((width, width), bf16),
            jax.ShapeDtypeStruct((width, width), bf16),
        ),
        scratch_shapes=[
            pltpu.VMEM((total, groups, 8, width), f32),
            pltpu.VMEM((total, groups, 8, width), f32),
            pltpu.VMEM((total - 2, 4, 8, width), f32),
            pltpu.VMEM((height // 8 + 1, BLOCKS, 8 * count, LANES), f32),
            pltpu.VMEM((height + 32, width), f32),
            pltpu.VMEM((4, height + 16, width), f32),
        ],
        compiler_params=PARAMS,
        cost_estimate=pl.CostEstimate(flops=cost, bytes_accessed=5 << 20, transcendentals=0),
        name="inner",
    )(vec, halo_a, log_own)


def call_edge(halo_b, log_own, rim, gram_inner, own_weights, forth, back, send_right, send_left):
    height, width = log_own.shape
    inner, count, band = send_right.shape
    groups = count // 8
    return pl.pallas_call(
        functools.partial(edge_kernel, "quad", "patch"),
        out_shape=(
            shape(SWEEPS, count, band),
            shape(SWEEPS, count, band),
            shape(SWEEPS, count, 2 * band),
            shape(height + 1, count, band),
            shape(height + 1, count, band),
        ),
        scratch_shapes=[
            pltpu.VMEM((2 * SWEEPS + 1, groups, 8, width), f32),
            pltpu.VMEM((2 * SWEEPS + 1, groups, 8, width), f32),
            pltpu.VMEM((2 * SWEEPS - 1, 4, 8, width), f32),
            pltpu.VMEM((BLOCKS, 8 * count, LANES), f32),
            pltpu.VMEM((40, width), f32),
            pltpu.VMEM((4, 24, width), f32),
        ],
        compiler_params=PARAMS,
        name="edge",
    )(halo_b, log_own, rim, gram_inner, own_weights, forth, back, send_right, send_left)


def call_product(left_in, left_edge, right_in, right_edge, from_right_pair, from_left_pair, sent):
    count = left_in.shape[1]
    return pl.pallas_call(
        functools.partial(product_kernel, "patch"),
        out_shape=shape(count, LANES),
        compiler_params=PARAMS,
        name="product",
    )(left_in, left_edge, right_in, right_edge, from_right_pair, from_left_pair, sent)


def call_final(gathered, sub_in, sub_edge):
    inner, count, sub_width = sub_in.shape
    height = inner + SWEEPS
    return pl.pallas_call(
        functools.partial(final_kernel, "quad", "patch"),
        out_shape=(shape(count, height, sub_width), shape(2, count, count)),
        out_specs=(ANY, VMEM),
        scratch_shapes=[
            pltpu.VMEM((sub_width // LANES, count, height + PAD, LANES), f32),
            pltpu.SemaphoreType.DMA((height // 8, sub_width // LANES)),
        ],
        compiler_params=PARAMS,
        name="final",
    )(gathered, sub_in, sub_edge)


def pairs(size, first):
    swaps = [(i, i + 1) for i in range(first, size - 1, 2)]
    return swaps + [(j, i) for i, j in swaps]


def on_device(vectors, log_kappa):
    vec, log_own = vectors[0], log_kappa[0]
    patch_size, quad_size = lax.axis_size("patch"), lax.axis_size("quad")
    send_a, send_b = call_prepare(vec, log_own)
    halo_a = lax.ppermute(send_a, "quad", pairs(quad_size, 0))
    halo_b = lax.ppermute(send_b, "quad", pairs(quad_size, 1))
    left_in, right_in, sub_in, send_1_in, send_2_in, *for_edge = call_inner(vec, halo_a, log_own)
    left_edge, right_edge, sub_edge, send_1, send_2 = call_edge(
        halo_b, log_own, *for_edge, send_1_in, send_2_in
    )
    from_2 = lax.ppermute(send_2, "patch", pairs(patch_size, 1))
    from_1 = lax.ppermute(send_1, "patch", pairs(patch_size, 0))
    packed = call_product(left_in, left_edge, right_in, right_edge, from_1, from_2, send_1)
    gathered = lax.all_gather(packed, "quad")
    basis, coupling = call_final(gathered, sub_in, sub_edge)
    return basis[None], coupling[None]


def solution(mesh):
    placed = (P("patch", None, "quad", None), P("patch", "quad", None))
    return jax.shard_map(
        on_device,
        mesh=mesh,
        in_specs=placed,
        out_specs=(P("patch", None, "quad", None), P("patch", None, None, None)),
        check_vma=False,
    )
```

```python
import functools

import jax
import jax.numpy as jnp
from jax import lax
from jax.experimental import pallas as pl
from jax.experimental.pallas import tpu as pltpu
from jax.sharding import PartitionSpec as P

SWEEPS = 8

mass_term = 0.1
lower_bound = 0.05
upper_bound = 2.0
mid_value = 0.5 * (upper_bound + lower_bound)
half_width = 0.5 * (upper_bound - lower_bound)
highest = lax.Precision.HIGHEST
f32 = jnp.float32
bf16 = jnp.bfloat16

CENTRE = 2.0 * (mid_value - 1.0) / half_width
FACE = 2.0 / half_width

BLOCKS = 4
LANES = 128
CHUNK = 8
PAD = 8
STEP = 8

PARAMS = pltpu.CompilerParams(vmem_limit_bytes=40 * 1024 * 1024)
ANY = pl.BlockSpec(memory_space=pl.ANY)
VMEM = pl.BlockSpec(memory_space=pltpu.VMEM)


def shape(*dims):
    return jax.ShapeDtypeStruct(dims, f32)


def dot_nt(a, b, precision=None):
    return lax.dot_general(
        a, b, (((1,), (1,)), ((), ())), precision=precision, preferred_element_type=f32
    )


def dot_nn(a, b, precision=None):
    return lax.dot_general(
        a, b, (((1,), (0,)), ((), ())), precision=precision, preferred_element_type=f32
    )


def two_parts(x):
    high = x.astype(bf16).astype(f32)
    return jnp.concatenate([high, x - high], axis=0).astype(bf16)


def gram_product(x, y):
    n, m = x.shape[0], y.shape[0]
    full = dot_nt(two_parts(x), two_parts(y))
    return (full[:n, :m] + full[n:, :m]) + (full[:n, m:] + full[n:, m:])


def permutation(width, inverse):
    row = lax.broadcasted_iota(jnp.int32, (width, width), 0)
    col = lax.broadcasted_iota(jnp.int32, (width, width), 1)
    if inverse:
        row, col = col, row
    target = (row % BLOCKS) * LANES + row // BLOCKS
    return jnp.where(target == col, 1.0, 0.0).astype(bf16)


def permute_columns(x, matrix):
    n = x.shape[0]
    out = dot_nn(two_parts(x), matrix)
    return out[:n] + out[n:]


def blocks_of(value):
    return [value[..., k * LANES : (k + 1) * LANES] for k in range(BLOCKS)]


def left_neighbour(x):
    b = blocks_of(x)
    axis = x.ndim - 1
    return jnp.concatenate([pltpu.roll(b[-1], 1, axis)] + b[:-1], axis=axis)


def right_neighbour(x):
    b = blocks_of(x)
    axis = x.ndim - 1
    return jnp.concatenate(b[1:] + [pltpu.roll(b[0], LANES - 1, axis)], axis=axis)


def face_weights(logs, alive):
    n, width = logs.shape
    kappa = jnp.exp(logs)
    rows = lax.slice_in_dim
    centre = rows(kappa, 8, n - 8, axis=0)
    before = rows(kappa, 7, n - 9, axis=0)
    after = rows(kappa, 9, n - 7, axis=0)
    lane = lax.broadcasted_iota(jnp.int32, centre.shape, 1)
    is_first, is_last = lane == 0, lane == width - 1
    left = jnp.where(is_first, 1.0, left_neighbour(centre))
    right = jnp.where(is_last, 1.0, right_neighbour(centre))
    upper_face = 0.5 * (centre + before)
    lower_face = 0.5 * (centre + after)
    left_face = 0.5 * (centre + left)
    right_face = 0.5 * (centre + right)
    diagonal = upper_face + lower_face + left_face + right_face + mass_term * centre
    scale = FACE * alive / diagonal
    return (
        upper_face * scale,
        lower_face * scale,
        jnp.where(is_first, 0.0, left_face * scale),
        jnp.where(is_last, 0.0, right_face * scale),
    )


def spread_weights(natural, weights, count, natural_row, odd):
    width = weights.shape[-1]

    def body(k, carry):
        r = natural_row(k)
        for i in range(4):
            source = jnp.where(odd == 1, 1 - i, i) if i < 2 else i
            weights[k, i] = jnp.broadcast_to(natural[source, pl.ds(r, 1), :], (8, width))
        return carry

    lax.fori_loop(0, count, body, 0, unroll=2)


def apply_row(now, row, weights, wrow):
    centre = now[row]
    return (
        CENTRE * centre
        + weights[wrow, 0] * now[row - 1]
        + weights[wrow, 1] * now[row + 1]
        + (weights[wrow, 2] * left_neighbour(centre) + weights[wrow, 3] * right_neighbour(centre))
    )


def row_loop(first, last, chunk, body):
    whole = (last - first) // chunk

    def step(k, carry):
        for i in range(chunk):
            body(first + chunk * k + i)
        return carry

    if whole > 1:
        lax.fori_loop(0, whole, step, 0)
    elif whole == 1:
        step(0, 0)
    for row in range(first + whole * chunk, last):
        body(row)


def sweep(level, now, new, weights, first, last, wfirst):
    def body(row):
        value = apply_row(now, row, weights, row - wfirst)
        if level == 1:
            new[row] = 0.5 * value
        else:
            new[row] = value - new[row]

    row_loop(first, last, CHUNK, body)


def load_rows(fields, mixed, target, first, odd, matrix):
    count, rows, width = fields.shape
    x = permute_columns(fields.reshape(count * rows, width), matrix)
    for k, block in enumerate(blocks_of(x)):
        mixed[k] = block
    for i in range(rows):
        r = jnp.where(odd == 1, rows - 1 - i, i)
        for g in range(count // 8):
            parts = [
                mixed[k, pl.ds(8 * rows * g + r, 8, stride=rows), :] for k in range(BLOCKS)
            ]
            target[first + i, g] = jnp.concatenate(parts, axis=1)


def emit(final, first, count, groups, matrix, swap, outs, out_first):
    outer_left, outer_right, sub, send_right_pair, send_left_pair = outs
    width = final.shape[-1]
    x = final[pl.ds(first, 8)].reshape(8 * count, width)
    x = permute_columns(x, matrix).reshape(8, count, width)
    b = blocks_of(x)
    at = pl.ds(out_first, 8)
    outer_left[at] = b[0]
    outer_right[at] = b[3]
    sub[at] = jnp.concatenate(b[1:3], axis=2)
    send_right_pair[at] = jnp.where(swap, b[1], b[2])
    send_left_pair[at] = jnp.where(swap, b[2], b[1])


def rows_as_columns(ref, first, count):
    return jnp.concatenate([ref[first + k] for k in range(count)], axis=1)


def prepare_kernel(quad, vec, log_kappa, send_a, send_b, sems):
    odd = lax.rem(lax.axis_index(quad), 2)
    count, height, _ = vec.shape
    far = height - SWEEPS
    row_a = pl.multiple_of((1 - odd) * far, 8)
    row_b = pl.multiple_of(odd * far, 8)
    copies = []
    for k, (row, dst) in enumerate(((row_b, send_b), (row_a, send_a))):
        copies.append(
            pltpu.make_async_copy(
                vec.at[:, pl.ds(row, SWEEPS), :], dst.at[pl.ds(0, count)], sems.at[2 * k]
            )
        )
        copies.append(
            pltpu.make_async_copy(
                log_kappa.at[pl.ds(row, SWEEPS), :], dst.at[count], sems.at[2 * k + 1]
            )
        )
    for c in copies:
        c.start()
    for c in copies:
        c.wait()


def inner_kernel(
    quad, patch, vec, halo_a, log_kappa,
    outer_left, outer_right, sub, send_right, send_left, rim, gram, own_weights, forth, back,
    even, odd_buf, weights, mixed, logs, natural,
):
    odd = lax.rem(lax.axis_index(quad), 2)
    swap = lax.rem(lax.axis_index(patch), 2) == 1
    total, groups = even.shape[:2]
    height = total - SWEEPS
    count = 8 * groups
    width = even.shape[-1]

    matrix = permutation(width, False)
    forth[...] = matrix
    logs[...] = jnp.zeros(logs.shape, f32)
    logs[pl.ds(16, height)] = permute_columns(log_kappa[...], matrix)
    below = pl.multiple_of(8 + (1 - odd) * (height + 8), 8)
    logs[pl.ds(below, 8)] = permute_columns(halo_a[count], matrix)
    values = face_weights(logs[...], 1.0)
    for i in range(4):
        natural[i] = values[i]

    def natural_row(k):
        return jnp.where(odd == 1, height + 7 - k, k + 8)

    load_rows(halo_a[pl.ds(0, count)], mixed.at[0], even, height, odd, matrix)
    for block in range(height // 8):
        own = pl.multiple_of(8 * jnp.where(odd == 1, height // 8 - 1 - block, block), 8)
        load_rows(
            vec[:, pl.ds(own, 8), :], mixed.at[block + 1], even, 8 * block, odd, matrix
        )
    spread_weights(natural, weights, total - 2, lambda k: natural_row(k + 1), odd)
    own_weights[...] = weights[pl.ds(0, SWEEPS - 1)]

    bufs = (even, odd_buf)
    for level in range(1, SWEEPS + 1):
        now, new = bufs[(level - 1) % 2], bufs[level % 2]
        rim[level - 1, 0] = now[level - 1]
        rim[level - 1, 1] = now[level]
        sweep(level, now, new, weights, level, total - level, 1)

    final = bufs[SWEEPS % 2]
    unmix = permutation(width, True)
    back[...] = unmix
    outs = (outer_left, outer_right, sub, send_right, send_left)

    def finish(block, carry):
        row = pl.multiple_of(8 * block, 8)
        emit(final, row + 8, count, groups, unmix, swap, outs, row)
        return carry

    lax.fori_loop(0, (height - SWEEPS) // 8, finish, 0, unroll=True)
    x = rows_as_columns(sub, 0, height - SWEEPS)
    gram[...] = gram_product(x, x)


def edge_kernel(
    quad, patch, halo_b, log_kappa, rim, gram_inner, own_weights, forth, back,
    send_right_in, send_left_in, outer_left, outer_right, sub, send_right, send_left,
    even, odd_buf, weights, mixed, logs, natural,
):
    index = lax.axis_index(quad)
    odd = lax.rem(index, 2)
    swap = lax.rem(lax.axis_index(patch), 2) == 1
    size = lax.axis_size(quad)
    inside = jnp.logical_and(index > 0, index < size - 1)
    alive = jnp.where(inside, 1.0, 0.0)
    groups = even.shape[1]
    width = even.shape[-1]
    height = log_kappa.shape[0]
    count = 8 * groups
    matrix = forth[...]
    logs[...] = jnp.zeros(logs.shape, f32)
    own_at = pl.multiple_of(odd * (height - 16), 8)
    place = pl.multiple_of(16 - 8 * odd, 8)
    logs[pl.ds(place, 16)] = permute_columns(log_kappa[pl.ds(own_at, 16), :], matrix)
    halo_at = pl.multiple_of(8 + 16 * odd, 8)
    logs[pl.ds(halo_at, 8)] = permute_columns(jnp.where(inside, halo_b[count], 0.0), matrix)
    position = lax.broadcasted_iota(jnp.int32, (24, width), 0)
    outside = jnp.logical_and(position >= 16 * odd, position < 8 + 16 * odd)
    values = face_weights(logs[...], jnp.where(outside, alive, 1.0))
    for i in range(4):
        natural[i] = values[i]

    fields = jnp.where(inside, halo_b[pl.ds(0, count)], 0.0)
    load_rows(fields, mixed, even, 0, odd, matrix)
    spread_weights(
        natural, weights, SWEEPS, lambda k: jnp.where(odd == 1, 22 - k, k + 1), odd
    )
    weights[pl.ds(SWEEPS, SWEEPS - 1)] = own_weights[...]

    bufs = (even, odd_buf)
    for level in range(1, SWEEPS + 1):
        now, new = bufs[(level - 1) % 2], bufs[level % 2]
        now[level + SWEEPS - 1] = rim[level - 1, 0]
        now[level + SWEEPS] = rim[level - 1, 1]
        sweep(level, now, new, weights, level, level + SWEEPS, 1)

    final = bufs[SWEEPS % 2]
    emit(final, SWEEPS, count, groups, back[...], swap, (outer_left, outer_right, sub, send_right, send_left), 0)
    x = rows_as_columns(sub, 0, SWEEPS)
    total = gram_inner[...] + gram_product(x, x)
    inner = height - SWEEPS
    for out, source in ((send_right, send_right_in), (send_left, send_left_in)):
        out[pl.ds(SWEEPS, inner)] = source[...]
        out[height] = jnp.zeros((count, LANES), f32)
        out[height, :, :count] = total


def product_kernel(
    patch, left_in, left_edge, right_in, right_edge, from_right_pair, from_left_pair, sent, out
):
    swap = lax.rem(lax.axis_index(patch), 2) == 1
    count = out.shape[0]
    inner = left_in.shape[0]
    height = inner + SWEEPS

    def products(mine, mine_edge, theirs):
        x = jnp.concatenate(
            [rows_as_columns(mine_edge, 0, SWEEPS), rows_as_columns(mine, 0, inner)], axis=1
        )
        return gram_product(x, rows_as_columns(theirs, 0, height))

    out[...] = jnp.zeros(out.shape, f32)

    def write(from_left, from_right):
        mats = (
            sent[height, :, :count],
            from_left[height, :, :count],
            from_right[height, :, :count],
            products(left_in, left_edge, from_left),
            products(right_in, right_edge, from_right),
        )
        for k, mat in enumerate(mats):
            out[:, k * count : (k + 1) * count] = mat

    @pl.when(swap)
    def _():
        write(from_right_pair, from_left_pair)

    @pl.when(jnp.logical_not(swap))
    def _():
        write(from_left_pair, from_right_pair)


def inverse_factors(mats, eye, lanes):
    count = eye.shape[0]
    sub = lax.broadcasted_iota(jnp.int32, (count, lanes), 0)
    lane = lax.broadcasted_iota(jnp.int32, (count, lanes), 1)
    zeros = jnp.zeros((count, lanes - 2 * count), f32)
    works = [jnp.concatenate([mat, eye, zeros], axis=1) for mat in mats]
    for j in range(0, count, STEP):
        for m, work in enumerate(works):
            cols = [jnp.broadcast_to(work[:, k : k + 1], (count, lanes)) for k in range(j, j + STEP)]
            rows = [work[k : k + 1] for k in range(j, j + STEP)]
            change = jnp.zeros_like(work)
            for i in range(STEP):
                over = 1.0 / cols[i][j + i : j + i + 1]
                scaled = rows[i] * over
                for k in range(i + 1, STEP):
                    rows[k] = rows[k] - cols[i][j + k : j + k + 1] * scaled
                    cols[k] = cols[k] - cols[i] * (cols[k][j + i : j + i + 1] * over)
                change = change + cols[i] * scaled
            work = jnp.where(sub >= j + STEP, work - change, work)
            for i in range(1, STEP):
                work = jnp.where(sub == j + i, rows[i], work)
            works[m] = work
    out = []
    for work in works:
        diagonal = jnp.sum(jnp.where(sub == lane, work, 0.0), axis=1, keepdims=True)
        out.append((work / jnp.sqrt(diagonal))[:, count : 2 * count])
    return out


def final_kernel(quad, patch, chip, other, sub_in, sub_edge, basis, coupling, slabs, sems):
    odd = lax.rem(lax.axis_index(quad), 2)
    place = lax.axis_index(patch)
    last = lax.axis_size(patch) - 1
    inner, count, sub_width = sub_in.shape
    height = inner + SWEEPS
    total = chip[...] + other[...]
    lanes = total.shape[1]
    mats = [total[:, k * count : (k + 1) * count] for k in range(5)]
    eye = (
        lax.broadcasted_iota(jnp.int32, (count, count), 0)
        == lax.broadcasted_iota(jnp.int32, (count, count), 1)
    ).astype(f32)
    grams = [
        mats[0],
        jnp.where(place == 0, eye, mats[1]),
        jnp.where(place == last, eye, mats[2]),
    ]
    own, left, right = inverse_factors(grams, eye, lanes)
    from_left = jnp.where(place == 0, 0.0, mats[3])
    from_right = jnp.where(place == last, 0.0, mats[4])

    high = own.astype(bf16).astype(f32)
    low = own - high
    factor = jnp.concatenate([high, high, low, low], axis=1).astype(bf16)
    stride = slabs.shape[2]
    copies = []
    for block in range(height // 8):
        natural = jnp.where(odd == 1, height // 8 - 1 - block, block)
        for k in range(8):
            row = 8 * block + k
            x = sub_edge[row] if row < SWEEPS else sub_in[row - SWEEPS]
            r = jnp.where(odd == 1, height - 1 - row, row)
            x_high = x.astype(bf16).astype(f32)
            x_low = x - x_high
            value = dot_nn(
                factor, jnp.concatenate([x_high, x_low, x_high, x_low], axis=0).astype(bf16)
            )
            for c in range(sub_width // LANES):
                flat = slabs.at[c].reshape(count * stride, LANES)
                for g in range(count // 8):
                    flat[pl.ds(8 * stride * g + r, 8, stride=stride), :] = value[
                        8 * g : 8 * g + 8, LANES * c : LANES * (c + 1)
                    ]
        at = pl.ds(pl.multiple_of(8 * natural, 8), 8)
        for c in range(sub_width // LANES):
            copy = pltpu.make_async_copy(
                slabs.at[c, :, at],
                basis.at[:, at, pl.ds(LANES * c, LANES)],
                sems.at[block, c],
            )
            copy.start()
            copies.append(copy)
    coupling[0] = dot_nt(dot_nn(own, from_left, highest), left, highest)
    coupling[1] = dot_nt(dot_nn(own, from_right, highest), right, highest)
    for copy in copies:
        copy.wait()


def call_prepare(vec, log_own):
    count, _, width = vec.shape
    return pl.pallas_call(
        functools.partial(prepare_kernel, "quad"),
        out_shape=(shape(count + 1, SWEEPS, width),) * 2,
        in_specs=[pl.BlockSpec(memory_space=pltpu.HBM)] * 2,
        out_specs=(VMEM, VMEM),
        scratch_shapes=[pltpu.SemaphoreType.DMA((4,))],
        compiler_params=PARAMS,
        name="prepare",
    )(
        pltpu.with_memory_space_constraint(vec, pltpu.HBM),
        pltpu.with_memory_space_constraint(log_own, pltpu.HBM),
    )


def call_inner(vec, halo_a, log_own):
    count, height, width = vec.shape
    band, groups, inner, total = width // 4, count // 8, height - SWEEPS, height + SWEEPS
    cost = 12 * count * width * SWEEPS * height
    return pl.pallas_call(
        functools.partial(inner_kernel, "quad", "patch"),
        out_shape=(
            shape(inner, count, band),
            shape(inner, count, band),
            shape(inner, count, 2 * band),
            shape(inner, count, band),
            shape(inner, count, band),
            shape(SWEEPS, 2, groups, 8, width),
            shape(count, count),
            shape(SWEEPS - 1, 4, 8, width),
            jax.ShapeDtypeStruct((width, width), bf16),
            jax.ShapeDtypeStruct((width, width), bf16),
        ),
        scratch_shapes=[
            pltpu.VMEM((total, groups, 8, width), f32),
            pltpu.VMEM((total, groups, 8, width), f32),
            pltpu.VMEM((total - 2, 4, 8, width), f32),
            pltpu.VMEM((height // 8 + 1, BLOCKS, 8 * count, LANES), f32),
            pltpu.VMEM((height + 32, width), f32),
            pltpu.VMEM((4, height + 16, width), f32),
        ],
        compiler_params=PARAMS,
        cost_estimate=pl.CostEstimate(flops=cost, bytes_accessed=5 << 20, transcendentals=0),
        name="inner",
    )(vec, halo_a, log_own)


def call_edge(halo_b, log_own, rim, gram_inner, own_weights, forth, back, send_right, send_left):
    height, width = log_own.shape
    inner, count, band = send_right.shape
    groups = count // 8
    return pl.pallas_call(
        functools.partial(edge_kernel, "quad", "patch"),
        out_shape=(
            shape(SWEEPS, count, band),
            shape(SWEEPS, count, band),
            shape(SWEEPS, count, 2 * band),
            shape(height + 1, count, band),
            shape(height + 1, count, band),
        ),
        scratch_shapes=[
            pltpu.VMEM((2 * SWEEPS + 1, groups, 8, width), f32),
            pltpu.VMEM((2 * SWEEPS + 1, groups, 8, width), f32),
            pltpu.VMEM((2 * SWEEPS - 1, 4, 8, width), f32),
            pltpu.VMEM((BLOCKS, 8 * count, LANES), f32),
            pltpu.VMEM((40, width), f32),
            pltpu.VMEM((4, 24, width), f32),
        ],
        compiler_params=PARAMS,
        name="edge",
    )(halo_b, log_own, rim, gram_inner, own_weights, forth, back, send_right, send_left)


def call_product(left_in, left_edge, right_in, right_edge, from_right_pair, from_left_pair, sent):
    count = left_in.shape[1]
    return pl.pallas_call(
        functools.partial(product_kernel, "patch"),
        out_shape=shape(count, LANES),
        compiler_params=PARAMS,
        name="product",
    )(left_in, left_edge, right_in, right_edge, from_right_pair, from_left_pair, sent)


def call_final(chip, other, sub_in, sub_edge):
    inner, count, sub_width = sub_in.shape
    height = inner + SWEEPS
    return pl.pallas_call(
        functools.partial(final_kernel, "quad", "patch"),
        out_shape=(shape(count, height, sub_width), shape(2, count, count)),
        out_specs=(ANY, VMEM),
        scratch_shapes=[
            pltpu.VMEM((sub_width // LANES, count, height + PAD, LANES), f32),
            pltpu.SemaphoreType.DMA((height // 8, sub_width // LANES)),
        ],
        compiler_params=PARAMS,
        name="final",
    )(chip, other, sub_in, sub_edge)


def swaps(size, first):
    route = [(i, i + 1) for i in range(first, size - 1, 2)]
    return route + [(j, i) for i, j in route]


def on_device(vectors, log_kappa):
    vec, log_own = vectors[0], log_kappa[0]
    patches, quads = lax.axis_size("patch"), lax.axis_size("quad")
    send_a, send_b = call_prepare(vec, log_own)
    halo_a = lax.ppermute(send_a, "quad", swaps(quads, 0))
    middle = [(quads * p + i, quads * p + j) for p in range(patches) for i, j in swaps(quads, 1)]
    idle = [
        (quads * i + q, quads * j + q) for i, j in swaps(patches, 0) for q in (0, quads - 1)
    ]
    halo_b = lax.ppermute(send_b, ("patch", "quad"), middle + idle)
    left_in, right_in, sub_in, send_1_in, send_2_in, *for_edge = call_inner(vec, halo_a, log_own)
    left_edge, right_edge, sub_edge, send_1, send_2 = call_edge(
        halo_b, log_own, *for_edge, send_1_in, send_2_in
    )
    partners = [
        (quads * i + q, quads * j + q) for i, j in swaps(patches, 1) for q in range(quads)
    ]
    idle = [
        (quads * p + i, quads * p + j) for p in (0, patches - 1) for i, j in swaps(quads, 0)
    ]
    from_2 = lax.ppermute(send_2, ("patch", "quad"), partners + idle)
    from_1 = lax.ppermute(send_1, "patch", swaps(patches, 0))
    packed = call_product(left_in, left_edge, right_in, right_edge, from_1, from_2, send_1)
    chip = packed + lax.ppermute(packed, "quad", swaps(quads, 0))
    half = quads // 2
    other = lax.ppermute(chip, "quad", [(i, (i + half) % quads) for i in range(quads)])
    basis, coupling = call_final(chip, other, sub_in, sub_edge)
    return basis[None], coupling[None]


def solution(mesh):
    placed = (P("patch", None, "quad", None), P("patch", "quad", None))
    return jax.shard_map(
        on_device,
        mesh=mesh,
        in_specs=placed,
        out_specs=(P("patch", None, "quad", None), P("patch", None, None, None)),
        check_vma=False,
    )
```

```python
import functools

import jax
import jax.numpy as jnp
from jax import lax
from jax.experimental import pallas as pl
from jax.experimental.pallas import tpu as pltpu
from jax.sharding import PartitionSpec as P

SWEEPS = 8

mass_term = 0.1
lower_bound = 0.05
upper_bound = 2.0
mid_value = 0.5 * (upper_bound + lower_bound)
half_width = 0.5 * (upper_bound - lower_bound)
highest = lax.Precision.HIGHEST
f32 = jnp.float32
bf16 = jnp.bfloat16

CENTRE = 2.0 * (mid_value - 1.0) / half_width
FACE = 2.0 / half_width

BLOCKS = 4
LANES = 128
CHUNK = 8
PAD = 8
STEP = 8

PARAMS = pltpu.CompilerParams(vmem_limit_bytes=40 * 1024 * 1024)
ANY = pl.BlockSpec(memory_space=pl.ANY)
VMEM = pl.BlockSpec(memory_space=pltpu.VMEM)


def shape(*dims):
    return jax.ShapeDtypeStruct(dims, f32)


def dot_nt(a, b, precision=None):
    return lax.dot_general(
        a, b, (((1,), (1,)), ((), ())), precision=precision, preferred_element_type=f32
    )


def dot_nn(a, b, precision=None):
    return lax.dot_general(
        a, b, (((1,), (0,)), ((), ())), precision=precision, preferred_element_type=f32
    )


def two_parts(x):
    high = x.astype(bf16).astype(f32)
    return jnp.concatenate([high, x - high], axis=0).astype(bf16)


def gram_product(x, y):
    n, m = x.shape[0], y.shape[0]
    full = dot_nt(two_parts(x), two_parts(y))
    return (full[:n, :m] + full[n:, :m]) + (full[:n, m:] + full[n:, m:])


def interleaved(column):
    return (column & (BLOCKS - 1)) * LANES + lax.shift_right_logical(column, 2)


def permutation(width, inverse):
    shape = (width, LANES)
    row = lax.broadcasted_iota(jnp.int32, shape, 0)
    lane = lax.broadcasted_iota(jnp.int32, shape, 1)
    wanted = row if inverse else interleaved(row)
    blocks = []
    for k in range(width // LANES):
        if inverse:
            one = lax.broadcasted_iota(jnp.int32, (8, LANES), 1) + k * LANES
            place = jnp.concatenate([interleaved(one)] * (width // 8), axis=0)
        else:
            place = lane + k * LANES
        blocks.append(jnp.where(wanted == place, 1.0, 0.0))
    return jnp.concatenate(blocks, axis=1).astype(bf16)


def permute_columns(x, matrix):
    n = x.shape[0]
    out = dot_nn(two_parts(x), matrix)
    return out[:n] + out[n:]


def blocks_of(value):
    return [value[..., k * LANES : (k + 1) * LANES] for k in range(BLOCKS)]


def left_neighbour(x):
    b = blocks_of(x)
    axis = x.ndim - 1
    return jnp.concatenate([pltpu.roll(b[-1], 1, axis)] + b[:-1], axis=axis)


def right_neighbour(x):
    b = blocks_of(x)
    axis = x.ndim - 1
    return jnp.concatenate(b[1:] + [pltpu.roll(b[0], LANES - 1, axis)], axis=axis)


def face_weights(logs, alive):
    n, width = logs.shape
    kappa = jnp.exp(logs)
    rows = lax.slice_in_dim
    centre = rows(kappa, 8, n - 8, axis=0)
    before = rows(kappa, 7, n - 9, axis=0)
    after = rows(kappa, 9, n - 7, axis=0)
    lane = lax.broadcasted_iota(jnp.int32, centre.shape, 1)
    is_first, is_last = lane == 0, lane == width - 1
    left = jnp.where(is_first, 1.0, left_neighbour(centre))
    right = jnp.where(is_last, 1.0, right_neighbour(centre))
    upper_face = 0.5 * (centre + before)
    lower_face = 0.5 * (centre + after)
    left_face = 0.5 * (centre + left)
    right_face = 0.5 * (centre + right)
    diagonal = upper_face + lower_face + left_face + right_face + mass_term * centre
    scale = FACE * alive / diagonal
    return (
        upper_face * scale,
        lower_face * scale,
        jnp.where(is_first, 0.0, left_face * scale),
        jnp.where(is_last, 0.0, right_face * scale),
    )


def spread_weights(natural, weights, count, natural_row, odd):
    width = weights.shape[-1]

    def body(k, carry):
        r = natural_row(k)
        for i in range(4):
            source = jnp.where(odd == 1, 1 - i, i) if i < 2 else i
            weights[k, i] = jnp.broadcast_to(natural[source, pl.ds(r, 1), :], (8, width))
        return carry

    lax.fori_loop(0, count, body, 0, unroll=8 if count % 8 == 0 else 19)


def apply_row(now, row, weights, wrow):
    centre = now[row]
    return (
        CENTRE * centre
        + weights[wrow, 0] * now[row - 1]
        + weights[wrow, 1] * now[row + 1]
        + (weights[wrow, 2] * left_neighbour(centre) + weights[wrow, 3] * right_neighbour(centre))
    )


def row_loop(first, last, chunk, body):
    whole = (last - first) // chunk

    def step(k, carry):
        for i in range(chunk):
            body(first + chunk * k + i)
        return carry

    if whole > 1:
        lax.fori_loop(0, whole, step, 0)
    elif whole == 1:
        step(0, 0)
    for row in range(first + whole * chunk, last):
        body(row)


def sweep(level, now, new, weights, first, last, wfirst):
    def body(row):
        value = apply_row(now, row, weights, row - wfirst)
        if level == 1:
            new[row] = 0.5 * value
        else:
            new[row] = value - new[row]

    row_loop(first, last, CHUNK, body)


def load_rows(fields, mixed, target, first, odd, matrix):
    count, rows, width = fields.shape
    x = permute_columns(fields.reshape(count * rows, width), matrix)
    for k, block in enumerate(blocks_of(x)):
        mixed[k] = block
    for i in range(rows):
        r = jnp.where(odd == 1, rows - 1 - i, i)
        for g in range(count // 8):
            parts = [
                mixed[k, pl.ds(8 * rows * g + r, 8, stride=rows), :] for k in range(BLOCKS)
            ]
            target[first + i, g] = jnp.concatenate(parts, axis=1)


def emit(final, first, count, groups, matrix, swap, outs, out_first):
    outer_left, outer_right, sub, send_right_pair, send_left_pair = outs
    width = final.shape[-1]
    x = final[pl.ds(first, 8)].reshape(8 * count, width)
    x = permute_columns(x, matrix).reshape(8, count, width)
    b = blocks_of(x)
    at = pl.ds(out_first, 8)
    outer_left[at] = b[0]
    outer_right[at] = b[3]
    sub[at] = jnp.concatenate(b[1:3], axis=2)
    send_right_pair[at] = jnp.where(swap, b[1], b[2])
    send_left_pair[at] = jnp.where(swap, b[2], b[1])


def rows_as_columns(ref, first, count):
    return jnp.concatenate([ref[first + k] for k in range(count)], axis=1)


def prepare_kernel(quad, vec, log_kappa, send_a, send_b, sems):
    odd = lax.rem(lax.axis_index(quad), 2)
    count, height, _ = vec.shape
    far = height - SWEEPS
    row_a = pl.multiple_of((1 - odd) * far, 8)
    row_b = pl.multiple_of(odd * far, 8)
    copies = []
    for k, (row, dst) in enumerate(((row_b, send_b), (row_a, send_a))):
        copies.append(
            pltpu.make_async_copy(
                vec.at[:, pl.ds(row, SWEEPS), :], dst.at[pl.ds(0, count)], sems.at[2 * k]
            )
        )
        copies.append(
            pltpu.make_async_copy(
                log_kappa.at[pl.ds(row, SWEEPS), :], dst.at[count], sems.at[2 * k + 1]
            )
        )
    for c in copies:
        c.start()
    for c in copies:
        c.wait()


def inner_kernel(
    quad, patch, vec, halo_a, log_kappa,
    outer_left, outer_right, sub, send_right, send_left, rim, gram, own_weights, forth, back,
    even, odd_buf, weights, mixed, logs, natural,
):
    odd = lax.rem(lax.axis_index(quad), 2)
    swap = lax.rem(lax.axis_index(patch), 2) == 1
    total, groups = even.shape[:2]
    height = total - SWEEPS
    count = 8 * groups
    width = even.shape[-1]

    matrix = permutation(width, False)
    forth[...] = matrix
    logs[...] = jnp.zeros(logs.shape, f32)
    logs[pl.ds(16, height)] = permute_columns(log_kappa[...], matrix)
    below = pl.multiple_of(8 + (1 - odd) * (height + 8), 8)
    logs[pl.ds(below, 8)] = permute_columns(halo_a[count], matrix)
    values = face_weights(logs[...], 1.0)
    for i in range(4):
        natural[i] = values[i]

    def natural_row(k):
        return jnp.where(odd == 1, height + 7 - k, k + 8)

    load_rows(halo_a[pl.ds(0, count)], mixed.at[0], even, height, odd, matrix)
    for block in range(height // 8):
        own = pl.multiple_of(8 * jnp.where(odd == 1, height // 8 - 1 - block, block), 8)
        load_rows(
            vec[:, pl.ds(own, 8), :], mixed.at[block + 1], even, 8 * block, odd, matrix
        )
    spread_weights(natural, weights, total - 2, lambda k: natural_row(k + 1), odd)
    own_weights[...] = weights[pl.ds(0, SWEEPS - 1)]

    bufs = (even, odd_buf)
    for level in range(1, SWEEPS + 1):
        now, new = bufs[(level - 1) % 2], bufs[level % 2]
        rim[level - 1, 0] = now[level - 1]
        rim[level - 1, 1] = now[level]
        sweep(level, now, new, weights, level, total - level, 1)

    final = bufs[SWEEPS % 2]
    unmix = permutation(width, True)
    back[...] = unmix
    outs = (outer_left, outer_right, sub, send_right, send_left)

    def finish(block, carry):
        row = pl.multiple_of(8 * block, 8)
        emit(final, row + 8, count, groups, unmix, swap, outs, row)
        return carry

    lax.fori_loop(0, (height - SWEEPS) // 8, finish, 0, unroll=True)
    x = rows_as_columns(sub, 0, height - SWEEPS)
    gram[...] = gram_product(x, x)


def edge_kernel(
    quad, patch, halo_b, log_kappa, rim, gram_inner, own_weights, forth, back,
    send_right_in, send_left_in, outer_left, outer_right, sub, send_right, send_left,
    even, odd_buf, weights, mixed, logs, natural,
):
    index = lax.axis_index(quad)
    odd = lax.rem(index, 2)
    swap = lax.rem(lax.axis_index(patch), 2) == 1
    size = lax.axis_size(quad)
    inside = jnp.logical_and(index > 0, index < size - 1)
    alive = jnp.where(inside, 1.0, 0.0)
    groups = even.shape[1]
    width = even.shape[-1]
    height = log_kappa.shape[0]
    count = 8 * groups
    matrix = forth[...]
    logs[...] = jnp.zeros(logs.shape, f32)
    own_at = pl.multiple_of(odd * (height - 16), 8)
    place = pl.multiple_of(16 - 8 * odd, 8)
    logs[pl.ds(place, 16)] = permute_columns(log_kappa[pl.ds(own_at, 16), :], matrix)
    halo_at = pl.multiple_of(8 + 16 * odd, 8)
    logs[pl.ds(halo_at, 8)] = permute_columns(jnp.where(inside, halo_b[count], 0.0), matrix)
    position = lax.broadcasted_iota(jnp.int32, (24, width), 0)
    outside = jnp.logical_and(position >= 16 * odd, position < 8 + 16 * odd)
    values = face_weights(logs[...], jnp.where(outside, alive, 1.0))
    for i in range(4):
        natural[i] = values[i]

    fields = jnp.where(inside, halo_b[pl.ds(0, count)], 0.0)
    load_rows(fields, mixed, even, 0, odd, matrix)
    spread_weights(
        natural, weights, SWEEPS, lambda k: jnp.where(odd == 1, 22 - k, k + 1), odd
    )
    weights[pl.ds(SWEEPS, SWEEPS - 1)] = own_weights[...]

    bufs = (even, odd_buf)
    for level in range(1, SWEEPS + 1):
        now, new = bufs[(level - 1) % 2], bufs[level % 2]
        now[level + SWEEPS - 1] = rim[level - 1, 0]
        now[level + SWEEPS] = rim[level - 1, 1]
        sweep(level, now, new, weights, level, level + SWEEPS, 1)

    final = bufs[SWEEPS % 2]
    emit(final, SWEEPS, count, groups, back[...], swap, (outer_left, outer_right, sub, send_right, send_left), 0)
    x = rows_as_columns(sub, 0, SWEEPS)
    total = gram_inner[...] + gram_product(x, x)
    inner = height - SWEEPS
    for out, source in ((send_right, send_right_in), (send_left, send_left_in)):
        out[pl.ds(SWEEPS, inner)] = source[...]
        out[height] = jnp.zeros((count, LANES), f32)
        out[height, :, :count] = total


def product_kernel(
    patch, left_in, left_edge, right_in, right_edge, from_right_pair, from_left_pair, sent, out
):
    swap = lax.rem(lax.axis_index(patch), 2) == 1
    count = out.shape[0]
    inner = left_in.shape[0]
    height = inner + SWEEPS

    def products(mine, mine_edge, theirs):
        x = jnp.concatenate(
            [rows_as_columns(mine_edge, 0, SWEEPS), rows_as_columns(mine, 0, inner)], axis=1
        )
        return gram_product(x, rows_as_columns(theirs, 0, height))

    out[...] = jnp.zeros(out.shape, f32)

    def write(from_left, from_right):
        mats = (
            sent[height, :, :count],
            from_left[height, :, :count],
            from_right[height, :, :count],
            products(left_in, left_edge, from_left),
            products(right_in, right_edge, from_right),
        )
        for k, mat in enumerate(mats):
            out[:, k * count : (k + 1) * count] = mat

    @pl.when(swap)
    def _():
        write(from_right_pair, from_left_pair)

    @pl.when(jnp.logical_not(swap))
    def _():
        write(from_left_pair, from_right_pair)


def inverse_factors(mats, eye, lanes):
    count = eye.shape[0]
    sub = lax.broadcasted_iota(jnp.int32, (count, lanes), 0)
    lane = lax.broadcasted_iota(jnp.int32, (count, lanes), 1)
    zeros = jnp.zeros((count, lanes - 2 * count), f32)
    works = [jnp.concatenate([mat, eye, zeros], axis=1) for mat in mats]
    for j in range(0, count, STEP):
        for m, work in enumerate(works):
            cols = [jnp.broadcast_to(work[:, k : k + 1], (count, lanes)) for k in range(j, j + STEP)]
            rows = [work[k : k + 1] for k in range(j, j + STEP)]
            change = jnp.zeros_like(work)
            for i in range(STEP):
                over = 1.0 / cols[i][j + i : j + i + 1]
                scaled = rows[i] * over
                for k in range(i + 1, STEP):
                    rows[k] = rows[k] - cols[i][j + k : j + k + 1] * scaled
                    cols[k] = cols[k] - cols[i] * (cols[k][j + i : j + i + 1] * over)
                change = change + cols[i] * scaled
            work = jnp.where(sub >= j + STEP, work - change, work)
            for i in range(1, STEP):
                work = jnp.where(sub == j + i, rows[i], work)
            works[m] = work
    out = []
    for work in works:
        diagonal = jnp.sum(jnp.where(sub == lane, work, 0.0), axis=1, keepdims=True)
        out.append((work / jnp.sqrt(diagonal))[:, count : 2 * count])
    return out


def final_kernel(quad, patch, chip, other, sub_in, sub_edge, basis, coupling, slabs, sems):
    odd = lax.rem(lax.axis_index(quad), 2)
    place = lax.axis_index(patch)
    last = lax.axis_size(patch) - 1
    inner, count, sub_width = sub_in.shape
    height = inner + SWEEPS
    total = chip[...] + other[...]
    lanes = total.shape[1]
    mats = [total[:, k * count : (k + 1) * count] for k in range(5)]
    eye = (
        lax.broadcasted_iota(jnp.int32, (count, count), 0)
        == lax.broadcasted_iota(jnp.int32, (count, count), 1)
    ).astype(f32)
    grams = [
        mats[0],
        jnp.where(place == 0, eye, mats[1]),
        jnp.where(place == last, eye, mats[2]),
    ]
    own, left, right = inverse_factors(grams, eye, lanes)
    from_left = jnp.where(place == 0, 0.0, mats[3])
    from_right = jnp.where(place == last, 0.0, mats[4])

    high = own.astype(bf16).astype(f32)
    low = own - high
    factor = jnp.concatenate([high, high, low, low], axis=1).astype(bf16)
    stride = slabs.shape[2]
    copies = []
    for block in range(height // 8):
        natural = jnp.where(odd == 1, height // 8 - 1 - block, block)
        for k in range(8):
            row = 8 * block + k
            x = sub_edge[row] if row < SWEEPS else sub_in[row - SWEEPS]
            r = jnp.where(odd == 1, height - 1 - row, row)
            x_high = x.astype(bf16).astype(f32)
            x_low = x - x_high
            value = dot_nn(
                factor, jnp.concatenate([x_high, x_low, x_high, x_low], axis=0).astype(bf16)
            )
            for c in range(sub_width // LANES):
                flat = slabs.at[c].reshape(count * stride, LANES)
                for g in range(count // 8):
                    flat[pl.ds(8 * stride * g + r, 8, stride=stride), :] = value[
                        8 * g : 8 * g + 8, LANES * c : LANES * (c + 1)
                    ]
        at = pl.ds(pl.multiple_of(8 * natural, 8), 8)
        for c in range(sub_width // LANES):
            copy = pltpu.make_async_copy(
                slabs.at[c, :, at],
                basis.at[:, at, pl.ds(LANES * c, LANES)],
                sems.at[block, c],
            )
            copy.start()
            copies.append(copy)
    coupling[0] = dot_nt(dot_nn(own, from_left, highest), left, highest)
    coupling[1] = dot_nt(dot_nn(own, from_right, highest), right, highest)
    for copy in copies:
        copy.wait()


def call_prepare(vec, log_own):
    count, _, width = vec.shape
    return pl.pallas_call(
        functools.partial(prepare_kernel, "quad"),
        out_shape=(shape(count + 1, SWEEPS, width),) * 2,
        in_specs=[pl.BlockSpec(memory_space=pltpu.HBM)] * 2,
        out_specs=(VMEM, VMEM),
        scratch_shapes=[pltpu.SemaphoreType.DMA((4,))],
        compiler_params=PARAMS,
        name="prepare",
    )(
        pltpu.with_memory_space_constraint(vec, pltpu.HBM),
        pltpu.with_memory_space_constraint(log_own, pltpu.HBM),
    )


def call_inner(vec, halo_a, log_own):
    count, height, width = vec.shape
    band, groups, inner, total = width // 4, count // 8, height - SWEEPS, height + SWEEPS
    cost = 12 * count * width * SWEEPS * height
    return pl.pallas_call(
        functools.partial(inner_kernel, "quad", "patch"),
        out_shape=(
            shape(inner, count, band),
            shape(inner, count, band),
            shape(inner, count, 2 * band),
            shape(inner, count, band),
            shape(inner, count, band),
            shape(SWEEPS, 2, groups, 8, width),
            shape(count, count),
            shape(SWEEPS - 1, 4, 8, width),
            jax.ShapeDtypeStruct((width, width), bf16),
            jax.ShapeDtypeStruct((width, width), bf16),
        ),
        scratch_shapes=[
            pltpu.VMEM((total, groups, 8, width), f32),
            pltpu.VMEM((total, groups, 8, width), f32),
            pltpu.VMEM((total - 2, 4, 8, width), f32),
            pltpu.VMEM((height // 8 + 1, BLOCKS, 8 * count, LANES), f32),
            pltpu.VMEM((height + 32, width), f32),
            pltpu.VMEM((4, height + 16, width), f32),
        ],
        compiler_params=PARAMS,
        cost_estimate=pl.CostEstimate(flops=cost, bytes_accessed=5 << 20, transcendentals=0),
        name="inner",
    )(vec, halo_a, log_own)


def call_edge(halo_b, log_own, rim, gram_inner, own_weights, forth, back, send_right, send_left):
    height, width = log_own.shape
    inner, count, band = send_right.shape
    groups = count // 8
    return pl.pallas_call(
        functools.partial(edge_kernel, "quad", "patch"),
        out_shape=(
            shape(SWEEPS, count, band),
            shape(SWEEPS, count, band),
            shape(SWEEPS, count, 2 * band),
            shape(height + 1, count, band),
            shape(height + 1, count, band),
        ),
        scratch_shapes=[
            pltpu.VMEM((2 * SWEEPS + 1, groups, 8, width), f32),
            pltpu.VMEM((2 * SWEEPS + 1, groups, 8, width), f32),
            pltpu.VMEM((2 * SWEEPS - 1, 4, 8, width), f32),
            pltpu.VMEM((BLOCKS, 8 * count, LANES), f32),
            pltpu.VMEM((40, width), f32),
            pltpu.VMEM((4, 24, width), f32),
        ],
        compiler_params=PARAMS,
        name="edge",
    )(halo_b, log_own, rim, gram_inner, own_weights, forth, back, send_right, send_left)


def call_product(left_in, left_edge, right_in, right_edge, from_right_pair, from_left_pair, sent):
    count = left_in.shape[1]
    return pl.pallas_call(
        functools.partial(product_kernel, "patch"),
        out_shape=shape(count, LANES),
        compiler_params=PARAMS,
        name="product",
    )(left_in, left_edge, right_in, right_edge, from_right_pair, from_left_pair, sent)


def call_final(chip, other, sub_in, sub_edge):
    inner, count, sub_width = sub_in.shape
    height = inner + SWEEPS
    return pl.pallas_call(
        functools.partial(final_kernel, "quad", "patch"),
        out_shape=(shape(count, height, sub_width), shape(2, count, count)),
        out_specs=(ANY, VMEM),
        scratch_shapes=[
            pltpu.VMEM((sub_width // LANES, count, height + PAD, LANES), f32),
            pltpu.SemaphoreType.DMA((height // 8, sub_width // LANES)),
        ],
        compiler_params=PARAMS,
        name="final",
    )(chip, other, sub_in, sub_edge)


def swaps(size, first):
    route = [(i, i + 1) for i in range(first, size - 1, 2)]
    return route + [(j, i) for i, j in route]


def on_device(vectors, log_kappa):
    vec, log_own = vectors[0], log_kappa[0]
    patches, quads = lax.axis_size("patch"), lax.axis_size("quad")
    send_a, send_b = call_prepare(vec, log_own)
    halo_a = lax.ppermute(send_a, "quad", swaps(quads, 0))
    middle = [(quads * p + i, quads * p + j) for p in range(patches) for i, j in swaps(quads, 1)]
    idle = [
        (quads * i + q, quads * j + q) for i, j in swaps(patches, 0) for q in (0, quads - 1)
    ]
    halo_b = lax.ppermute(send_b, ("patch", "quad"), middle + idle)
    left_in, right_in, sub_in, send_1_in, send_2_in, *for_edge = call_inner(vec, halo_a, log_own)
    left_edge, right_edge, sub_edge, send_1, send_2 = call_edge(
        halo_b, log_own, *for_edge, send_1_in, send_2_in
    )
    partners = [
        (quads * i + q, quads * j + q) for i, j in swaps(patches, 1) for q in range(quads)
    ]
    idle = [
        (quads * p + i, quads * p + j) for p in (0, patches - 1) for i, j in swaps(quads, 0)
    ]
    from_2 = lax.ppermute(send_2, ("patch", "quad"), partners + idle)
    from_1 = lax.ppermute(send_1, "patch", swaps(patches, 0))
    packed = call_product(left_in, left_edge, right_in, right_edge, from_1, from_2, send_1)
    chip = packed + lax.ppermute(packed, "quad", swaps(quads, 0))
    half = quads // 2
    other = lax.ppermute(chip, "quad", [(i, (i + half) % quads) for i in range(quads)])
    basis, coupling = call_final(chip, other, sub_in, sub_edge)
    return basis[None], coupling[None]


def solution(mesh):
    placed = (P("patch", None, "quad", None), P("patch", "quad", None))
    return jax.shard_map(
        on_device,
        mesh=mesh,
        in_specs=placed,
        out_specs=(P("patch", None, "quad", None), P("patch", None, None, None)),
        check_vma=False,
    )
```

```python
import functools

import jax
import jax.numpy as jnp
from jax import lax
from jax.experimental import pallas as pl
from jax.experimental.pallas import tpu as pltpu
from jax.sharding import PartitionSpec as P

SWEEPS = 8

mass_term = 0.1
lower_bound = 0.05
upper_bound = 2.0
mid_value = 0.5 * (upper_bound + lower_bound)
half_width = 0.5 * (upper_bound - lower_bound)
highest = lax.Precision.HIGHEST
f32 = jnp.float32
bf16 = jnp.bfloat16

CENTRE = 2.0 * (mid_value - 1.0) / half_width
FACE = 2.0 / half_width

BLOCKS = 4
LANES = 128
CHUNK = 8
PAD = 8
STEP = 8

PARAMS = pltpu.CompilerParams(vmem_limit_bytes=40 * 1024 * 1024)
ANY = pl.BlockSpec(memory_space=pl.ANY)
VMEM = pl.BlockSpec(memory_space=pltpu.VMEM)


def shape(*dims):
    return jax.ShapeDtypeStruct(dims, f32)


def dot_nt(a, b, precision=None):
    return lax.dot_general(
        a, b, (((1,), (1,)), ((), ())), precision=precision, preferred_element_type=f32
    )


def dot_nn(a, b, precision=None):
    return lax.dot_general(
        a, b, (((1,), (0,)), ((), ())), precision=precision, preferred_element_type=f32
    )


def two_parts(x):
    high = x.astype(bf16).astype(f32)
    return jnp.concatenate([high, x - high], axis=0).astype(bf16)


def gram_product(x, y):
    n, m = x.shape[0], y.shape[0]
    full = dot_nt(two_parts(x), two_parts(y))
    return (full[:n, :m] + full[n:, :m]) + (full[:n, m:] + full[n:, m:])


def interleaved(column):
    return (column & (BLOCKS - 1)) * LANES + lax.shift_right_logical(column, 2)


def permutation(width, inverse):
    shape = (width, LANES)
    row = lax.broadcasted_iota(jnp.int32, shape, 0)
    lane = lax.broadcasted_iota(jnp.int32, shape, 1)
    wanted = row if inverse else interleaved(row)
    blocks = []
    for k in range(width // LANES):
        if inverse:
            one = lax.broadcasted_iota(jnp.int32, (8, LANES), 1) + k * LANES
            place = jnp.concatenate([interleaved(one)] * (width // 8), axis=0)
        else:
            place = lane + k * LANES
        blocks.append(jnp.where(wanted == place, 1.0, 0.0))
    return jnp.concatenate(blocks, axis=1).astype(bf16)


def permute_columns(x, matrix):
    n = x.shape[0]
    out = dot_nn(two_parts(x), matrix)
    return out[:n] + out[n:]


def blocks_of(value):
    return [value[..., k * LANES : (k + 1) * LANES] for k in range(BLOCKS)]


def left_neighbour(x):
    b = blocks_of(x)
    axis = x.ndim - 1
    return jnp.concatenate([pltpu.roll(b[-1], 1, axis)] + b[:-1], axis=axis)


def right_neighbour(x):
    b = blocks_of(x)
    axis = x.ndim - 1
    return jnp.concatenate(b[1:] + [pltpu.roll(b[0], LANES - 1, axis)], axis=axis)


def face_weights(logs, alive):
    n, width = logs.shape
    kappa = jnp.exp(logs)
    rows = lax.slice_in_dim
    centre = rows(kappa, 8, n - 8, axis=0)
    before = rows(kappa, 7, n - 9, axis=0)
    after = rows(kappa, 9, n - 7, axis=0)
    lane = lax.broadcasted_iota(jnp.int32, centre.shape, 1)
    is_first, is_last = lane == 0, lane == width - 1
    left = jnp.where(is_first, 1.0, left_neighbour(centre))
    right = jnp.where(is_last, 1.0, right_neighbour(centre))
    upper_face = 0.5 * (centre + before)
    lower_face = 0.5 * (centre + after)
    left_face = 0.5 * (centre + left)
    right_face = 0.5 * (centre + right)
    diagonal = upper_face + lower_face + left_face + right_face + mass_term * centre
    scale = FACE * alive / diagonal
    return (
        upper_face * scale,
        lower_face * scale,
        jnp.where(is_first, 0.0, left_face * scale),
        jnp.where(is_last, 0.0, right_face * scale),
    )


def spread_weights(natural, weights, count, natural_row, odd):
    width = weights.shape[-1]

    def body(k, carry):
        r = natural_row(k)
        for i in range(4):
            source = jnp.where(odd == 1, 1 - i, i) if i < 2 else i
            weights[k, i] = jnp.broadcast_to(natural[source, pl.ds(r, 1), :], (8, width))
        return carry

    lax.fori_loop(0, count, body, 0, unroll=8 if count % 8 == 0 else 19)


def apply_row(now, row, weights, wrow):
    centre = now[row]
    return (
        CENTRE * centre
        + weights[wrow, 0] * now[row - 1]
        + weights[wrow, 1] * now[row + 1]
        + (weights[wrow, 2] * left_neighbour(centre) + weights[wrow, 3] * right_neighbour(centre))
    )


def row_loop(first, last, chunk, body):
    whole = (last - first) // chunk

    def step(k, carry):
        for i in range(chunk):
            body(first + chunk * k + i)
        return carry

    if whole > 1:
        lax.fori_loop(0, whole, step, 0)
    elif whole == 1:
        step(0, 0)
    for row in range(first + whole * chunk, last):
        body(row)


def sweep(level, now, new, weights, first, last, wfirst):
    def body(row):
        value = apply_row(now, row, weights, row - wfirst)
        if level == 1:
            new[row] = 0.5 * value
        else:
            new[row] = value - new[row]

    row_loop(first, last, CHUNK, body)


def load_rows(fields, mixed, target, first, odd, matrix):
    count, rows, width = fields.shape
    x = permute_columns(fields.reshape(count * rows, width), matrix)
    for k, block in enumerate(blocks_of(x)):
        mixed[k] = block
    for i in range(rows):
        r = jnp.where(odd == 1, rows - 1 - i, i)
        for g in range(count // 8):
            parts = [
                mixed[k, pl.ds(8 * rows * g + r, 8, stride=rows), :] for k in range(BLOCKS)
            ]
            target[first + i, g] = jnp.concatenate(parts, axis=1)


def emit(final, first, count, groups, matrix, swap, outs, out_first):
    outer_left, outer_right, sub, send_right_pair, send_left_pair = outs
    width = final.shape[-1]
    x = final[pl.ds(first, 8)].reshape(8 * count, width)
    x = permute_columns(x, matrix).reshape(8, count, width)
    b = blocks_of(x)
    at = pl.ds(out_first, 8)
    outer_left[at] = b[0]
    outer_right[at] = b[3]
    sub[at] = jnp.concatenate(b[1:3], axis=2)
    send_right_pair[at] = jnp.where(swap, b[1], b[2])
    send_left_pair[at] = jnp.where(swap, b[2], b[1])


def rows_as_columns(ref, first, count):
    return jnp.concatenate([ref[first + k] for k in range(count)], axis=1)


def prepare_kernel(quad, vec, log_kappa, send_a, send_b, sems):
    odd = lax.rem(lax.axis_index(quad), 2)
    count, height, _ = vec.shape
    far = height - SWEEPS
    row_a = pl.multiple_of((1 - odd) * far, 8)
    row_b = pl.multiple_of(odd * far, 8)
    copies = []
    for k, (row, dst) in enumerate(((row_b, send_b), (row_a, send_a))):
        copies.append(
            pltpu.make_async_copy(
                vec.at[:, pl.ds(row, SWEEPS), :], dst.at[pl.ds(0, count)], sems.at[2 * k]
            )
        )
        copies.append(
            pltpu.make_async_copy(
                log_kappa.at[pl.ds(row, SWEEPS), :], dst.at[count], sems.at[2 * k + 1]
            )
        )
    for c in copies:
        c.start()
    for c in copies:
        c.wait()


def inner_kernel(
    quad, patch, vec, halo_a, log_kappa,
    outer_left, outer_right, sub, send_right, send_left, rim, gram, own_weights, forth, back,
    even, odd_buf, weights, mixed, logs, natural,
):
    odd = lax.rem(lax.axis_index(quad), 2)
    swap = lax.rem(lax.axis_index(patch), 2) == 1
    total, groups = even.shape[:2]
    height = total - SWEEPS
    count = 8 * groups
    width = even.shape[-1]

    matrix = permutation(width, False)
    forth[...] = matrix
    logs[...] = jnp.zeros(logs.shape, f32)
    logs[pl.ds(16, height)] = permute_columns(log_kappa[...], matrix)
    below = pl.multiple_of(8 + (1 - odd) * (height + 8), 8)
    logs[pl.ds(below, 8)] = permute_columns(halo_a[count], matrix)
    values = face_weights(logs[...], 1.0)
    for i in range(4):
        natural[i] = values[i]

    def natural_row(k):
        return jnp.where(odd == 1, height + 7 - k, k + 8)

    load_rows(halo_a[pl.ds(0, count)], mixed.at[0], even, height, odd, matrix)
    for block in range(height // 8):
        own = pl.multiple_of(8 * jnp.where(odd == 1, height // 8 - 1 - block, block), 8)
        load_rows(
            vec[:, pl.ds(own, 8), :], mixed.at[block + 1], even, 8 * block, odd, matrix
        )
    spread_weights(natural, weights, total - 2, lambda k: natural_row(k + 1), odd)
    own_weights[...] = weights[pl.ds(0, SWEEPS - 1)]

    bufs = (even, odd_buf)
    for level in range(1, SWEEPS + 1):
        now, new = bufs[(level - 1) % 2], bufs[level % 2]
        rim[level - 1, 0] = now[level - 1]
        rim[level - 1, 1] = now[level]
        sweep(level, now, new, weights, level, total - level, 1)

    final = bufs[SWEEPS % 2]
    unmix = permutation(width, True)
    back[...] = unmix
    outs = (outer_left, outer_right, sub, send_right, send_left)

    def finish(block, carry):
        row = pl.multiple_of(8 * block, 8)
        emit(final, row + 8, count, groups, unmix, swap, outs, row)
        return carry

    lax.fori_loop(0, (height - SWEEPS) // 8, finish, 0, unroll=True)
    x = rows_as_columns(sub, 0, height - SWEEPS)
    gram[...] = gram_product(x, x)


def edge_kernel(
    quad, patch, halo_b, log_kappa, rim, gram_inner, own_weights, forth, back,
    send_right_in, send_left_in, outer_left, outer_right, sub, send_right, send_left,
    even, odd_buf, weights, mixed, logs, natural,
):
    index = lax.axis_index(quad)
    odd = lax.rem(index, 2)
    swap = lax.rem(lax.axis_index(patch), 2) == 1
    size = lax.axis_size(quad)
    inside = jnp.logical_and(index > 0, index < size - 1)
    alive = jnp.where(inside, 1.0, 0.0)
    groups = even.shape[1]
    width = even.shape[-1]
    height = log_kappa.shape[0]
    count = 8 * groups
    matrix = forth[...]
    logs[...] = jnp.zeros(logs.shape, f32)
    own_at = pl.multiple_of(odd * (height - 16), 8)
    place = pl.multiple_of(16 - 8 * odd, 8)
    logs[pl.ds(place, 16)] = permute_columns(log_kappa[pl.ds(own_at, 16), :], matrix)
    halo_at = pl.multiple_of(8 + 16 * odd, 8)
    logs[pl.ds(halo_at, 8)] = permute_columns(jnp.where(inside, halo_b[count], 0.0), matrix)
    position = lax.broadcasted_iota(jnp.int32, (24, width), 0)
    outside = jnp.logical_and(position >= 16 * odd, position < 8 + 16 * odd)
    values = face_weights(logs[...], jnp.where(outside, alive, 1.0))
    for i in range(4):
        natural[i] = values[i]

    fields = jnp.where(inside, halo_b[pl.ds(0, count)], 0.0)
    load_rows(fields, mixed, even, 0, odd, matrix)
    spread_weights(
        natural, weights, SWEEPS, lambda k: jnp.where(odd == 1, 22 - k, k + 1), odd
    )
    weights[pl.ds(SWEEPS, SWEEPS - 1)] = own_weights[...]

    bufs = (even, odd_buf)
    for level in range(1, SWEEPS + 1):
        now, new = bufs[(level - 1) % 2], bufs[level % 2]
        now[level + SWEEPS - 1] = rim[level - 1, 0]
        now[level + SWEEPS] = rim[level - 1, 1]
        sweep(level, now, new, weights, level, level + SWEEPS, 1)

    final = bufs[SWEEPS % 2]
    emit(final, SWEEPS, count, groups, back[...], swap, (outer_left, outer_right, sub, send_right, send_left), 0)
    x = rows_as_columns(sub, 0, SWEEPS)
    total = gram_inner[...] + gram_product(x, x)
    inner = height - SWEEPS
    for out, source in ((send_right, send_right_in), (send_left, send_left_in)):
        out[pl.ds(SWEEPS, inner)] = source[...]
        out[height] = jnp.zeros((count, LANES), f32)
        out[height, :, :count] = total


def product_kernel(
    patch, left_in, left_edge, right_in, right_edge, from_right_pair, from_left_pair, sent, out
):
    swap = lax.rem(lax.axis_index(patch), 2) == 1
    count = out.shape[0]
    inner = left_in.shape[0]
    height = inner + SWEEPS

    def products(mine, mine_edge, theirs):
        x = jnp.concatenate(
            [rows_as_columns(mine_edge, 0, SWEEPS), rows_as_columns(mine, 0, inner)], axis=1
        )
        return gram_product(x, rows_as_columns(theirs, 0, height))

    out[...] = jnp.zeros(out.shape, f32)

    def write(from_left, from_right):
        mats = (
            products(left_in, left_edge, from_left),
            sent[height, :, :count],
            from_left[height, :, :count],
            from_right[height, :, :count],
            products(right_in, right_edge, from_right),
        )
        for k, mat in enumerate(mats):
            out[:, k * count : (k + 1) * count] = mat

    @pl.when(swap)
    def _():
        write(from_right_pair, from_left_pair)

    @pl.when(jnp.logical_not(swap))
    def _():
        write(from_left_pair, from_right_pair)


def inverse_factors(works, offsets, count):
    sub = lax.broadcasted_iota(jnp.int32, works[0].shape, 0)
    scales = [jnp.zeros_like(work) for work in works]
    for j in range(0, count, STEP):
        for m, work in enumerate(works):
            at = [offsets[m] + k for k in range(j, j + STEP)]
            cols = [jnp.broadcast_to(work[:, k : k + 1], work.shape) for k in at]
            rows = [work[k : k + 1] for k in range(j, j + STEP)]
            change = jnp.zeros_like(work)
            for i in range(STEP):
                pivot = cols[i][j + i : j + i + 1]
                scales[m] = jnp.where(sub == j + i, 1.0 / jnp.sqrt(pivot), scales[m])
                over = 1.0 / pivot
                scaled = rows[i] * over
                for k in range(i + 1, STEP):
                    rows[k] = rows[k] - cols[i][j + k : j + k + 1] * scaled
                    cols[k] = cols[k] - cols[i] * (cols[k][j + i : j + i + 1] * over)
                change = change + cols[i] * scaled
            work = jnp.where(sub >= j + STEP, work - change, work)
            for i in range(1, STEP):
                work = jnp.where(sub == j + i, rows[i], work)
            works[m] = work
    return [(work * scale)[:, :count] for work, scale in zip(works, scales)]


def final_kernel(quad, patch, chip, other, sub_in, sub_edge, basis, coupling, slabs, sems):
    odd = lax.rem(lax.axis_index(quad), 2)
    place = lax.axis_index(patch)
    last = lax.axis_size(patch) - 1
    inner, count, sub_width = sub_in.shape
    height = inner + SWEEPS
    total = chip[...] + other[...]
    sub = lax.broadcasted_iota(jnp.int32, total.shape, 0)
    lane = lax.broadcasted_iota(jnp.int32, total.shape, 1)
    works = []
    for k, missing in ((1, None), (2, place == 0), (3, place == last)):
        column = lane - k * count
        work = total if missing is None else jnp.where(missing, (sub == column).astype(f32), total)
        work = jnp.where(jnp.logical_and(column >= 0, column < count), work, 0.0)
        works.append(jnp.where(lane < count, (sub == lane).astype(f32), work))
    own, left, right = inverse_factors(works, (count, 2 * count, 3 * count), count)
    from_left = jnp.where(place == 0, 0.0, total[:, :count])
    from_right = jnp.where(place == last, 0.0, total[:, 4 * count : 5 * count])

    high = own.astype(bf16).astype(f32)
    low = own - high
    factor = jnp.concatenate([high, high, low, low], axis=1).astype(bf16)
    stride = slabs.shape[2]
    copies = []
    for block in range(height // 8):
        natural = jnp.where(odd == 1, height // 8 - 1 - block, block)
        for k in range(8):
            row = 8 * block + k
            x = sub_edge[row] if row < SWEEPS else sub_in[row - SWEEPS]
            r = jnp.where(odd == 1, height - 1 - row, row)
            x_high = x.astype(bf16).astype(f32)
            x_low = x - x_high
            value = dot_nn(
                factor, jnp.concatenate([x_high, x_low, x_high, x_low], axis=0).astype(bf16)
            )
            for c in range(sub_width // LANES):
                flat = slabs.at[c].reshape(count * stride, LANES)
                for g in range(count // 8):
                    flat[pl.ds(8 * stride * g + r, 8, stride=stride), :] = value[
                        8 * g : 8 * g + 8, LANES * c : LANES * (c + 1)
                    ]
        at = pl.ds(pl.multiple_of(8 * natural, 8), 8)
        for c in range(sub_width // LANES):
            copy = pltpu.make_async_copy(
                slabs.at[c, :, at],
                basis.at[:, at, pl.ds(LANES * c, LANES)],
                sems.at[block, c],
            )
            copy.start()
            copies.append(copy)
    coupling[0] = dot_nt(dot_nn(own, from_left, highest), left, highest)
    coupling[1] = dot_nt(dot_nn(own, from_right, highest), right, highest)
    for copy in copies:
        copy.wait()


def call_prepare(vec, log_own):
    count, _, width = vec.shape
    return pl.pallas_call(
        functools.partial(prepare_kernel, "quad"),
        out_shape=(shape(count + 1, SWEEPS, width),) * 2,
        in_specs=[pl.BlockSpec(memory_space=pltpu.HBM)] * 2,
        out_specs=(VMEM, VMEM),
        scratch_shapes=[pltpu.SemaphoreType.DMA((4,))],
        compiler_params=PARAMS,
        name="prepare",
    )(
        pltpu.with_memory_space_constraint(vec, pltpu.HBM),
        pltpu.with_memory_space_constraint(log_own, pltpu.HBM),
    )


def call_inner(vec, halo_a, log_own):
    count, height, width = vec.shape
    band, groups, inner, total = width // 4, count // 8, height - SWEEPS, height + SWEEPS
    cost = 12 * count * width * SWEEPS * height
    return pl.pallas_call(
        functools.partial(inner_kernel, "quad", "patch"),
        out_shape=(
            shape(inner, count, band),
            shape(inner, count, band),
            shape(inner, count, 2 * band),
            shape(inner, count, band),
            shape(inner, count, band),
            shape(SWEEPS, 2, groups, 8, width),
            shape(count, count),
            shape(SWEEPS - 1, 4, 8, width),
            jax.ShapeDtypeStruct((width, width), bf16),
            jax.ShapeDtypeStruct((width, width), bf16),
        ),
        scratch_shapes=[
            pltpu.VMEM((total, groups, 8, width), f32),
            pltpu.VMEM((total, groups, 8, width), f32),
            pltpu.VMEM((total - 2, 4, 8, width), f32),
            pltpu.VMEM((height // 8 + 1, BLOCKS, 8 * count, LANES), f32),
            pltpu.VMEM((height + 32, width), f32),
            pltpu.VMEM((4, height + 16, width), f32),
        ],
        compiler_params=PARAMS,
        cost_estimate=pl.CostEstimate(flops=cost, bytes_accessed=5 << 20, transcendentals=0),
        name="inner",
    )(vec, halo_a, log_own)


def call_edge(halo_b, log_own, rim, gram_inner, own_weights, forth, back, send_right, send_left):
    height, width = log_own.shape
    inner, count, band = send_right.shape
    groups = count // 8
    return pl.pallas_call(
        functools.partial(edge_kernel, "quad", "patch"),
        out_shape=(
            shape(SWEEPS, count, band),
            shape(SWEEPS, count, band),
            shape(SWEEPS, count, 2 * band),
            shape(height + 1, count, band),
            shape(height + 1, count, band),
        ),
        scratch_shapes=[
            pltpu.VMEM((2 * SWEEPS + 1, groups, 8, width), f32),
            pltpu.VMEM((2 * SWEEPS + 1, groups, 8, width), f32),
            pltpu.VMEM((2 * SWEEPS - 1, 4, 8, width), f32),
            pltpu.VMEM((BLOCKS, 8 * count, LANES), f32),
            pltpu.VMEM((40, width), f32),
            pltpu.VMEM((4, 24, width), f32),
        ],
        compiler_params=PARAMS,
        name="edge",
    )(halo_b, log_own, rim, gram_inner, own_weights, forth, back, send_right, send_left)


def call_product(left_in, left_edge, right_in, right_edge, from_right_pair, from_left_pair, sent):
    count = left_in.shape[1]
    return pl.pallas_call(
        functools.partial(product_kernel, "patch"),
        out_shape=shape(count, LANES),
        compiler_params=PARAMS,
        name="product",
    )(left_in, left_edge, right_in, right_edge, from_right_pair, from_left_pair, sent)


def call_final(chip, other, sub_in, sub_edge):
    inner, count, sub_width = sub_in.shape
    height = inner + SWEEPS
    return pl.pallas_call(
        functools.partial(final_kernel, "quad", "patch"),
        out_shape=(shape(count, height, sub_width), shape(2, count, count)),
        out_specs=(ANY, VMEM),
        scratch_shapes=[
            pltpu.VMEM((sub_width // LANES, count, height + PAD, LANES), f32),
            pltpu.SemaphoreType.DMA((height // 8, sub_width // LANES)),
        ],
        compiler_params=PARAMS,
        name="final",
    )(chip, other, sub_in, sub_edge)


def swaps(size, first):
    route = [(i, i + 1) for i in range(first, size - 1, 2)]
    return route + [(j, i) for i, j in route]


def on_device(vectors, log_kappa):
    vec, log_own = vectors[0], log_kappa[0]
    patches, quads = lax.axis_size("patch"), lax.axis_size("quad")
    send_a, send_b = call_prepare(vec, log_own)
    halo_a = lax.ppermute(send_a, "quad", swaps(quads, 0))
    middle = [(quads * p + i, quads * p + j) for p in range(patches) for i, j in swaps(quads, 1)]
    idle = [
        (quads * i + q, quads * j + q) for i, j in swaps(patches, 0) for q in (0, quads - 1)
    ]
    halo_b = lax.ppermute(send_b, ("patch", "quad"), middle + idle)
    left_in, right_in, sub_in, send_1_in, send_2_in, *for_edge = call_inner(vec, halo_a, log_own)
    left_edge, right_edge, sub_edge, send_1, send_2 = call_edge(
        halo_b, log_own, *for_edge, send_1_in, send_2_in
    )
    partners = [
        (quads * i + q, quads * j + q) for i, j in swaps(patches, 1) for q in range(quads)
    ]
    idle = [
        (quads * p + i, quads * p + j) for p in (0, patches - 1) for i, j in swaps(quads, 0)
    ]
    from_2 = lax.ppermute(send_2, ("patch", "quad"), partners + idle)
    from_1 = lax.ppermute(send_1, "patch", swaps(patches, 0))
    packed = call_product(left_in, left_edge, right_in, right_edge, from_1, from_2, send_1)
    chip = packed + lax.ppermute(packed, "quad", swaps(quads, 0))
    half = quads // 2
    other = lax.ppermute(chip, "quad", [(i, (i + half) % quads) for i in range(quads)])
    basis, coupling = call_final(chip, other, sub_in, sub_edge)
    return basis[None], coupling[None]


def solution(mesh):
    placed = (P("patch", None, "quad", None), P("patch", "quad", None))
    return jax.shard_map(
        on_device,
        mesh=mesh,
        in_specs=placed,
        out_specs=(P("patch", None, "quad", None), P("patch", None, None, None)),
        check_vma=False,
    )
```

```python
import functools

import jax
import jax.numpy as jnp
from jax import lax
from jax.experimental import pallas as pl
from jax.experimental.pallas import tpu as pltpu
from jax.sharding import PartitionSpec as P

SWEEPS = 8

mass_term = 0.1
lower_bound = 0.05
upper_bound = 2.0
mid_value = 0.5 * (upper_bound + lower_bound)
half_width = 0.5 * (upper_bound - lower_bound)
highest = lax.Precision.HIGHEST
f32 = jnp.float32
bf16 = jnp.bfloat16

CENTRE = 2.0 * (mid_value - 1.0) / half_width
FACE = 2.0 / half_width

BLOCKS = 4
LANES = 128
CHUNK = 8
PAD = 8
STEP = 8

PARAMS = pltpu.CompilerParams(vmem_limit_bytes=40 * 1024 * 1024)
ANY = pl.BlockSpec(memory_space=pl.ANY)
VMEM = pl.BlockSpec(memory_space=pltpu.VMEM)


def shape(*dims):
    return jax.ShapeDtypeStruct(dims, f32)


def dot_nt(a, b, precision=None):
    return lax.dot_general(
        a, b, (((1,), (1,)), ((), ())), precision=precision, preferred_element_type=f32
    )


def dot_nn(a, b, precision=None):
    return lax.dot_general(
        a, b, (((1,), (0,)), ((), ())), precision=precision, preferred_element_type=f32
    )


def two_parts(x):
    high = x.astype(bf16).astype(f32)
    return jnp.concatenate([high, x - high], axis=0).astype(bf16)


def gram_product(x, y):
    n, m = x.shape[0], y.shape[0]
    full = dot_nt(two_parts(x), two_parts(y))
    return (full[:n, :m] + full[n:, :m]) + (full[:n, m:] + full[n:, m:])


def interleaved(column):
    return (column & (BLOCKS - 1)) * LANES + lax.shift_right_logical(column, 2)


def permutation(width, inverse):
    shape = (width, LANES)
    row = lax.broadcasted_iota(jnp.int32, shape, 0)
    lane = lax.broadcasted_iota(jnp.int32, shape, 1)
    wanted = row if inverse else interleaved(row)
    blocks = []
    for k in range(width // LANES):
        if inverse:
            one = lax.broadcasted_iota(jnp.int32, (8, LANES), 1) + k * LANES
            place = jnp.concatenate([interleaved(one)] * (width // 8), axis=0)
        else:
            place = lane + k * LANES
        blocks.append(jnp.where(wanted == place, 1.0, 0.0))
    return jnp.concatenate(blocks, axis=1).astype(bf16)


def permute_columns(x, matrix):
    n = x.shape[0]
    out = dot_nn(two_parts(x), matrix)
    return out[:n] + out[n:]


def blocks_of(value):
    return [value[..., k * LANES : (k + 1) * LANES] for k in range(BLOCKS)]


def left_neighbour(x):
    b = blocks_of(x)
    axis = x.ndim - 1
    return jnp.concatenate([pltpu.roll(b[-1], 1, axis)] + b[:-1], axis=axis)


def right_neighbour(x):
    b = blocks_of(x)
    axis = x.ndim - 1
    return jnp.concatenate(b[1:] + [pltpu.roll(b[0], LANES - 1, axis)], axis=axis)


def face_weights(logs, alive):
    n, width = logs.shape
    kappa = jnp.exp(logs)
    rows = lax.slice_in_dim
    centre = rows(kappa, 8, n - 8, axis=0)
    before = rows(kappa, 7, n - 9, axis=0)
    after = rows(kappa, 9, n - 7, axis=0)
    lane = lax.broadcasted_iota(jnp.int32, centre.shape, 1)
    is_first, is_last = lane == 0, lane == width - 1
    left = jnp.where(is_first, 1.0, left_neighbour(centre))
    right = jnp.where(is_last, 1.0, right_neighbour(centre))
    upper_face = 0.5 * (centre + before)
    lower_face = 0.5 * (centre + after)
    left_face = 0.5 * (centre + left)
    right_face = 0.5 * (centre + right)
    diagonal = upper_face + lower_face + left_face + right_face + mass_term * centre
    scale = FACE * alive / diagonal
    return (
        upper_face * scale,
        lower_face * scale,
        jnp.where(is_first, 0.0, left_face * scale),
        jnp.where(is_last, 0.0, right_face * scale),
    )


def spread_weights(natural, weights, count, natural_row, odd):
    width = weights.shape[-1]

    def body(k, carry):
        r = natural_row(k)
        for i in range(4):
            source = jnp.where(odd == 1, 1 - i, i) if i < 2 else i
            weights[k, i] = jnp.broadcast_to(natural[source, pl.ds(r, 1), :], (8, width))
        return carry

    lax.fori_loop(0, count, body, 0, unroll=8 if count % 8 == 0 else 19)


def apply_row(now, row, weights, wrow):
    centre = now[row]
    return (
        CENTRE * centre
        + weights[wrow, 0] * now[row - 1]
        + weights[wrow, 1] * now[row + 1]
        + (weights[wrow, 2] * left_neighbour(centre) + weights[wrow, 3] * right_neighbour(centre))
    )


def row_loop(first, last, chunk, body):
    whole = (last - first) // chunk

    def step(k, carry):
        for i in range(chunk):
            body(first + chunk * k + i)
        return carry

    if whole > 1:
        lax.fori_loop(0, whole, step, 0)
    elif whole == 1:
        step(0, 0)
    for row in range(first + whole * chunk, last):
        body(row)


def sweep(level, now, new, weights, first, last, wfirst):
    def body(row):
        value = apply_row(now, row, weights, row - wfirst)
        if level == 1:
            new[row] = 0.5 * value
        else:
            new[row] = value - new[row]

    row_loop(first, last, CHUNK, body)


def load_rows(fields, mixed, target, first, odd, matrix):
    count, rows, width = fields.shape
    x = permute_columns(fields.reshape(count * rows, width), matrix)
    for k, block in enumerate(blocks_of(x)):
        mixed[k] = block
    for i in range(rows):
        r = jnp.where(odd == 1, rows - 1 - i, i)
        for g in range(count // 8):
            parts = [
                mixed[k, pl.ds(8 * rows * g + r, 8, stride=rows), :] for k in range(BLOCKS)
            ]
            target[first + i, g] = jnp.concatenate(parts, axis=1)


def emit(final, first, count, groups, matrix, swap, outs, out_first):
    outer_left, outer_right, sub, send_right_pair, send_left_pair = outs
    width = final.shape[-1]
    x = final[pl.ds(first, 8)].reshape(8 * count, width)
    x = permute_columns(x, matrix).reshape(8, count, width)
    b = blocks_of(x)
    at = pl.ds(out_first, 8)
    outer_left[at] = b[0]
    outer_right[at] = b[3]
    sub[at] = jnp.concatenate(b[1:3], axis=2)
    send_right_pair[at] = jnp.where(swap, b[1], b[2])
    send_left_pair[at] = jnp.where(swap, b[2], b[1])


def rows_as_columns(ref, first, count):
    return jnp.concatenate([ref[first + k] for k in range(count)], axis=1)


def prepare_kernel(quad, vec, log_kappa, send_a, send_b, sems):
    odd = lax.rem(lax.axis_index(quad), 2)
    count, height, _ = vec.shape
    far = height - SWEEPS
    row_a = pl.multiple_of((1 - odd) * far, 8)
    row_b = pl.multiple_of(odd * far, 8)
    copies = []
    for k, (row, dst) in enumerate(((row_b, send_b), (row_a, send_a))):
        copies.append(
            pltpu.make_async_copy(
                vec.at[:, pl.ds(row, SWEEPS), :], dst.at[pl.ds(0, count)], sems.at[2 * k]
            )
        )
        copies.append(
            pltpu.make_async_copy(
                log_kappa.at[pl.ds(row, SWEEPS), :], dst.at[count], sems.at[2 * k + 1]
            )
        )
    for c in copies:
        c.start()
    for c in copies:
        c.wait()


def inner_kernel(
    quad, patch, vec, halo_a, log_kappa,
    outer_left, outer_right, sub, send_right, send_left, rim, gram, own_weights, forth, back,
    even, odd_buf, weights, mixed, logs, natural,
):
    odd = lax.rem(lax.axis_index(quad), 2)
    swap = lax.rem(lax.axis_index(patch), 2) == 1
    total, groups = even.shape[:2]
    height = total - SWEEPS
    count = 8 * groups
    width = even.shape[-1]

    matrix = permutation(width, False)
    forth[...] = matrix
    logs[...] = jnp.zeros(logs.shape, f32)
    logs[pl.ds(16, height)] = permute_columns(log_kappa[...], matrix)
    below = pl.multiple_of(8 + (1 - odd) * (height + 8), 8)
    logs[pl.ds(below, 8)] = permute_columns(halo_a[count], matrix)
    values = face_weights(logs[...], 1.0)
    for i in range(4):
        natural[i] = values[i]

    def natural_row(k):
        return jnp.where(odd == 1, height + 7 - k, k + 8)

    load_rows(halo_a[pl.ds(0, count)], mixed.at[0], even, height, odd, matrix)
    for block in range(height // 8):
        own = pl.multiple_of(8 * jnp.where(odd == 1, height // 8 - 1 - block, block), 8)
        load_rows(
            vec[:, pl.ds(own, 8), :], mixed.at[block + 1], even, 8 * block, odd, matrix
        )
    spread_weights(natural, weights, total - 2, lambda k: natural_row(k + 1), odd)
    own_weights[...] = weights[pl.ds(0, SWEEPS - 1)]

    bufs = (even, odd_buf)
    for level in range(1, SWEEPS + 1):
        now, new = bufs[(level - 1) % 2], bufs[level % 2]
        rim[level - 1, 0] = now[level - 1]
        rim[level - 1, 1] = now[level]
        sweep(level, now, new, weights, level, total - level, 1)

    final = bufs[SWEEPS % 2]
    unmix = permutation(width, True)
    back[...] = unmix
    outs = (outer_left, outer_right, sub, send_right, send_left)

    def finish(block, carry):
        row = pl.multiple_of(8 * block, 8)
        emit(final, row + 8, count, groups, unmix, swap, outs, row)
        return carry

    lax.fori_loop(0, (height - SWEEPS) // 8, finish, 0, unroll=True)
    x = rows_as_columns(sub, 0, height - SWEEPS)
    gram[...] = gram_product(x, x)


def edge_kernel(
    quad, patch, halo_b, log_kappa, rim, gram_inner, own_weights, forth, back,
    send_right_in, send_left_in, outer_left, outer_right, sub, send_right, send_left,
    even, odd_buf, weights, mixed, logs, natural,
):
    index = lax.axis_index(quad)
    odd = lax.rem(index, 2)
    swap = lax.rem(lax.axis_index(patch), 2) == 1
    size = lax.axis_size(quad)
    inside = jnp.logical_and(index > 0, index < size - 1)
    alive = jnp.where(inside, 1.0, 0.0)
    groups = even.shape[1]
    width = even.shape[-1]
    height = log_kappa.shape[0]
    count = 8 * groups
    matrix = forth[...]
    logs[...] = jnp.zeros(logs.shape, f32)
    own_at = pl.multiple_of(odd * (height - 16), 8)
    place = pl.multiple_of(16 - 8 * odd, 8)
    logs[pl.ds(place, 16)] = permute_columns(log_kappa[pl.ds(own_at, 16), :], matrix)
    halo_at = pl.multiple_of(8 + 16 * odd, 8)
    logs[pl.ds(halo_at, 8)] = permute_columns(jnp.where(inside, halo_b[count], 0.0), matrix)
    position = lax.broadcasted_iota(jnp.int32, (24, width), 0)
    outside = jnp.logical_and(position >= 16 * odd, position < 8 + 16 * odd)
    values = face_weights(logs[...], jnp.where(outside, alive, 1.0))
    for i in range(4):
        natural[i] = values[i]

    fields = jnp.where(inside, halo_b[pl.ds(0, count)], 0.0)
    load_rows(fields, mixed, even, 0, odd, matrix)
    spread_weights(
        natural, weights, SWEEPS, lambda k: jnp.where(odd == 1, 22 - k, k + 1), odd
    )
    weights[pl.ds(SWEEPS, SWEEPS - 1)] = own_weights[...]

    bufs = (even, odd_buf)
    for level in range(1, SWEEPS + 1):
        now, new = bufs[(level - 1) % 2], bufs[level % 2]
        now[level + SWEEPS - 1] = rim[level - 1, 0]
        now[level + SWEEPS] = rim[level - 1, 1]
        sweep(level, now, new, weights, level, level + SWEEPS, 1)

    final = bufs[SWEEPS % 2]
    emit(final, SWEEPS, count, groups, back[...], swap, (outer_left, outer_right, sub, send_right, send_left), 0)
    x = rows_as_columns(sub, 0, SWEEPS)
    total = gram_inner[...] + gram_product(x, x)
    inner = height - SWEEPS
    for out, source in ((send_right, send_right_in), (send_left, send_left_in)):
        out[pl.ds(SWEEPS, inner)] = source[...]
        out[height] = jnp.zeros((count, LANES), f32)
        out[height, :, :count] = total


def product_kernel(
    patch, left_in, left_edge, right_in, right_edge, from_right_pair, from_left_pair, sent, out
):
    swap = lax.rem(lax.axis_index(patch), 2) == 1
    count = out.shape[0]
    inner = left_in.shape[0]
    height = inner + SWEEPS

    def products(mine, mine_edge, theirs):
        x = jnp.concatenate(
            [rows_as_columns(mine_edge, 0, SWEEPS), rows_as_columns(mine, 0, inner)], axis=1
        )
        return gram_product(x, rows_as_columns(theirs, 0, height))

    out[...] = jnp.zeros(out.shape, f32)

    def write(from_left, from_right):
        mats = (
            products(left_in, left_edge, from_left),
            sent[height, :, :count],
            from_left[height, :, :count],
            from_right[height, :, :count],
            products(right_in, right_edge, from_right),
        )
        for k, mat in enumerate(mats):
            out[:, k * count : (k + 1) * count] = mat

    @pl.when(swap)
    def _():
        write(from_right_pair, from_left_pair)

    @pl.when(jnp.logical_not(swap))
    def _():
        write(from_left_pair, from_right_pair)


def inverse_factors(works, offsets, count):
    sub = lax.broadcasted_iota(jnp.int32, works[0].shape, 0)
    scales = [jnp.zeros_like(work) for work in works]
    for j in range(0, count, STEP):
        for m, work in enumerate(works):
            at = [offsets[m] + k for k in range(j, j + STEP)]
            cols = [jnp.broadcast_to(work[:, k : k + 1], work.shape) for k in at]
            rows = [work[k : k + 1] for k in range(j, j + STEP)]
            change = jnp.zeros_like(work)
            for i in range(STEP):
                pivot = cols[i][j + i : j + i + 1]
                scales[m] = jnp.where(sub == j + i, 1.0 / jnp.sqrt(pivot), scales[m])
                over = 1.0 / pivot
                scaled = rows[i] * over
                for k in range(i + 1, STEP):
                    rows[k] = rows[k] - cols[i][j + k : j + k + 1] * scaled
                    cols[k] = cols[k] - cols[i] * (cols[k][j + i : j + i + 1] * over)
                change = change + cols[i] * scaled
            work = jnp.where(sub >= j + STEP, work - change, work)
            for i in range(1, STEP):
                work = jnp.where(sub == j + i, rows[i], work)
            works[m] = work
    return [(work * scale)[:, :count] for work, scale in zip(works, scales)]


def final_kernel(quad, patch, chip, other, sub_in, sub_edge, basis, coupling, slabs, sems):
    odd = lax.rem(lax.axis_index(quad), 2)
    place = lax.axis_index(patch)
    last = lax.axis_size(patch) - 1
    inner, count, sub_width = sub_in.shape
    height = inner + SWEEPS
    total = chip[...] + other[...]
    sub = lax.broadcasted_iota(jnp.int32, total.shape, 0)
    lane = lax.broadcasted_iota(jnp.int32, total.shape, 1)
    works = []
    for k, missing in ((1, None), (2, place == 0), (3, place == last)):
        column = lane - k * count
        work = total if missing is None else jnp.where(missing, (sub == column).astype(f32), total)
        work = jnp.where(jnp.logical_and(column >= 0, column < count), work, 0.0)
        works.append(jnp.where(lane < count, (sub == lane).astype(f32), work))
    own, left, right = inverse_factors(works, (count, 2 * count, 3 * count), count)
    from_left = jnp.where(place == 0, 0.0, total[:, :count])
    from_right = jnp.where(place == last, 0.0, total[:, 4 * count : 5 * count])

    high = own.astype(bf16).astype(f32)
    low = own - high
    factor = jnp.concatenate([high, high, low], axis=1).astype(bf16)
    stride = slabs.shape[2]
    copies = []
    for block in range(height // 8):
        natural = jnp.where(odd == 1, height // 8 - 1 - block, block)
        for k in range(8):
            row = 8 * block + k
            x = sub_edge[row] if row < SWEEPS else sub_in[row - SWEEPS]
            r = jnp.where(odd == 1, height - 1 - row, row)
            x_high = x.astype(bf16).astype(f32)
            x_low = x - x_high
            value = dot_nn(
                factor, jnp.concatenate([x_high, x_low, x_high], axis=0).astype(bf16)
            )
            for c in range(sub_width // LANES):
                flat = slabs.at[c].reshape(count * stride, LANES)
                for g in range(count // 8):
                    flat[pl.ds(8 * stride * g + r, 8, stride=stride), :] = value[
                        8 * g : 8 * g + 8, LANES * c : LANES * (c + 1)
                    ]
        at = pl.ds(pl.multiple_of(8 * natural, 8), 8)
        for c in range(sub_width // LANES):
            copy = pltpu.make_async_copy(
                slabs.at[c, :, at],
                basis.at[:, at, pl.ds(LANES * c, LANES)],
                sems.at[block, c],
            )
            copy.start()
            copies.append(copy)
    coupling[0] = dot_nt(dot_nn(own, from_left, highest), left, highest)
    coupling[1] = dot_nt(dot_nn(own, from_right, highest), right, highest)
    for copy in copies:
        copy.wait()


def call_prepare(vec, log_own):
    count, _, width = vec.shape
    return pl.pallas_call(
        functools.partial(prepare_kernel, "quad"),
        out_shape=(shape(count + 1, SWEEPS, width),) * 2,
        in_specs=[pl.BlockSpec(memory_space=pltpu.HBM)] * 2,
        out_specs=(VMEM, VMEM),
        scratch_shapes=[pltpu.SemaphoreType.DMA((4,))],
        compiler_params=PARAMS,
        name="prepare",
    )(
        pltpu.with_memory_space_constraint(vec, pltpu.HBM),
        pltpu.with_memory_space_constraint(log_own, pltpu.HBM),
    )


def call_inner(vec, halo_a, log_own):
    count, height, width = vec.shape
    band, groups, inner, total = width // 4, count // 8, height - SWEEPS, height + SWEEPS
    cost = 12 * count * width * SWEEPS * height
    return pl.pallas_call(
        functools.partial(inner_kernel, "quad", "patch"),
        out_shape=(
            shape(inner, count, band),
            shape(inner, count, band),
            shape(inner, count, 2 * band),
            shape(inner, count, band),
            shape(inner, count, band),
            shape(SWEEPS, 2, groups, 8, width),
            shape(count, count),
            shape(SWEEPS - 1, 4, 8, width),
            jax.ShapeDtypeStruct((width, width), bf16),
            jax.ShapeDtypeStruct((width, width), bf16),
        ),
        scratch_shapes=[
            pltpu.VMEM((total, groups, 8, width), f32),
            pltpu.VMEM((total, groups, 8, width), f32),
            pltpu.VMEM((total - 2, 4, 8, width), f32),
            pltpu.VMEM((height // 8 + 1, BLOCKS, 8 * count, LANES), f32),
            pltpu.VMEM((height + 32, width), f32),
            pltpu.VMEM((4, height + 16, width), f32),
        ],
        compiler_params=PARAMS,
        cost_estimate=pl.CostEstimate(flops=cost, bytes_accessed=5 << 20, transcendentals=0),
        name="inner",
    )(vec, halo_a, log_own)


def call_edge(halo_b, log_own, rim, gram_inner, own_weights, forth, back, send_right, send_left):
    height, width = log_own.shape
    inner, count, band = send_right.shape
    groups = count // 8
    return pl.pallas_call(
        functools.partial(edge_kernel, "quad", "patch"),
        out_shape=(
            shape(SWEEPS, count, band),
            shape(SWEEPS, count, band),
            shape(SWEEPS, count, 2 * band),
            shape(height + 1, count, band),
            shape(height + 1, count, band),
        ),
        scratch_shapes=[
            pltpu.VMEM((2 * SWEEPS + 1, groups, 8, width), f32),
            pltpu.VMEM((2 * SWEEPS + 1, groups, 8, width), f32),
            pltpu.VMEM((2 * SWEEPS - 1, 4, 8, width), f32),
            pltpu.VMEM((BLOCKS, 8 * count, LANES), f32),
            pltpu.VMEM((40, width), f32),
            pltpu.VMEM((4, 24, width), f32),
        ],
        compiler_params=PARAMS,
        name="edge",
    )(halo_b, log_own, rim, gram_inner, own_weights, forth, back, send_right, send_left)


def call_product(left_in, left_edge, right_in, right_edge, from_right_pair, from_left_pair, sent):
    count = left_in.shape[1]
    return pl.pallas_call(
        functools.partial(product_kernel, "patch"),
        out_shape=shape(count, LANES),
        compiler_params=PARAMS,
        name="product",
    )(left_in, left_edge, right_in, right_edge, from_right_pair, from_left_pair, sent)


def call_final(chip, other, sub_in, sub_edge):
    inner, count, sub_width = sub_in.shape
    height = inner + SWEEPS
    return pl.pallas_call(
        functools.partial(final_kernel, "quad", "patch"),
        out_shape=(shape(count, height, sub_width), shape(2, count, count)),
        out_specs=(ANY, VMEM),
        scratch_shapes=[
            pltpu.VMEM((sub_width // LANES, count, height + PAD, LANES), f32),
            pltpu.SemaphoreType.DMA((height // 8, sub_width // LANES)),
        ],
        compiler_params=PARAMS,
        name="final",
    )(chip, other, sub_in, sub_edge)


def swaps(size, first):
    route = [(i, i + 1) for i in range(first, size - 1, 2)]
    return route + [(j, i) for i, j in route]


def on_device(vectors, log_kappa):
    vec, log_own = vectors[0], log_kappa[0]
    patches, quads = lax.axis_size("patch"), lax.axis_size("quad")
    send_a, send_b = call_prepare(vec, log_own)
    halo_a = lax.ppermute(send_a, "quad", swaps(quads, 0))
    middle = [(quads * p + i, quads * p + j) for p in range(patches) for i, j in swaps(quads, 1)]
    idle = [
        (quads * i + q, quads * j + q) for i, j in swaps(patches, 0) for q in (0, quads - 1)
    ]
    halo_b = lax.ppermute(send_b, ("patch", "quad"), middle + idle)
    left_in, right_in, sub_in, send_1_in, send_2_in, *for_edge = call_inner(vec, halo_a, log_own)
    left_edge, right_edge, sub_edge, send_1, send_2 = call_edge(
        halo_b, log_own, *for_edge, send_1_in, send_2_in
    )
    partners = [
        (quads * i + q, quads * j + q) for i, j in swaps(patches, 1) for q in range(quads)
    ]
    idle = [
        (quads * p + i, quads * p + j) for p in (0, patches - 1) for i, j in swaps(quads, 0)
    ]
    from_2 = lax.ppermute(send_2, ("patch", "quad"), partners + idle)
    from_1 = lax.ppermute(send_1, "patch", swaps(patches, 0))
    packed = call_product(left_in, left_edge, right_in, right_edge, from_1, from_2, send_1)
    chip = packed + lax.ppermute(packed, "quad", swaps(quads, 0))
    other = lax.ppermute(chip, "quad", [(i, quads - 1 - i) for i in range(quads)])
    basis, coupling = call_final(chip, other, sub_in, sub_edge)
    return basis[None], coupling[None]


def solution(mesh):
    placed = (P("patch", None, "quad", None), P("patch", "quad", None))
    return jax.shard_map(
        on_device,
        mesh=mesh,
        in_specs=placed,
        out_specs=(P("patch", None, "quad", None), P("patch", None, None, None)),
        check_vma=False,
    )
```
